32 devices in a mesh: seq: 16 (over z, x, core), fsdp: 2 (over y).
Axes of the slice: x: 2, y: 2, z: 4, core: 2. Of those that a mesh axis runs over, the one named last changes fastest.
Arguments:
- inputs: bfloat16 [2, 2048, 2304], P('fsdp', 'seq'), may hold values from -6 to 6
- queries: bfloat16 [2, 2048, 2048], P('fsdp', 'seq'), may hold values from -96 to 96
- w_kv: bfloat16 [2304, 2048], P('fsdp'), may hold values from -0.125 to 0.125
- doc_lengths: int32 [2, 8], P('fsdp'), may hold values from 1 to 1536, 2048 in all within a row
- grad_out: bfloat16 [2, 2048, 2048], P('fsdp', 'seq'), may hold values from -6 to 6
Outputs:
- attn_out: bfloat16 [2, 2048, 2048], P('fsdp', 'seq')
- grad_inputs: bfloat16 [2, 2048, 2304], P('fsdp', 'seq')
- grad_weights: float32 [2304, 2048], P('fsdp', 'seq')
The draws below stay inside these ranges and needn't reach their ends.
Inputs may be any that keep to these rules, and one draw needn't show every extreme that they name: `doc_lengths`: each row lists the lengths of the 8 documents packed in order into one sequence; a row sums to 2048 and its longest document has 1536 tokens.
All inputs are finite; a program needn't handle non-finite values.
Results may differ from the reference program's by a relative error of at most 0.03.
Values may be sent and summed in bfloat16 or wider, within the bound.
No kernel may reach another device: no remote copies, remote signals or barrier semaphores. Data moves between devices by JAX's collectives and lax.ppermute only.
A program may use at most 128 MiB of HBM per device.

```python
import math
import jax
import jax.numpy as jnp
import numpy as np
from jax import lax

D = 2304
QH = 16
KVH = 8
HD = 128
WIN = 1024
NDOC = 8
TOK_DEV = 128
G = 2
KW = 2048
SEQLEN = 2048
SEQS = 2
MOST = 1536
N_SEQ = 16


def raised(result, stream_key, source, target, shards_of, factor):
    def block_of(axis_at):
        return (jnp.arange(result.shape[axis_at]) // (result.shape[axis_at] // shards_of)).reshape((-1,) + (1,) * (result.ndim - 1 - axis_at))

    first = jax.random.permutation(stream_key, shards_of)[block_of(target)]
    second = (block_of(target) + shards_of // 2) % shards_of
    return jnp.where((block_of(source) == first) | (block_of(source) == second), factor * result, result)


def shard_levels(stream_key, shape, cuts, low, high):
    loudness = 1.0
    for axis_at, parts in cuts:
        draws = jax.random.uniform(jax.random.fold_in(jax.random.fold_in(stream_key, 6), axis_at), (parts,), jnp.float32, low / len(cuts), high / len(cuts))
        loudness = loudness * jnp.repeat(jnp.exp(draws), shape[axis_at] // parts).reshape((-1,) + (1,) * (len(shape) - 1 - axis_at))
    return loudness


def profile(amount, total, limit, skew):
    loads = [(1 << 20) // math.isqrt(grade ** skew) + 1 for grade in range(2, amount + 1)]
    spare, holding = total - limit - (amount - 1), [1] * (amount - 1)
    while spare > 0:
        candidates = [i for i in range(amount - 1) if holding[i] < limit]
        whole, budget = sum([loads[i] for i in candidates]), spare
        for i in candidates:
            addition = min(limit - holding[i], max(1, budget * loads[i] // whole), spare)
            holding[i] = holding[i] + addition
            spare = spare - addition
    return np.array([limit] + holding)


def ragged_sizes(key, number_of, total, bound, lean):
    if number_of == 2:
        one = jax.random.randint(key, (), max(1, total - bound), min(bound, total - 1) + 1)
        return jnp.stack([one, total - one])
    sizes = jnp.asarray(profile(number_of, total, bound, lean), jnp.int32)
    twos = (number_of - 1) // 2
    donor, taker = sizes[1:1 + 2 * twos:2], sizes[2:2 + 2 * twos:2]
    slack = jnp.minimum(donor - 1, bound - taker)
    passed = jax.random.randint(jax.random.fold_in(key, 1), (twos,), 0, 1 << 20) % (slack + 1)
    sizes = sizes.at[1:1 + 2 * twos:2].set(donor - passed).at[2:2 + 2 * twos:2].set(taker + passed)
    return sizes[jax.random.permutation(jax.random.fold_in(key, 2), number_of)]


def scatter_about(stream_key, dims, spread, limit, split=(), kind=jnp.bfloat16):
    level = shard_levels(stream_key, dims, split, -0.22, 0.18) if split else 1.0
    entries = jax.random.normal(stream_key, dims, jnp.float32) * spread * level
    return jnp.minimum(jnp.maximum(entries, -limit), limit).astype(kind)


def gaussian_with(own_key, dims, deviation, bound, shards, heavy, kind=jnp.bfloat16):
    array = deviation * jax.random.normal(own_key, dims, jnp.float32)
    if shards:
        array = array * shard_levels(own_key, dims, shards, -0.22, 0.18)
    return jnp.clip(raised(array, jax.random.fold_in(own_key, 3), *heavy), -bound, bound).astype(kind)


def setup_inputs(seed: int = 0) -> dict:
    keys = jax.random.split(jax.random.key(seed), 6)
    return {
        "inputs": gaussian_with(keys[0], (SEQS, SEQLEN, D), 1.0, 6.0, ((0, 2), (1, 16)), (0, 2, 2, 2.0)),
        "queries": scatter_about(keys[1], (SEQS, SEQLEN, QH * HD), 16.0, 96.0, ((0, 2), (1, 16))),
        "w_kv": scatter_about(keys[2], (D, KW), D ** -0.5, 0.125, ((0, 2),)),
        "doc_lengths": jax.vmap(lambda own: ragged_sizes(own, NDOC, SEQLEN, MOST, 2))(jax.random.split(keys[3], SEQS)).reshape((SEQS, NDOC)).astype(jnp.int32),
        "grad_out": scatter_about(keys[4], (SEQS, SEQLEN, QH * HD), 1.0, 6.0, ((0, 2), (1, 16))),
    }


SOFT_CAP = 50.0
QUERY_SCALE = 1.0 / 12.0
ROPE_BASE = 10000.0


def doc_layout(lengths, places):
    lengths = lengths.astype(jnp.int32)
    doc_ends = jnp.cumsum(lengths).astype(jnp.int32)
    doc_ended = doc_ends[None, :] <= places[:, None]
    doc_index = jnp.sum(doc_ended.astype(jnp.int32), axis=1).astype(jnp.int32)
    before = jnp.sum(jnp.where(doc_ended, lengths[None, :], 0), axis=1).astype(jnp.int32)
    return doc_index, (places - before).astype(jnp.int32)


def rotate(values, places, direction):
    half_dim = values.shape[-1] // 2
    exponent = jnp.arange(half_dim, dtype=jnp.float32) * (2.0 / values.shape[-1])
    inverse_rate = jnp.power(ROPE_BASE, -exponent)
    angles = places.astype(jnp.float32)[:, None] * inverse_rate[None, :]
    cosine = jnp.cos(angles)[:, None, :]
    sine_part = direction * jnp.sin(angles)[:, None, :]
    first_half = values[..., :half_dim]
    second_half = values[..., half_dim:]
    return jnp.concatenate([first_half * cosine - second_half * sine_part, second_half * cosine + first_half * sine_part], axis=-1)


def rounded_copy(values):
    return lax.optimization_barrier(values.astype(jnp.bfloat16)).astype(jnp.float32)


def one_sequence(tokens, query_rows, lengths, cotangent, w_kv):
    half_kv = KVH * HD
    places = jnp.arange(SEQLEN, dtype=jnp.int32)
    doc_index, within = doc_layout(lengths, places)
    projected = jnp.dot(tokens, w_kv, preferred_element_type=jnp.float32)
    key_rows = rotate(projected[:, :half_kv].reshape(SEQLEN, KVH, HD), within, 1.0).reshape(SEQLEN, half_kv).astype(jnp.bfloat16)
    value_rows = projected[:, half_kv:].astype(jnp.bfloat16)
    distance = places[:, None] - places[None, :]
    allowed = (doc_index[:, None] == doc_index[None, :]) & (distance >= 0) & (distance <= WIN - 1)
    owner = (places // TOK_DEV).astype(jnp.int32)
    own_term = jnp.arange(N_SEQ, dtype=jnp.int32)[:, None] == owner[None, :]

    def one_head(head_index):
        q_part = lax.dynamic_slice_in_dim(query_rows, head_index * G * HD, G * HD, 1).reshape(SEQLEN, G, HD).astype(jnp.float32)
        d_part = lax.dynamic_slice_in_dim(cotangent, head_index * G * HD, G * HD, 1).reshape(SEQLEN, G, HD).astype(jnp.float32)
        k_part = lax.dynamic_slice_in_dim(key_rows, head_index * HD, HD, 1).astype(jnp.float32)
        v_part = lax.dynamic_slice_in_dim(value_rows, head_index * HD, HD, 1).astype(jnp.float32)
        scores = jnp.einsum('tgd,nd->gtn', q_part, k_part) * QUERY_SCALE
        squashed = jnp.tanh(scores / SOFT_CAP)
        weights = jnp.where(allowed[None], jnp.exp(SOFT_CAP * squashed), 0.0)
        probs = weights / jnp.sum(weights, axis=-1, keepdims=True)
        rounded = rounded_copy(probs)
        attended = rounded_copy(jnp.einsum('gtn,nd->tgd', rounded, v_part))
        delta_row = jnp.einsum('tgd,tgd->gt', d_part, attended)
        dprob = jnp.einsum('tgd,nd->gtn', d_part, v_part)
        dscore = rounded_copy(probs * (dprob - delta_row[:, :, None]) * (1.0 - squashed * squashed))
        q_shards = q_part.reshape(N_SEQ, TOK_DEV, G, HD)
        d_shards = d_part.reshape(N_SEQ, TOK_DEV, G, HD)
        key_terms = jnp.einsum('gstn,stgd->snd', dscore.reshape(G, N_SEQ, TOK_DEV, SEQLEN), q_shards) * QUERY_SCALE
        value_terms = jnp.einsum('gstn,stgd->snd', rounded.reshape(G, N_SEQ, TOK_DEV, SEQLEN), d_shards)
        key_grad = jnp.sum(jnp.where(own_term[:, :, None], key_terms, rounded_copy(key_terms)), axis=0)
        value_grad = jnp.sum(jnp.where(own_term[:, :, None], value_terms, rounded_copy(value_terms)), axis=0)
        return attended.astype(jnp.bfloat16), key_grad, value_grad

    attended, key_grad, value_grad = lax.map(one_head, jnp.arange(KVH, dtype=jnp.int32))
    out_rows = jnp.transpose(attended, (1, 0, 2, 3)).reshape(SEQLEN, QH * HD)
    key_total = rotate(jnp.transpose(key_grad, (1, 0, 2)), within, -1.0).reshape(SEQLEN, half_kv)
    value_total = jnp.transpose(value_grad, (1, 0, 2)).reshape(SEQLEN, half_kv)
    grad_kv = jnp.concatenate([key_total, value_total], axis=1).astype(jnp.bfloat16)
    grad_rows = jnp.dot(grad_kv, w_kv.T, preferred_element_type=jnp.float32).astype(jnp.bfloat16)
    return out_rows, grad_rows, grad_kv


def reference(inputs, queries, w_kv, doc_lengths, grad_out):
    def per_sequence(operands):
        return one_sequence(operands[0], operands[1], operands[2], operands[3], w_kv)

    attn_out, grad_inputs, grad_kv = lax.map(per_sequence, (inputs, queries, doc_lengths, grad_out))
    token_blocks = inputs.reshape(SEQS * N_SEQ, TOK_DEV, D)
    grad_blocks = grad_kv.reshape(SEQS * N_SEQ, TOK_DEV, KW)

    def accumulate(running, pieces):
        device_term = jnp.dot(pieces[0].T, pieces[1], preferred_element_type=jnp.float32)
        return running + rounded_copy(device_term), None

    grad_weights, ignored = lax.scan(accumulate, jnp.zeros((D, KW), jnp.float32), (token_blocks, grad_blocks))
    return attn_out, grad_inputs, grad_weights
```

```python
import jax
import jax.numpy as jnp
from jax import lax
from jax.experimental import pallas as pl
from jax.experimental.pallas import tpu as pltpu
from jax.sharding import PartitionSpec as P

QH = 16
KVH = 8
HD = 128
WIN = 1024
G = 2

SOFT_CAP = 50.0
QUERY_SCALE = 1.0 / 12.0
ROPE_BASE = 10000.0

SEQ = 16
PLANES = 4
BLK = 256
REACH = WIN // BLK + 1


def shift_planes(value, steps):
    pairs = [(s, (s + 4 * steps) % SEQ) for s in range(SEQ)]
    return lax.ppermute(value, "seq", pairs)


def swap_sides(value):
    return lax.ppermute(value, "seq", [(s, s ^ 2) for s in range(SEQ)])


def swap_cores(value):
    return lax.ppermute(value, "seq", [(s, s ^ 1) for s in range(SEQ)])


def shift_rows(value, steps):
    count = lax.axis_size("fsdp")
    return lax.ppermute(value, "fsdp", [(i, (i + steps) % count) for i in range(count)])


def columns(value, start, size):
    return lax.dynamic_slice_in_dim(value, start, size, value.ndim - 1)


def attention_kernel(
    len_ref, pos_ref, kept_ref, came_ref, own_ref, oth_ref, cos_ref, sin_ref,
    out_ref, keep_ref, send_ref,
    q_s, d_s, kv_s, vt_s, e_s, t_s, dk_s, dv_s,
):
    plane, side, core = pos_ref[0], pos_ref[1], pos_ref[2]
    rows = out_ref.shape[3]
    total = q_s.shape[0]
    f32 = jnp.float32
    nt = (((1,), (1,)), ((), ()))

    def flipped(bit, flip):
        return 1 - bit if flip else bit

    for step in range(PLANES):
        at_plane = lax.rem(plane + (PLANES - step), PLANES)
        for xr in range(2):
            for cr in range(2):
                base = at_plane * (4 * rows) + flipped(side, xr) * (2 * rows)
                mine = pl.multiple_of(base + flipped(core, cr) * rows, rows)
                theirs = pl.multiple_of(base + flipped(core, 1 - cr) * rows, rows)
                source = came_ref if cr else kept_ref
                q_s[pl.ds(mine, rows), :] = source[xr, step, 0]
                d_s[pl.ds(mine, rows), :] = source[xr, step, 1]
                piece = pl.ds((2 * cr + xr) * rows, rows)
                kv_s[core, pl.ds(mine, rows), :] = own_ref[step, piece, :]
                kv_s[1 - core, pl.ds(theirs, rows), :] = oth_ref[step, piece, :]

    for block in range(total // BLK):
        span = pl.ds(block * BLK, BLK)
        vt_s[:, span] = kv_s[1, span, :].astype(f32).T.astype(jnp.bfloat16)
    dk_s[...] = jnp.zeros_like(dk_s)
    dv_s[...] = jnp.zeros_like(dv_s)

    ends = []
    run = 0
    for j in range(len_ref.shape[0]):
        run = run + len_ref[j]
        ends.append(run)

    def query_block(i, carry):
        base = pl.multiple_of(i * BLK, BLK)
        span = pl.ds(base, BLK)
        qb = q_s[span, :]
        db = d_s[span, :]
        p_row = base + lax.broadcasted_iota(jnp.int32, (1, BLK), 1)
        start_row = jnp.zeros((1, BLK), jnp.int32)
        first = jnp.int32(0)
        for end in ends:
            start_row = jnp.where(end <= p_row, end, start_row)
            first = jnp.where(end <= base, end, first)
        low_row = jnp.maximum(start_row, p_row - (WIN - 1))
        low_block = jnp.maximum(first, jnp.maximum(base - (WIN - 1), 0)) // BLK
        count = i - low_block + 1

        def body(n):
            def key_span(j):
                return pl.ds(pl.multiple_of((low_block + j) * BLK, BLK), BLK)

            norm = jnp.zeros((1, BLK), f32)
            out_t = jnp.zeros((HD, BLK), f32)
            for j in range(n):
                keys = key_span(j)
                scores = lax.dot_general(kv_s[0, keys, :], qb, nt, preferred_element_type=f32)
                squashed = jnp.tanh(scores * (QUERY_SCALE / SOFT_CAP))
                weights = jnp.exp(squashed * SOFT_CAP)
                n_col = (low_block + j) * BLK + lax.broadcasted_iota(jnp.int32, (BLK, 1), 0)
                allowed = n_col >= low_row
                if j == n - 1:
                    allowed = allowed & (n_col <= p_row)
                weights = jnp.where(allowed, weights, 0.0)
                t_s[j] = squashed
                e_s[j] = weights
                norm = norm + jnp.sum(weights, axis=0, keepdims=True)
                out_t = out_t + jnp.dot(
                    vt_s[:, keys], weights.astype(jnp.bfloat16), preferred_element_type=f32
                )
            inverse = 1.0 / norm
            out_f = (out_t * inverse).astype(jnp.bfloat16).astype(f32)
            delta = jnp.sum(db.astype(f32).T * out_f, axis=0, keepdims=True)
            out_b = out_f.T.astype(jnp.bfloat16)
            to_step = lax.rem(i // 2 + PLANES - plane, PLANES)
            to_side = lax.rem(i + side, 2)
            out_ref[to_step, core, to_side] = out_b[:rows]
            out_ref[to_step, 1 - core, to_side] = out_b[rows:]
            for j in range(n):
                keys = key_span(j)
                probs = e_s[j] * inverse
                squashed = t_s[j]
                dv_s[keys, :] += jnp.dot(
                    probs.astype(jnp.bfloat16), db, preferred_element_type=f32
                )
                dprob = lax.dot_general(kv_s[1, keys, :], db, nt, preferred_element_type=f32)
                dscore = probs * (dprob - delta) * (1.0 - squashed * squashed)
                dk_s[keys, :] += jnp.dot(
                    dscore.astype(jnp.bfloat16), qb, preferred_element_type=f32
                )

        for n in range(1, REACH + 1):
            pl.when(count == n)(lambda n=n: body(n))
        return carry

    lax.fori_loop(0, total // BLK, query_block, 0)

    def finish(block, carry):
        span = pl.ds(pl.multiple_of(block * rows, rows), rows)
        key_part = dk_s[span, :] * QUERY_SCALE
        key_part = key_part * cos_ref[span, :] - pltpu.roll(key_part, HD // 2, 1) * sin_ref[span, :]
        value_part = dv_s[span, :]
        to_step = lax.rem(block // 4 + PLANES - plane, PLANES)
        to_side = lax.rem(block // 2 + side, 2)
        to_core = lax.rem(block + core, 2)
        is_key = core == 0
        keep_ref[to_step, to_core, to_side] = jnp.where(is_key, key_part, value_part)
        send_ref[to_step, 1 - to_core, to_side] = jnp.where(is_key, value_part, key_part).astype(
            jnp.bfloat16
        )
        return carry

    lax.fori_loop(0, total // rows, finish, 0)


def attention(lengths, position, kept, came, own, other, cosine, sine):
    rows = kept.shape[3]
    total = SEQ * rows
    split = (PLANES, 2, 2, rows, HD)
    bf16, f32 = jnp.bfloat16, jnp.float32
    pairs = 30 * BLK * BLK
    return pl.pallas_call(
        attention_kernel,
        out_shape=(
            jax.ShapeDtypeStruct(split, bf16),
            jax.ShapeDtypeStruct(split, f32),
            jax.ShapeDtypeStruct(split, bf16),
        ),
        in_specs=[pl.BlockSpec(memory_space=pltpu.SMEM)] * 2
        + [pl.BlockSpec(memory_space=pltpu.VMEM)] * 6,
        out_specs=[pl.BlockSpec(memory_space=pltpu.VMEM)] * 3,
        scratch_shapes=[
            pltpu.VMEM((total, HD), bf16),
            pltpu.VMEM((total, HD), bf16),
            pltpu.VMEM((2, total, HD), bf16),
            pltpu.VMEM((HD, total), bf16),
            pltpu.VMEM((REACH, BLK, BLK), f32),
            pltpu.VMEM((REACH, BLK, BLK), f32),
            pltpu.VMEM((total, HD), f32),
            pltpu.VMEM((total, HD), f32),
        ],
        compiler_params=pltpu.CompilerParams(vmem_limit_bytes=40 * 2**20),
        cost_estimate=pl.CostEstimate(
            flops=10 * pairs * HD, bytes_accessed=7 * 2**20, transcendentals=2 * pairs
        ),
    )(lengths, position, kept, came, own, other, cosine, sine)


def place_kernel(pos_ref, near_ref, far_ref, out_ref):
    plane, side, core = pos_ref[0], pos_ref[1], pos_ref[2]
    for step in range(PLANES):
        home = lax.rem(plane + (PLANES - step), PLANES)
        for hx in range(2):
            for hc in range(2):
                x = 1 - side if hx else side
                c = 1 - core if hc else core
                head = 8 * (home // 2) + 4 * x + 2 * lax.rem(home, 2) + c
                source = far_ref if hx else near_ref
                at = pl.multiple_of(head * HD, HD)
                out_ref[:, pl.ds(at, HD)] = source[hc, step]


def place_heads(position, near, far):
    return pl.pallas_call(
        place_kernel,
        out_shape=jax.ShapeDtypeStruct((near.shape[2], QH * HD), near.dtype),
        in_specs=[pl.BlockSpec(memory_space=pltpu.SMEM)]
        + [pl.BlockSpec(memory_space=pltpu.VMEM)] * 2,
        out_specs=pl.BlockSpec(memory_space=pltpu.VMEM),
        compiler_params=pltpu.CompilerParams(vmem_limit_bytes=16 * 2**20),
        cost_estimate=pl.CostEstimate(flops=0, bytes_accessed=2**20, transcendentals=0),
    )(position, near, far)


def on_device(inputs, queries, w_kv, doc_lengths, grad_out):
    bf16, f32 = jnp.bfloat16, jnp.float32
    tokens = inputs[0]
    query_rows = queries[0]
    cotangent = grad_out[0]
    lengths = doc_lengths[0]
    rows, width = tokens.shape
    total = SEQ * rows
    half_kv = KVH * HD
    seqs = lax.axis_size("fsdp")
    depth = w_kv.shape[0]
    here = lax.axis_index("seq")
    own_seq = lax.axis_index("fsdp")
    plane, side, core = here // 4, (here // 2) % 2, here % 2
    position = jnp.stack([plane, side, core]).astype(jnp.int32)

    first = core * half_kv + side * 256
    w_own = jnp.concatenate(
        [columns(w_kv, first, 256), columns(w_kv, first + half_kv // 2, 256)], axis=1
    )
    w_parts = [w_own] + [shift_rows(w_own, o) for o in range(1, seqs)]
    origins = [(own_seq - o) % seqs for o in range(seqs)]

    near = jnp.concatenate([tokens, swap_sides(tokens)], axis=0)
    far = swap_cores(near)

    def for_plane(at):
        start = (at // 2) * 1024 + (at % 2) * 256
        return jnp.stack(
            [
                jnp.concatenate([columns(a, start, 256), columns(a, start + 512, 256)], axis=1)
                for a in (query_rows, cotangent)
            ]
        )

    by_plane = jnp.stack(
        [for_plane(plane)]
        + [shift_planes(for_plane((plane + k) % PLANES), k) for k in range(1, PLANES)]
    )
    crossed = swap_sides(columns(by_plane, (1 - side) * 256, 256))
    by_side = jnp.stack([columns(by_plane, side * 256, 256), crossed])
    kept = columns(by_side, core * HD, HD)
    came = swap_cores(columns(by_side, (1 - core) * HD, HD))

    places = jnp.arange(total, dtype=jnp.int32)
    doc_ends = jnp.cumsum(lengths)
    ended = doc_ends[None, :] <= places[:, None]
    within = places - jnp.sum(jnp.where(ended, lengths[None, :], 0), axis=1)
    exponent = jnp.arange(HD // 2, dtype=f32) * (2.0 / HD)
    rate = jnp.power(ROPE_BASE, -exponent)
    angles = within.astype(f32)[:, None] * rate[None, :]
    cos_half, sin_half = jnp.cos(angles), jnp.sin(angles)
    cosine = jnp.concatenate([cos_half, cos_half], axis=1)
    sine = jnp.concatenate([-sin_half, sin_half], axis=1)

    def project(part, cr):
        acc = 0.0
        for o in range(seqs):
            acc = acc + jnp.dot(
                columns(part, origins[o] * depth, depth), w_parts[o], preferred_element_type=f32
            )
        starts = [
            plane * 4 * rows + (side ^ xr) * 2 * rows + (core ^ cr) * rows for xr in range(2)
        ]
        is_key = core == 0
        cos_part = jnp.concatenate([lax.dynamic_slice_in_dim(cosine, s, rows) for s in starts])
        sin_part = jnp.concatenate([lax.dynamic_slice_in_dim(sine, s, rows) for s in starts])
        cos_part = jnp.where(is_key, cos_part, 1.0)[:, None, :]
        sin_part = jnp.where(is_key, sin_part, 0.0)[:, None, :]
        heads = acc.reshape(2 * rows, PLANES, HD)
        turned = jnp.concatenate([heads[..., HD // 2 :], heads[..., : HD // 2]], axis=-1)
        return (heads * cos_part + turned * sin_part).astype(bf16).reshape(2 * rows, PLANES * HD)

    kv_plane = jnp.concatenate([project(near, 0), project(far, 1)], axis=0)
    own = jnp.stack(
        [columns(kv_plane, plane * HD, HD)]
        + [
            shift_planes(columns(kv_plane, ((plane + k) % PLANES) * HD, HD), k)
            for k in range(1, PLANES)
        ]
    )
    other = swap_cores(own)

    out_parts, keep, send = attention(lengths, position, kept, came, own, other, cosine, sine)

    grads = (keep + swap_cores(send).astype(f32)).astype(bf16)
    grads = grads.reshape(PLANES, 4 * rows, HD)
    gathered = jnp.stack(
        [grads[0]] + [shift_planes(grads[k], k) for k in range(1, PLANES)]
    )
    grad_plane = jnp.concatenate(
        [
            lax.dynamic_index_in_dim(gathered, (plane - b) % PLANES, 0, keepdims=False)
            for b in range(PLANES)
        ],
        axis=1,
    )

    plane_tokens = jnp.concatenate([near, far], axis=0)
    tok_parts = [columns(plane_tokens, own_seq * depth, depth)] + [
        shift_rows(columns(plane_tokens, ((own_seq + o) % seqs) * depth, depth), o)
        for o in range(1, seqs)
    ]
    grad_parts = [grad_plane] + [shift_rows(grad_plane, o) for o in range(1, seqs)]
    weight_terms = sum(
        lax.dot_general(t, g, (((0,), (0,)), ((), ())), preferred_element_type=f32)
        for t, g in zip(tok_parts, grad_parts)
    ).astype(bf16)
    finished = 0.0
    for k in range(PLANES):
        block = columns(weight_terms, ((plane - k) % PLANES) * HD, HD)
        pairs = []
        for s in range(SEQ):
            at = (s // 4 - k) % PLANES
            pairs.append((s, (2 * (s % 2) + at // 2) * 4 + (s & 2) + at % 2))
        finished = finished + lax.ppermute(block, "seq", pairs).astype(f32)

    w_full = jnp.zeros((width, PLANES * HD), bf16)
    for o in range(seqs):
        w_full = lax.dynamic_update_slice_in_dim(w_full, w_parts[o], origins[o] * depth, 0)
    nt = (((1,), (1,)), ((), ()))
    for_core = lax.dot_general(grad_plane[2 * rows :], w_full, nt, preferred_element_type=f32)
    for_self = lax.dot_general(grad_plane[: 2 * rows], w_full, nt, preferred_element_type=f32)
    for_self = for_self + swap_cores(for_core.astype(bf16)).astype(f32)
    grad_rows = (
        for_self[:rows] + swap_sides(for_self[rows:].astype(bf16)).astype(f32)
    ).astype(bf16)

    outs = jnp.stack(
        [out_parts[0]] + [shift_planes(out_parts[k], k) for k in range(1, PLANES)]
    )
    by_core = jnp.stack([outs[:, 0], swap_cores(outs[:, 1])])
    out_rows = place_heads(position, by_core[:, :, 0], swap_sides(by_core[:, :, 1]))
    return (out_rows[None], grad_rows[None], finished)


def solution(mesh):
    in_specs = (
        P("fsdp", "seq", None),
        P("fsdp", "seq", None),
        P("fsdp", None),
        P("fsdp", None),
        P("fsdp", "seq", None),
    )
    out_specs = (P("fsdp", "seq", None), P("fsdp", "seq", None), P("fsdp", "seq"))
    return jax.shard_map(
        on_device, mesh=mesh, in_specs=in_specs, out_specs=out_specs, check_vma=False
    )
```

```python
import jax
import jax.numpy as jnp
from jax import lax
from jax.experimental import pallas as pl
from jax.experimental.pallas import tpu as pltpu
from jax.sharding import PartitionSpec as P

QH = 16
KVH = 8
HD = 128
WIN = 1024
G = 2

SOFT_CAP = 50.0
QUERY_SCALE = 1.0 / 12.0
ROPE_BASE = 10000.0

SEQ = 16
PLANES = 4
BLK = 256
REACH = WIN // BLK + 1


def shift_planes(value, steps):
    pairs = [(s, (s + 4 * steps) % SEQ) for s in range(SEQ)]
    return lax.ppermute(value, "seq", pairs)


def swap(value, mask):
    return lax.ppermute(value, "seq", [(s, s ^ mask) for s in range(SEQ)])


def swap_sides(value):
    return swap(value, 2)


def swap_cores(value):
    return swap(value, 1)


def shift_rows(value, steps):
    count = lax.axis_size("fsdp")
    return lax.ppermute(value, "fsdp", [(i, (i + steps) % count) for i in range(count)])


def columns(value, start, size):
    return lax.dynamic_slice_in_dim(value, start, size, value.ndim - 1)


def attention_kernel(
    len_ref, pos_ref, kept_ref, came_ref, cos_ref, sin_ref,
    own_0, own_1, own_2, own_3, oth_0, oth_1, oth_2, oth_3,
    out_ref, keep_ref, send_ref,
    q_s, d_s, kv_s, vt_s, e_s, t_s, dk_s, dv_s,
):
    own_refs = (own_0, own_1, own_2, own_3)
    oth_refs = (oth_0, oth_1, oth_2, oth_3)
    plane, side, core = pos_ref[0], pos_ref[1], pos_ref[2]
    rows = out_ref.shape[3]
    total = q_s.shape[0]
    f32 = jnp.float32
    nt = (((1,), (1,)), ((), ()))

    def flipped(bit, flip):
        return 1 - bit if flip else bit

    for step in range(PLANES):
        at_plane = lax.rem(plane + (PLANES - step), PLANES)
        for xr in range(2):
            for cr in range(2):
                base = at_plane * (4 * rows) + flipped(side, xr) * (2 * rows)
                mine = pl.multiple_of(base + flipped(core, cr) * rows, rows)
                theirs = pl.multiple_of(base + flipped(core, 1 - cr) * rows, rows)
                source = came_ref if cr else kept_ref
                q_s[pl.ds(mine, rows), :] = source[xr, step, 0]
                d_s[pl.ds(mine, rows), :] = source[xr, step, 1]
                piece = pl.ds((2 * cr + xr) * rows, rows)
                kv_s[core, pl.ds(mine, rows), :] = own_refs[step][piece, :]
                kv_s[1 - core, pl.ds(theirs, rows), :] = oth_refs[step][piece, :]

    for block in range(total // BLK):
        span = pl.ds(block * BLK, BLK)
        vt_s[:, span] = kv_s[1, span, :].astype(f32).T.astype(jnp.bfloat16)
    dk_s[...] = jnp.zeros_like(dk_s)
    dv_s[...] = jnp.zeros_like(dv_s)

    ends = []
    run = 0
    for j in range(len_ref.shape[0]):
        run = run + len_ref[j]
        ends.append(run)

    def query_block(i, carry):
        base = pl.multiple_of(i * BLK, BLK)
        span = pl.ds(base, BLK)
        qb = q_s[span, :]
        db = d_s[span, :]
        p_row = base + lax.broadcasted_iota(jnp.int32, (1, BLK), 1)
        start_row = jnp.zeros((1, BLK), jnp.int32)
        first = jnp.int32(0)
        for end in ends:
            start_row = jnp.where(end <= p_row, end, start_row)
            first = jnp.where(end <= base, end, first)
        low_row = jnp.maximum(start_row, p_row - (WIN - 1))
        low_block = jnp.maximum(first, jnp.maximum(base - (WIN - 1), 0)) // BLK
        count = i - low_block + 1

        def body(n):
            def key_span(j):
                return pl.ds(pl.multiple_of((low_block + j) * BLK, BLK), BLK)

            norm = jnp.zeros((1, BLK), f32)
            out_t = jnp.zeros((HD, BLK), f32)
            for j in range(n):
                keys = key_span(j)
                scores = lax.dot_general(kv_s[0, keys, :], qb, nt, preferred_element_type=f32)
                squashed = jnp.tanh(scores * (QUERY_SCALE / SOFT_CAP))
                weights = jnp.exp(squashed * SOFT_CAP)
                n_col = (low_block + j) * BLK + lax.broadcasted_iota(jnp.int32, (BLK, 1), 0)
                allowed = n_col >= low_row
                if j == n - 1:
                    allowed = allowed & (n_col <= p_row)
                weights = jnp.where(allowed, weights, 0.0)
                t_s[j] = squashed
                e_s[j] = weights
                norm = norm + jnp.sum(weights, axis=0, keepdims=True)
                out_t = out_t + jnp.dot(
                    vt_s[:, keys], weights.astype(jnp.bfloat16), preferred_element_type=f32
                )
            inverse = 1.0 / norm
            out_f = (out_t * inverse).astype(jnp.bfloat16).astype(f32)
            delta = jnp.sum(db.astype(f32).T * out_f, axis=0, keepdims=True)
            out_b = out_f.T.astype(jnp.bfloat16)
            to_step = lax.rem(i // 2 + PLANES - plane, PLANES)
            to_side = lax.rem(i + side, 2)
            out_ref[to_step, core, to_side] = out_b[:rows]
            out_ref[to_step, 1 - core, to_side] = out_b[rows:]
            for j in range(n):
                keys = key_span(j)
                probs = e_s[j] * inverse
                squashed = t_s[j]
                dv_s[keys, :] += jnp.dot(
                    probs.astype(jnp.bfloat16), db, preferred_element_type=f32
                )
                dprob = lax.dot_general(kv_s[1, keys, :], db, nt, preferred_element_type=f32)
                dscore = probs * (dprob - delta) * (1.0 - squashed * squashed)
                dk_s[keys, :] += jnp.dot(
                    dscore.astype(jnp.bfloat16), qb, preferred_element_type=f32
                )

        for n in range(1, REACH + 1):
            pl.when(count == n)(lambda n=n: body(n))
        return carry

    lax.fori_loop(0, total // BLK, query_block, 0)

    def finish(block, carry):
        span = pl.ds(pl.multiple_of(block * rows, rows), rows)
        key_part = dk_s[span, :] * QUERY_SCALE
        key_part = key_part * cos_ref[span, :] - pltpu.roll(key_part, HD // 2, 1) * sin_ref[span, :]
        value_part = dv_s[span, :]
        to_pair = lax.rem(block // 8 + plane // 2, 2)
        to_plane = lax.rem(block // 4 + plane, 2)
        to_side = lax.rem(block // 2 + side, 2)
        to_core = lax.rem(block + core, 2)
        is_key = core == 0
        keep_ref[to_pair, to_core, to_plane, to_side] = jnp.where(is_key, key_part, value_part)
        send_ref[to_pair, 1 - to_core, to_plane, to_side] = jnp.where(
            is_key, value_part, key_part
        ).astype(jnp.bfloat16)
        return carry

    lax.fori_loop(0, total // rows, finish, 0)


def vmem_specs(count):
    return [pl.BlockSpec(memory_space=pltpu.VMEM)] * count


def smem_specs(count):
    return [pl.BlockSpec(memory_space=pltpu.SMEM)] * count


def attention(lengths, position, kept, came, cosine, sine, own, other):
    rows = kept.shape[3]
    total = SEQ * rows
    bf16, f32 = jnp.bfloat16, jnp.float32
    pairs = 30 * BLK * BLK
    return pl.pallas_call(
        attention_kernel,
        out_shape=(
            jax.ShapeDtypeStruct((PLANES, 2, 2, rows, HD), bf16),
            jax.ShapeDtypeStruct((2, 2, 2, 2, rows, HD), f32),
            jax.ShapeDtypeStruct((2, 2, 2, 2, rows, HD), bf16),
        ),
        in_specs=smem_specs(2) + vmem_specs(12),
        out_specs=vmem_specs(3),
        scratch_shapes=[
            pltpu.VMEM((total, HD), bf16),
            pltpu.VMEM((total, HD), bf16),
            pltpu.VMEM((2, total, HD), bf16),
            pltpu.VMEM((HD, total), bf16),
            pltpu.VMEM((REACH, BLK, BLK), f32),
            pltpu.VMEM((REACH, BLK, BLK), f32),
            pltpu.VMEM((total, HD), f32),
            pltpu.VMEM((total, HD), f32),
        ],
        compiler_params=pltpu.CompilerParams(vmem_limit_bytes=40 * 2**20),
        cost_estimate=pl.CostEstimate(
            flops=10 * pairs * HD, bytes_accessed=7 * 2**20, transcendentals=2 * pairs
        ),
    )(lengths, position, kept, came, cosine, sine, *own, *other)


def project_kernel(pos_ref, cos_ref, sin_ref, *refs):
    tok_refs, w_refs, out_ref = refs[:4], refs[4:-1], refs[-1]
    plane, side, core = pos_ref[0], pos_ref[1], pos_ref[2]
    rows = tok_refs[0].shape[0]
    is_key = core == 0
    for half in range(PLANES // 2):
        acc = jnp.zeros((4 * rows, 2 * HD), jnp.float32)
        for o, w_ref in enumerate(w_refs):
            depth = w_ref.shape[0]
            span = pl.ds(pl.multiple_of(pos_ref[3 + o] * depth, HD), depth)
            part = jnp.concatenate([t[:, span] for t in tok_refs], axis=0)
            acc = acc + jnp.dot(
                part,
                w_ref[:, half * 2 * HD : (half + 1) * 2 * HD],
                preferred_element_type=jnp.float32,
            )
        for b in range(2):
            step = lax.rem(2 * half + b + PLANES - plane, PLANES)
            for piece in range(4):
                x = 1 - side if piece % 2 else side
                c = 1 - core if piece // 2 else core
                start = pl.multiple_of((plane * 4 + 2 * x + c) * rows, rows)
                head = acc[piece * rows : (piece + 1) * rows, b * HD : (b + 1) * HD]
                cosine = jnp.where(is_key, cos_ref[pl.ds(start, rows), :], 1.0)
                sine = jnp.where(is_key, sin_ref[pl.ds(start, rows), :], 0.0)
                turned = head * cosine + pltpu.roll(head, HD // 2, 1) * sine
                out_ref[step, piece * rows : (piece + 1) * rows] = turned.astype(jnp.bfloat16)


def project(position, cosine, sine, pieces, weights):
    rows, width = pieces[0].shape
    return pl.pallas_call(
        project_kernel,
        out_shape=jax.ShapeDtypeStruct((PLANES, 4 * rows, HD), jnp.bfloat16),
        in_specs=smem_specs(1) + vmem_specs(6 + len(weights)),
        out_specs=vmem_specs(1)[0],
        compiler_params=pltpu.CompilerParams(vmem_limit_bytes=32 * 2**20),
        cost_estimate=pl.CostEstimate(
            flops=2 * 4 * rows * width * PLANES * HD, bytes_accessed=7 * 2**20, transcendentals=0
        ),
    )(position, cosine, sine, *pieces, *weights)


def fill_columns(pos_ref, cr, mine_ref, its_ref, near_ref, grad_s):
    for ar in range(2):
        for br in range(2):
            block = pos_ref[0] ^ (2 * ar + br)
            if br:
                value = near_ref[ar, cr]
            else:
                value = (its_ref if ar else mine_ref)[cr, 0]
            grad_s[:, pl.ds(pl.multiple_of(block * HD, HD), HD)] = value


def other_core_kernel(pos_ref, mine_ref, its_ref, near_ref, *refs):
    w_refs, out_ref, grad_s = refs[:-2], refs[-2], refs[-1]
    fill_columns(pos_ref, 1, mine_ref, its_ref, near_ref, grad_s)
    for o, w_ref in enumerate(w_refs):
        depth = w_ref.shape[0]
        span = pl.ds(pl.multiple_of(pos_ref[3 + o] * depth, HD), depth)
        out_ref[:, span] = lax.dot_general(
            grad_s[...], w_ref[...], (((1,), (1,)), ((), ())), preferred_element_type=jnp.float32
        ).astype(out_ref.dtype)


def same_core_kernel(pos_ref, mine_ref, its_ref, near_ref, came_ref, *refs):
    w_refs, (keep_ref, send_ref, grad_s) = refs[:-3], refs[-3:]
    rows = keep_ref.shape[0]
    fill_columns(pos_ref, 0, mine_ref, its_ref, near_ref, grad_s)
    for o, w_ref in enumerate(w_refs):
        depth = w_ref.shape[0]
        span = pl.ds(pl.multiple_of(pos_ref[3 + o] * depth, HD), depth)
        term = lax.dot_general(
            grad_s[...], w_ref[...], (((1,), (1,)), ((), ())), preferred_element_type=jnp.float32
        ) + came_ref[:, span].astype(jnp.float32)
        keep_ref[:, span] = term[:rows]
        send_ref[:, span] = term[rows:].astype(send_ref.dtype)


def input_terms(position, mine, its, near, weights, came=None):
    rows = mine.shape[2]
    width = sum(w.shape[0] for w in weights)
    bf16 = jnp.bfloat16
    if came is None:
        kernel, extra = other_core_kernel, ()
        shapes = jax.ShapeDtypeStruct((rows, width), bf16)
        out_specs = vmem_specs(1)[0]
    else:
        kernel, extra = same_core_kernel, (came,)
        shapes = (
            jax.ShapeDtypeStruct((rows // 2, width), jnp.float32),
            jax.ShapeDtypeStruct((rows // 2, width), bf16),
        )
        out_specs = vmem_specs(2)
    return pl.pallas_call(
        kernel,
        out_shape=shapes,
        in_specs=smem_specs(1) + vmem_specs(3 + len(extra) + len(weights)),
        out_specs=out_specs,
        scratch_shapes=[pltpu.VMEM((rows, PLANES * HD), bf16)],
        compiler_params=pltpu.CompilerParams(vmem_limit_bytes=32 * 2**20),
        cost_estimate=pl.CostEstimate(
            flops=2 * rows * width * PLANES * HD, bytes_accessed=5 * 2**20, transcendentals=0
        ),
    )(position, mine, its, near, *extra, *weights)


def place_kernel(pos_ref, near_ref, far_ref, out_ref):
    plane, side, core = pos_ref[0], pos_ref[1], pos_ref[2]
    for step in range(PLANES):
        home = lax.rem(plane + (PLANES - step), PLANES)
        for hx in range(2):
            for hc in range(2):
                x = 1 - side if hx else side
                c = 1 - core if hc else core
                head = 8 * (home // 2) + 4 * x + 2 * lax.rem(home, 2) + c
                source = far_ref if hx else near_ref
                at = pl.multiple_of(head * HD, HD)
                out_ref[:, pl.ds(at, HD)] = source[hc, step]


def place_heads(position, near, far):
    return pl.pallas_call(
        place_kernel,
        out_shape=jax.ShapeDtypeStruct((near.shape[2], QH * HD), near.dtype),
        in_specs=smem_specs(1) + vmem_specs(2),
        out_specs=vmem_specs(1)[0],
        compiler_params=pltpu.CompilerParams(vmem_limit_bytes=16 * 2**20),
        cost_estimate=pl.CostEstimate(flops=0, bytes_accessed=2**20, transcendentals=0),
    )(position, near, far)


def on_device(inputs, queries, w_kv, doc_lengths, grad_out):
    bf16, f32 = jnp.bfloat16, jnp.float32
    tokens = inputs[0]
    query_rows = queries[0]
    cotangent = grad_out[0]
    lengths = doc_lengths[0]
    rows, width = tokens.shape
    total = SEQ * rows
    half_kv = KVH * HD
    seqs = lax.axis_size("fsdp")
    depth = w_kv.shape[0]
    here = lax.axis_index("seq")
    own_seq = lax.axis_index("fsdp")
    plane, side, core = here >> 2, (here >> 1) & 1, here & 1
    origins = [(own_seq - o) % seqs for o in range(seqs)]

    first = core * half_kv + side * 256
    w_own = jnp.concatenate(
        [columns(w_kv, first, 256), columns(w_kv, first + half_kv // 2, 256)], axis=1
    )
    w_parts = [w_own] + [shift_rows(w_own, o) for o in range(1, seqs)]
    if depth % HD:
        w_full = jnp.zeros((width, PLANES * HD), bf16)
        for o in range(seqs):
            w_full = lax.dynamic_update_slice_in_dim(w_full, w_parts[o], origins[o] * depth, 0)
        w_parts, places_of = [w_full], [jnp.int32(0)]
    else:
        places_of = origins
    position = jnp.stack([plane, side, core] + places_of).astype(jnp.int32)

    pieces = [tokens] + [swap(tokens, mask) for mask in (2, 1, 3)]

    def for_plane(at):
        start = (at >> 1) * 1024 + (at & 1) * 256
        return jnp.stack(
            [
                jnp.concatenate([columns(a, start, 256), columns(a, start + 512, 256)], axis=1)
                for a in (query_rows, cotangent)
            ]
        )

    by_plane = jnp.stack(
        [for_plane(plane)]
        + [shift_planes(for_plane((plane + k) & 3), k) for k in range(1, PLANES)]
    )
    crossed = swap_sides(columns(by_plane, (1 - side) * 256, 256))
    by_side = jnp.stack([columns(by_plane, side * 256, 256), crossed])
    kept = columns(by_side, core * HD, HD)
    came = swap_cores(columns(by_side, (1 - core) * HD, HD))

    places = jnp.arange(total, dtype=jnp.int32)
    doc_ends = jnp.cumsum(lengths)
    ended = doc_ends[None, :] <= places[:, None]
    within = places - jnp.sum(jnp.where(ended, lengths[None, :], 0), axis=1)
    exponent = jnp.arange(HD // 2, dtype=f32) * (2.0 / HD)
    rate = jnp.power(ROPE_BASE, -exponent)
    angles = within.astype(f32)[:, None] * rate[None, :]
    cos_half, sin_half = jnp.cos(angles), jnp.sin(angles)
    cosine = jnp.concatenate([cos_half, cos_half], axis=1)
    sine = jnp.concatenate([-sin_half, sin_half], axis=1)

    kv_blocks = project(position, cosine, sine, pieces, w_parts)
    own = [kv_blocks[0]] + [shift_planes(kv_blocks[k], k) for k in range(1, PLANES)]
    other = [swap_cores(part) for part in own]

    near = jnp.concatenate(pieces[:2], axis=0)
    of_seqs = jnp.stack(
        [columns(near, own_seq * depth, depth)]
        + [
            shift_rows(columns(near, ((own_seq + o) % seqs) * depth, depth), o)
            for o in range(1, seqs)
        ]
    )
    of_planes = jnp.stack([of_seqs, swap(of_seqs, 4)], axis=1)
    pair_tokens = jnp.stack([of_planes, swap_cores(of_planes)], axis=1)
    pair_tokens = pair_tokens.reshape(seqs * 8 * rows, depth)

    out_parts, keep, send = attention(
        lengths, position, kept, came, cosine, sine, own, other
    )

    grads = (keep + swap_cores(send).astype(f32)).astype(bf16)
    grads = grads.reshape(2, 2, 2, 2 * rows, HD)
    mine = grads[0]
    its = swap(grads[1], 8)

    finished = 0.0
    for ar, part in enumerate((mine, its)):
        flat = part.reshape(8 * rows, HD)
        of_all = jnp.concatenate([flat] + [shift_rows(flat, o) for o in range(1, seqs)], axis=0)
        term = lax.dot_general(
            pair_tokens, of_all, (((0,), (0,)), ((), ())), preferred_element_type=f32
        ).astype(bf16)
        pairs = []
        for s in range(SEQ):
            half = (s // 8 + ar) % 2
            pairs.append((s, (2 * (s % 2) + half) * 4 + (s & 2) + (s // 4) % 2))
        finished = finished + lax.ppermute(term, "seq", pairs).astype(f32)

    beside = swap(jnp.stack([mine[:, 1], its[:, 1]]), 4)
    for_core = input_terms(position, mine, its, beside, w_parts)
    for_self, for_side = input_terms(
        position, mine, its, beside, w_parts, swap_cores(for_core)
    )
    grad_rows = (for_self + swap_sides(for_side).astype(f32)).astype(bf16)

    out_parts, its = lax.optimization_barrier((out_parts, its))
    outs = jnp.stack(
        [out_parts[0]] + [shift_planes(out_parts[k], k) for k in range(1, PLANES)]
    )
    by_core = jnp.stack([outs[:, 0], swap_cores(outs[:, 1])])
    out_rows = place_heads(position, by_core[:, :, 0], swap_sides(by_core[:, :, 1]))
    return (out_rows[None], grad_rows[None], finished)


def solution(mesh):
    in_specs = (
        P("fsdp", "seq", None),
        P("fsdp", "seq", None),
        P("fsdp", None),
        P("fsdp", None),
        P("fsdp", "seq", None),
    )
    out_specs = (P("fsdp", "seq", None), P("fsdp", "seq", None), P("fsdp", "seq"))
    return jax.shard_map(
        on_device, mesh=mesh, in_specs=in_specs, out_specs=out_specs, check_vma=False
    )
```

```python
import jax
import jax.numpy as jnp
from jax import lax
from jax.experimental import pallas as pl
from jax.experimental.pallas import tpu as pltpu
from jax.sharding import PartitionSpec as P

QH = 16
KVH = 8
HD = 128
WIN = 1024
G = 2

SOFT_CAP = 50.0
QUERY_SCALE = 1.0 / 12.0
ROPE_BASE = 10000.0

SEQ = 16
PLANES = 4
BLK = 256
REACH = WIN // BLK + 1


def shift_planes(value, steps):
    pairs = [(s, (s + 4 * steps) % SEQ) for s in range(SEQ)]
    return lax.ppermute(value, "seq", pairs)


def swap(value, mask):
    return lax.ppermute(value, "seq", [(s, s ^ mask) for s in range(SEQ)])


def swap_sides(value):
    return swap(value, 2)


def swap_cores(value):
    return swap(value, 1)


def shift_rows(value, steps):
    count = lax.axis_size("fsdp")
    return lax.ppermute(value, "fsdp", [(i, (i + steps) % count) for i in range(count)])


def columns(value, start, size):
    return lax.dynamic_slice_in_dim(value, start, size, value.ndim - 1)


def attention_kernel(
    len_ref, pos_ref, kept_ref, came_ref, cos_ref, sin_ref,
    own_0, own_1, own_2, own_3, oth_0, oth_1, oth_2, oth_3,
    out_ref, keep_ref, send_ref,
    q_s, d_s, kv_s, vt_s, e_s, t_s, dk_s, dv_s,
):
    own_refs = (own_0, own_1, own_2, own_3)
    oth_refs = (oth_0, oth_1, oth_2, oth_3)
    plane, side, core = pos_ref[0], pos_ref[1], pos_ref[2]
    rows = out_ref.shape[3]
    total = q_s.shape[0]
    f32 = jnp.float32
    nt = (((1,), (1,)), ((), ()))

    def flipped(bit, flip):
        return 1 - bit if flip else bit

    for step in range(PLANES):
        at_plane = lax.rem(plane + (PLANES - step), PLANES)
        for xr in range(2):
            for cr in range(2):
                base = at_plane * (4 * rows) + flipped(side, xr) * (2 * rows)
                mine = pl.multiple_of(base + flipped(core, cr) * rows, rows)
                theirs = pl.multiple_of(base + flipped(core, 1 - cr) * rows, rows)
                source = came_ref if cr else kept_ref
                q_s[pl.ds(mine, rows), :] = source[xr, step, 0]
                d_s[pl.ds(mine, rows), :] = source[xr, step, 1]
                piece = pl.ds((2 * cr + xr) * rows, rows)
                kv_s[core, pl.ds(mine, rows), :] = own_refs[step][piece, :]
                kv_s[1 - core, pl.ds(theirs, rows), :] = oth_refs[step][piece, :]

    for block in range(total // BLK):
        span = pl.ds(block * BLK, BLK)
        vt_s[:, span] = kv_s[1, span, :].astype(f32).T.astype(jnp.bfloat16)
    dk_s[...] = jnp.zeros_like(dk_s)
    dv_s[...] = jnp.zeros_like(dv_s)

    ends = []
    run = 0
    for j in range(len_ref.shape[0]):
        run = run + len_ref[j]
        ends.append(run)

    def query_block(i, carry):
        base = pl.multiple_of(i * BLK, BLK)
        span = pl.ds(base, BLK)
        qb = q_s[span, :]
        db = d_s[span, :]
        p_row = base + lax.broadcasted_iota(jnp.int32, (1, BLK), 1)
        start_row = jnp.zeros((1, BLK), jnp.int32)
        first = jnp.int32(0)
        for end in ends:
            start_row = jnp.where(end <= p_row, end, start_row)
            first = jnp.where(end <= base, end, first)
        low_row = jnp.maximum(start_row, p_row - (WIN - 1))
        low_block = jnp.maximum(first, jnp.maximum(base - (WIN - 1), 0)) // BLK
        count = i - low_block + 1

        def body(n):
            def key_span(j):
                return pl.ds(pl.multiple_of((low_block + j) * BLK, BLK), BLK)

            norm = jnp.zeros((1, BLK), f32)
            out_t = jnp.zeros((HD, BLK), f32)
            for j in range(n):
                keys = key_span(j)
                scores = lax.dot_general(kv_s[0, keys, :], qb, nt, preferred_element_type=f32)
                squashed = jnp.tanh(scores * (QUERY_SCALE / SOFT_CAP))
                weights = jnp.exp(squashed * SOFT_CAP)
                n_col = (low_block + j) * BLK + lax.broadcasted_iota(jnp.int32, (BLK, 1), 0)
                allowed = n_col >= low_row
                if j == n - 1:
                    allowed = allowed & (n_col <= p_row)
                weights = jnp.where(allowed, weights, 0.0)
                t_s[j] = squashed
                e_s[j] = weights
                norm = norm + jnp.sum(weights, axis=0, keepdims=True)
                out_t = out_t + jnp.dot(
                    vt_s[:, keys], weights.astype(jnp.bfloat16), preferred_element_type=f32
                )
            inverse = 1.0 / norm
            out_f = (out_t * inverse).astype(jnp.bfloat16).astype(f32)
            delta = jnp.sum(db.astype(f32).T * out_f, axis=0, keepdims=True)
            out_b = out_f.T.astype(jnp.bfloat16)
            to_step = lax.rem(i // 2 + PLANES - plane, PLANES)
            to_side = lax.rem(i + side, 2)
            out_ref[to_step, core, to_side] = out_b[:rows]
            out_ref[to_step, 1 - core, to_side] = out_b[rows:]
            for j in range(n):
                keys = key_span(j)
                probs = e_s[j] * inverse
                squashed = t_s[j]
                dv_s[keys, :] += jnp.dot(
                    probs.astype(jnp.bfloat16), db, preferred_element_type=f32
                )
                dprob = lax.dot_general(kv_s[1, keys, :], db, nt, preferred_element_type=f32)
                dscore = probs * (dprob - delta) * (1.0 - squashed * squashed)
                dk_s[keys, :] += jnp.dot(
                    dscore.astype(jnp.bfloat16), qb, preferred_element_type=f32
                )

        for n in range(1, REACH + 1):
            pl.when(count == n)(lambda n=n: body(n))
        return carry

    lax.fori_loop(0, total // BLK, query_block, 0)

    def finish(block, carry):
        span = pl.ds(pl.multiple_of(block * rows, rows), rows)
        key_part = dk_s[span, :] * QUERY_SCALE
        key_part = key_part * cos_ref[span, :] - pltpu.roll(key_part, HD // 2, 1) * sin_ref[span, :]
        value_part = dv_s[span, :]
        to_pair = lax.rem(block // 8 + plane // 2, 2)
        to_plane = lax.rem(block // 4 + plane, 2)
        to_side = lax.rem(block // 2 + side, 2)
        to_core = lax.rem(block + core, 2)
        is_key = core == 0
        at = pl.ds(pl.multiple_of(to_side * rows, rows), rows)
        keep_ref[to_pair, to_core, to_plane, at, :] = jnp.where(is_key, key_part, value_part)
        send_ref[to_pair, 1 - to_core, to_plane, at, :] = jnp.where(
            is_key, value_part, key_part
        ).astype(jnp.bfloat16)
        return carry

    lax.fori_loop(0, total // rows, finish, 0)


def vmem_specs(count):
    return [pl.BlockSpec(memory_space=pltpu.VMEM)] * count


def smem_specs(count):
    return [pl.BlockSpec(memory_space=pltpu.SMEM)] * count


def attention(lengths, position, kept, came, cosine, sine, own, other):
    rows = kept.shape[3]
    total = SEQ * rows
    bf16, f32 = jnp.bfloat16, jnp.float32
    pairs = 30 * BLK * BLK
    return pl.pallas_call(
        attention_kernel,
        out_shape=(
            jax.ShapeDtypeStruct((PLANES, 2, 2, rows, HD), bf16),
            jax.ShapeDtypeStruct((2, 2, 2, 2 * rows, HD), f32),
            jax.ShapeDtypeStruct((2, 2, 2, 2 * rows, HD), bf16),
        ),
        in_specs=smem_specs(2) + vmem_specs(12),
        out_specs=vmem_specs(3),
        scratch_shapes=[
            pltpu.VMEM((total, HD), bf16),
            pltpu.VMEM((total, HD), bf16),
            pltpu.VMEM((2, total, HD), bf16),
            pltpu.VMEM((HD, total), bf16),
            pltpu.VMEM((REACH, BLK, BLK), f32),
            pltpu.VMEM((REACH, BLK, BLK), f32),
            pltpu.VMEM((total, HD), f32),
            pltpu.VMEM((total, HD), f32),
        ],
        compiler_params=pltpu.CompilerParams(vmem_limit_bytes=40 * 2**20),
        cost_estimate=pl.CostEstimate(
            flops=10 * pairs * HD, bytes_accessed=7 * 2**20, transcendentals=2 * pairs
        ),
    )(lengths, position, kept, came, cosine, sine, *own, *other)


def project_kernel(pos_ref, cos_ref, sin_ref, *refs):
    tok_refs, w_refs, out_ref = refs[:4], refs[4:-1], refs[-1]
    plane, side, core = pos_ref[0], pos_ref[1], pos_ref[2]
    rows = tok_refs[0].shape[0]
    is_key = core == 0
    for half in range(PLANES // 2):
        acc = jnp.zeros((4 * rows, 2 * HD), jnp.float32)
        for o, w_ref in enumerate(w_refs):
            depth = w_ref.shape[0]
            span = pl.ds(pl.multiple_of(pos_ref[3 + o] * depth, HD), depth)
            part = jnp.concatenate([t[:, span] for t in tok_refs], axis=0)
            acc = acc + jnp.dot(
                part,
                w_ref[:, half * 2 * HD : (half + 1) * 2 * HD],
                preferred_element_type=jnp.float32,
            )
        for b in range(2):
            step = lax.rem(2 * half + b + PLANES - plane, PLANES)
            for piece in range(4):
                x = 1 - side if piece % 2 else side
                c = 1 - core if piece // 2 else core
                start = pl.multiple_of((plane * 4 + 2 * x + c) * rows, rows)
                head = acc[piece * rows : (piece + 1) * rows, b * HD : (b + 1) * HD]
                cosine = jnp.where(is_key, cos_ref[pl.ds(start, rows), :], 1.0)
                sine = jnp.where(is_key, sin_ref[pl.ds(start, rows), :], 0.0)
                turned = head * cosine + pltpu.roll(head, HD // 2, 1) * sine
                out_ref[step, piece * rows : (piece + 1) * rows] = turned.astype(jnp.bfloat16)


def project(position, cosine, sine, pieces, weights):
    rows, width = pieces[0].shape
    return pl.pallas_call(
        project_kernel,
        out_shape=jax.ShapeDtypeStruct((PLANES, 4 * rows, HD), jnp.bfloat16),
        in_specs=smem_specs(1) + vmem_specs(6 + len(weights)),
        out_specs=vmem_specs(1)[0],
        compiler_params=pltpu.CompilerParams(vmem_limit_bytes=32 * 2**20),
        cost_estimate=pl.CostEstimate(
            flops=2 * 4 * rows * width * PLANES * HD, bytes_accessed=7 * 2**20, transcendentals=0
        ),
    )(position, cosine, sine, *pieces, *weights)


def fill_columns(pos_ref, cr, mine_ref, its_ref, near_mine_ref, near_its_ref, grad_s):
    for ar in range(2):
        for br in range(2):
            block = pos_ref[0] ^ (2 * ar + br)
            if br:
                value = (near_its_ref if ar else near_mine_ref)[cr]
            else:
                value = (its_ref if ar else mine_ref)[cr, 0]
            grad_s[:, pl.ds(pl.multiple_of(block * HD, HD), HD)] = value


def other_core_kernel(pos_ref, mine_ref, its_ref, near_mine_ref, near_its_ref, *refs):
    w_refs, out_ref, grad_s = refs[:-2], refs[-2], refs[-1]
    fill_columns(pos_ref, 1, mine_ref, its_ref, near_mine_ref, near_its_ref, grad_s)
    for o, w_ref in enumerate(w_refs):
        depth = w_ref.shape[0]
        span = pl.ds(pl.multiple_of(pos_ref[3 + o] * depth, HD), depth)
        out_ref[:, span] = lax.dot_general(
            grad_s[...], w_ref[...], (((1,), (1,)), ((), ())), preferred_element_type=jnp.float32
        ).astype(out_ref.dtype)


def same_core_kernel(pos_ref, mine_ref, its_ref, near_mine_ref, near_its_ref, came_ref, *refs):
    w_refs, (keep_ref, send_ref, grad_s) = refs[:-3], refs[-3:]
    rows = keep_ref.shape[0]
    fill_columns(pos_ref, 0, mine_ref, its_ref, near_mine_ref, near_its_ref, grad_s)
    for o, w_ref in enumerate(w_refs):
        depth = w_ref.shape[0]
        span = pl.ds(pl.multiple_of(pos_ref[3 + o] * depth, HD), depth)
        term = lax.dot_general(
            grad_s[...], w_ref[...], (((1,), (1,)), ((), ())), preferred_element_type=jnp.float32
        ) + came_ref[:, span].astype(jnp.float32)
        keep_ref[:, span] = term[:rows]
        send_ref[:, span] = term[rows:].astype(send_ref.dtype)


def input_terms(position, blocks, weights, came=None):
    rows = blocks[0].shape[2]
    width = sum(w.shape[0] for w in weights)
    bf16 = jnp.bfloat16
    if came is None:
        kernel, extra = other_core_kernel, ()
        shapes = jax.ShapeDtypeStruct((rows, width), bf16)
        out_specs = vmem_specs(1)[0]
    else:
        kernel, extra = same_core_kernel, (came,)
        shapes = (
            jax.ShapeDtypeStruct((rows // 2, width), jnp.float32),
            jax.ShapeDtypeStruct((rows // 2, width), bf16),
        )
        out_specs = vmem_specs(2)
    return pl.pallas_call(
        kernel,
        out_shape=shapes,
        in_specs=smem_specs(1) + vmem_specs(4 + len(extra) + len(weights)),
        out_specs=out_specs,
        scratch_shapes=[pltpu.VMEM((rows, PLANES * HD), bf16)],
        compiler_params=pltpu.CompilerParams(vmem_limit_bytes=32 * 2**20),
        cost_estimate=pl.CostEstimate(
            flops=2 * rows * width * PLANES * HD, bytes_accessed=5 * 2**20, transcendentals=0
        ),
    )(position, *blocks, *extra, *weights)


def after(values, *earlier):
    count = len(values)
    anywhere = pl.BlockSpec(memory_space=pl.ANY)
    return pl.pallas_call(
        lambda *refs: None,
        out_shape=tuple(jax.ShapeDtypeStruct(v.shape, v.dtype) for v in values),
        in_specs=[anywhere] * (count + len(earlier)),
        out_specs=(anywhere,) * count,
        input_output_aliases={i: i for i in range(count)},
    )(*values, *earlier)


def simple_kernel(kernel, shapes, scalars, arrays, earlier=()):
    anywhere = pl.BlockSpec(memory_space=pl.ANY)
    moved = sum(a.size * a.dtype.itemsize for a in arrays)
    return pl.pallas_call(
        kernel,
        out_shape=shapes,
        in_specs=smem_specs(1) + vmem_specs(len(arrays)) + [anywhere] * len(earlier),
        out_specs=jax.tree.map(lambda _: vmem_specs(1)[0], shapes),
        compiler_params=pltpu.CompilerParams(vmem_limit_bytes=24 * 2**20),
        cost_estimate=pl.CostEstimate(flops=0, bytes_accessed=2 * moved, transcendentals=0),
    )(scalars, *arrays, *earlier)


def head_columns(at):
    return (at // 2) * 1024 + lax.rem(at, 2) * 256


def planes_kernel(pos_ref, q_ref, d_ref, _, *out_refs):
    for step, out_ref in enumerate(out_refs, 1):
        start = pl.multiple_of(head_columns(lax.rem(pos_ref[0] + step, PLANES)), 256)
        for i, ref in enumerate((q_ref, d_ref)):
            out_ref[i, :, :256] = ref[:, pl.ds(start, 256)]
            out_ref[i, :, 256:] = ref[:, pl.ds(start + 512, 256)]


def sides_kernel(pos_ref, q_ref, d_ref, one_ref, two_ref, three_ref, _, kept_ref, send_ref):
    plane, side = pos_ref[0], pos_ref[1]
    for out_ref, x in ((kept_ref, side), (send_ref, 1 - side)):
        start = pl.multiple_of(head_columns(plane) + 512 * x, 256)
        for i, ref in enumerate((q_ref, d_ref)):
            out_ref[0, i] = ref[:, pl.ds(start, 256)]
        for step, ref in enumerate((one_ref, two_ref, three_ref), 1):
            out_ref[step] = ref[:, :, pl.ds(pl.multiple_of(256 * x, 256), 256)]


def cores_kernel(pos_ref, same_ref, other_ref, _, kept_ref, send_ref):
    core = pos_ref[2]
    for out_ref, c in ((kept_ref, core), (send_ref, 1 - core)):
        span = pl.ds(pl.multiple_of(HD * c, HD), HD)
        out_ref[0] = same_ref[:, :, :, span]
        out_ref[1] = other_ref[:, :, :, span]


def add_kernel(pos_ref, keep_ref, came_ref, mine_ref, theirs_ref, beside_ref):
    for cr in range(2):
        for pr in range(2):
            total = keep_ref[0, cr, pr] + came_ref[0, cr, pr].astype(jnp.float32)
            mine_ref[cr, pr] = total.astype(mine_ref.dtype)
            if pr:
                beside_ref[cr] = total.astype(mine_ref.dtype)
            total = keep_ref[1, cr, pr] + came_ref[1, cr, pr].astype(jnp.float32)
            theirs_ref[cr, pr] = total.astype(mine_ref.dtype)


def out_cores_kernel(pos_ref, zero_ref, one_ref, two_ref, three_ref, _, kept_ref, send_ref):
    for step, ref in enumerate((zero_ref, one_ref, two_ref, three_ref)):
        kept_ref[step] = ref[0]
        send_ref[step] = ref[1]


def place_kernel(pos_ref, kept_ref, came_ref, far_ref, out_ref):
    plane, side, core = pos_ref[0], pos_ref[1], pos_ref[2]
    for step in range(PLANES):
        home = lax.rem(plane + (PLANES - step), PLANES)
        for hx in range(2):
            for hc in range(2):
                x = 1 - side if hx else side
                c = 1 - core if hc else core
                head = 8 * (home // 2) + 4 * x + 2 * lax.rem(home, 2) + c
                at = pl.ds(pl.multiple_of(head * HD, HD), HD)
                if hx:
                    out_ref[:, at] = far_ref[hc, step]
                else:
                    out_ref[:, at] = (came_ref if hc else kept_ref)[step, 0]


def out_sides_kernel(pos_ref, kept_ref, came_ref, out_ref):
    out_ref[0] = kept_ref[:, 1]
    out_ref[1] = came_ref[:, 1]


def on_device(inputs, queries, w_kv, doc_lengths, grad_out):
    bf16, f32 = jnp.bfloat16, jnp.float32
    tokens = inputs[0]
    query_rows = queries[0]
    cotangent = grad_out[0]
    lengths = doc_lengths[0]
    rows, width = tokens.shape
    total = SEQ * rows
    half_kv = KVH * HD
    seqs = lax.axis_size("fsdp")
    depth = w_kv.shape[0]
    here = lax.axis_index("seq")
    own_seq = lax.axis_index("fsdp")
    plane, side, core = here >> 2, (here >> 1) & 1, here & 1
    origins = [(own_seq - o) % seqs for o in range(seqs)]

    first = core * half_kv + side * 256
    w_own = jnp.concatenate(
        [columns(w_kv, first, 256), columns(w_kv, first + half_kv // 2, 256)], axis=1
    )
    w_parts = [w_own] + [shift_rows(w_own, o) for o in range(1, seqs)]
    if depth % HD:
        w_full = jnp.zeros((width, PLANES * HD), bf16)
        for o in range(seqs):
            w_full = lax.dynamic_update_slice_in_dim(w_full, w_parts[o], origins[o] * depth, 0)
        w_parts, places_of = [w_full], [jnp.int32(0)]
    else:
        places_of = origins
    position = jnp.stack([plane, side, core] + places_of).astype(jnp.int32)

    crossed = swap(tokens, 2)
    pieces = [tokens, crossed, swap(tokens, 1), swap(crossed, 1)]
    beside = swap(tokens, 4)

    def bf16s(*shape):
        return jax.ShapeDtypeStruct(shape, bf16)

    for_planes = simple_kernel(
        planes_kernel, (bf16s(2, rows, 512),) * 3, position, (query_rows, cotangent), (w_own,)
    )
    from_planes = [shift_planes(part, k) for k, part in enumerate(for_planes, 1)]
    same_side, for_side = simple_kernel(
        sides_kernel,
        (bf16s(4, 2, rows, 256),) * 2,
        position,
        (query_rows, cotangent, *from_planes),
        (pieces[3],),
    )
    from_side = swap_sides(for_side)

    places = jnp.arange(total, dtype=jnp.int32)
    doc_ends = jnp.cumsum(lengths)
    ended = doc_ends[None, :] <= places[:, None]
    within = places - jnp.sum(jnp.where(ended, lengths[None, :], 0), axis=1)
    exponent = jnp.arange(HD // 2, dtype=f32) * (2.0 / HD)
    rate = jnp.power(ROPE_BASE, -exponent)
    angles = within.astype(f32)[:, None] * rate[None, :]
    cos_half, sin_half = jnp.cos(angles), jnp.sin(angles)
    cosine = jnp.concatenate([cos_half, cos_half], axis=1)
    sine = jnp.concatenate([-sin_half, sin_half], axis=1)

    kv_blocks = project(position, cosine, sine, pieces, w_parts)
    own = [kv_blocks[0]] + [shift_planes(kv_blocks[k], k) for k in range(1, PLANES)]
    other = [swap_cores(part) for part in own]
    kept, for_other = simple_kernel(
        cores_kernel,
        (bf16s(2, 4, 2, rows, HD),) * 2,
        position,
        (same_side, from_side),
        (kv_blocks,),
    )
    came = swap_cores(for_other)

    near = jnp.concatenate([pieces[0], pieces[1], beside, swap(beside, 2)], axis=0)
    for_seqs = [
        columns(near, ((own_seq + o) % seqs) * depth, depth) for o in range(seqs)
    ]
    for_seqs = [for_seqs[0], *after(for_seqs[1:], kv_blocks)]
    from_seqs = [shift_rows(part, o) if o else part for o, part in enumerate(for_seqs)]

    out_parts, keep, send = attention(
        lengths, position, kept, came, cosine, sine, own, other
    )

    mine, theirs, mine_next = simple_kernel(
        add_kernel,
        (bf16s(2, 2, 2 * rows, HD),) * 2 + (bf16s(2, 2 * rows, HD),),
        position,
        (keep, swap_cores(send)),
    )
    its = swap(theirs, 8)
    mine_seqs = [shift_rows(mine, o) for o in range(1, seqs)]
    beside_mine = swap(mine_next, 4)
    from_seqs = after(from_seqs, mine)
    of_seqs = jnp.stack(from_seqs)
    pair_tokens = jnp.stack([of_seqs, swap_cores(of_seqs)], axis=1)
    pair_tokens = pair_tokens.reshape(seqs * 8 * rows, depth)
    (its,) = after((its,), beside_mine, *mine_seqs)
    its_seqs = [shift_rows(its, o) for o in range(1, seqs)]
    beside_its = swap(its[:, 1], 4)

    def weight_term(ar, parts):
        of_all = jnp.stack(parts).reshape(seqs * 8 * rows, HD)
        term = lax.dot_general(
            pair_tokens, of_all, (((0,), (0,)), ((), ())), preferred_element_type=f32
        ).astype(bf16)
        pairs = []
        for s in range(SEQ):
            half = (s // 8 + ar) % 2
            pairs.append((s, (2 * (s % 2) + half) * 4 + (s & 2) + (s // 4) % 2))
        return lax.ppermute(term, "seq", pairs)

    mine_sum = weight_term(0, [mine, *mine_seqs])

    outs = [out_parts[0], *after([out_parts[k] for k in range(1, PLANES)], its)]
    outs = [shift_planes(part, k) if k else part for k, part in enumerate(outs)]

    blocks = (mine, its, beside_mine, beside_its)
    for_core = input_terms(position, blocks, w_parts)
    for_self, for_side = input_terms(position, blocks, w_parts, swap_cores(for_core))
    from_side = swap_sides(for_side)

    its_sum = weight_term(1, [its, *its_seqs])

    kept_out, out_send = simple_kernel(
        out_cores_kernel, (bf16s(4, 2, rows, HD),) * 2, position, outs, (for_side,)
    )
    came_out = swap_cores(out_send)
    far_send = simple_kernel(
        out_sides_kernel, bf16s(2, 4, rows, HD), position, (kept_out, came_out)
    )
    out_rows = simple_kernel(
        place_kernel,
        bf16s(rows, QH * HD),
        position,
        (kept_out, came_out, swap_sides(far_send)),
    )
    grad_rows = (for_self + from_side.astype(f32)).astype(bf16)
    finished = mine_sum.astype(f32) + its_sum.astype(f32)
    return (out_rows[None], grad_rows[None], finished)


def solution(mesh):
    in_specs = (
        P("fsdp", "seq", None),
        P("fsdp", "seq", None),
        P("fsdp", None),
        P("fsdp", None),
        P("fsdp", "seq", None),
    )
    out_specs = (P("fsdp", "seq", None), P("fsdp", "seq", None), P("fsdp", "seq"))
    return jax.shard_map(
        on_device, mesh=mesh, in_specs=in_specs, out_specs=out_specs, check_vma=False
    )
```

```python
import functools

import jax
import jax.numpy as jnp
from jax import lax
from jax.experimental import pallas as pl
from jax.experimental.pallas import tpu as pltpu
from jax.sharding import PartitionSpec as P

QH = 16
KVH = 8
HD = 128
WIN = 1024
G = 2

SOFT_CAP = 50.0
QUERY_SCALE = 1.0 / 12.0
ROPE_BASE = 10000.0

SEQ = 16
PLANES = 4
BLK = 256
REACH = WIN // BLK + 1

LIGHT = pl.CostEstimate(flops=1, bytes_accessed=1, transcendentals=0)


def shift_planes(value, steps):
    pairs = [(s, (s + 4 * steps) % SEQ) for s in range(SEQ)]
    return lax.ppermute(value, "seq", pairs)


def swap(value, mask):
    return lax.ppermute(value, "seq", [(s, s ^ mask) for s in range(SEQ)])


def swap_sides(value):
    return swap(value, 2)


def swap_cores(value):
    return swap(value, 1)


def shift_rows(value, steps):
    count = lax.axis_size("fsdp")
    return lax.ppermute(value, "fsdp", [(i, (i + steps) % count) for i in range(count)])


def columns(value, start, size):
    return lax.dynamic_slice_in_dim(value, start, size, value.ndim - 1)


def attention_kernel(
    len_ref, pos_ref, kept_ref, came_ref, cos_ref, sin_ref,
    own_0, own_1, own_2, own_3, oth_0, oth_1, oth_2, oth_3,
    out_ref, keep_ref, send_ref,
    q_s, d_s, kv_s, vt_s, e_s, t_s, dk_s, dv_s,
):
    own_refs = (own_0, own_1, own_2, own_3)
    oth_refs = (oth_0, oth_1, oth_2, oth_3)
    plane, side, core = pos_ref[0], pos_ref[1], pos_ref[2]
    rows = out_ref.shape[3]
    total = q_s.shape[0]
    f32 = jnp.float32
    nt = (((1,), (1,)), ((), ()))

    def flipped(bit, flip):
        return 1 - bit if flip else bit

    for step in range(PLANES):
        at_plane = lax.rem(plane + (PLANES - step), PLANES)
        for xr in range(2):
            for cr in range(2):
                base = at_plane * (4 * rows) + flipped(side, xr) * (2 * rows)
                mine = pl.multiple_of(base + flipped(core, cr) * rows, rows)
                theirs = pl.multiple_of(base + flipped(core, 1 - cr) * rows, rows)
                source = came_ref if xr else kept_ref
                q_s[pl.ds(mine, rows), :] = source[step, cr, 0]
                d_s[pl.ds(mine, rows), :] = source[step, cr, 1]
                piece = pl.ds((2 * cr + xr) * rows, rows)
                kv_s[core, pl.ds(mine, rows), :] = own_refs[step][piece, :]
                kv_s[1 - core, pl.ds(theirs, rows), :] = oth_refs[step][piece, :]

    for block in range(total // BLK):
        span = pl.ds(block * BLK, BLK)
        vt_s[:, span] = kv_s[1, span, :].astype(f32).T.astype(jnp.bfloat16)
    dk_s[...] = jnp.zeros_like(dk_s)
    dv_s[...] = jnp.zeros_like(dv_s)

    ends = []
    run = 0
    for j in range(len_ref.shape[0]):
        run = run + len_ref[j]
        ends.append(run)

    def query_block(i, carry):
        base = pl.multiple_of(i * BLK, BLK)
        span = pl.ds(base, BLK)
        qb = q_s[span, :]
        db = d_s[span, :]
        p_row = base + lax.broadcasted_iota(jnp.int32, (1, BLK), 1)
        start_row = jnp.zeros((1, BLK), jnp.int32)
        first = jnp.int32(0)
        for end in ends:
            start_row = jnp.where(end <= p_row, end, start_row)
            first = jnp.where(end <= base, end, first)
        low_row = jnp.maximum(start_row, p_row - (WIN - 1))
        low_block = jnp.maximum(first, jnp.maximum(base - (WIN - 1), 0)) // BLK
        count = i - low_block + 1

        def body(n):
            def key_span(j):
                return pl.ds(pl.multiple_of((low_block + j) * BLK, BLK), BLK)

            norm = jnp.zeros((1, BLK), f32)
            out_t = jnp.zeros((HD, BLK), f32)
            for j in range(n):
                keys = key_span(j)
                scores = lax.dot_general(kv_s[0, keys, :], qb, nt, preferred_element_type=f32)
                squashed = jnp.tanh(scores * (QUERY_SCALE / SOFT_CAP))
                weights = jnp.exp(squashed * SOFT_CAP)
                n_col = (low_block + j) * BLK + lax.broadcasted_iota(jnp.int32, (BLK, 1), 0)
                allowed = n_col >= low_row
                if j == n - 1:
                    allowed = allowed & (n_col <= p_row)
                weights = jnp.where(allowed, weights, 0.0)
                t_s[j] = squashed
                e_s[j] = weights
                norm = norm + jnp.sum(weights, axis=0, keepdims=True)
                out_t = out_t + jnp.dot(
                    vt_s[:, keys], weights.astype(jnp.bfloat16), preferred_element_type=f32
                )
            inverse = 1.0 / norm
            out_f = (out_t * inverse).astype(jnp.bfloat16).astype(f32)
            delta = jnp.sum(db.astype(f32).T * out_f, axis=0, keepdims=True)
            out_b = out_f.T.astype(jnp.bfloat16)
            to_step = lax.rem(i // 2 + PLANES - plane, PLANES)
            to_side = lax.rem(i + side, 2)
            out_ref[to_step, core, to_side] = out_b[:rows]
            out_ref[to_step, 1 - core, to_side] = out_b[rows:]
            for j in range(n):
                keys = key_span(j)
                probs = e_s[j] * inverse
                squashed = t_s[j]
                dv_s[keys, :] += jnp.dot(
                    probs.astype(jnp.bfloat16), db, preferred_element_type=f32
                )
                dprob = lax.dot_general(kv_s[1, keys, :], db, nt, preferred_element_type=f32)
                dscore = probs * (dprob - delta) * (1.0 - squashed * squashed)
                dk_s[keys, :] += jnp.dot(
                    dscore.astype(jnp.bfloat16), qb, preferred_element_type=f32
                )

        for n in range(1, REACH + 1):
            pl.when(count == n)(lambda n=n: body(n))
        return carry

    lax.fori_loop(0, total // BLK, query_block, 0)

    def finish(block, carry):
        span = pl.ds(pl.multiple_of(block * rows, rows), rows)
        key_part = dk_s[span, :] * QUERY_SCALE
        key_part = key_part * cos_ref[span, :] - pltpu.roll(key_part, HD // 2, 1) * sin_ref[span, :]
        value_part = dv_s[span, :]
        to_pair = lax.rem(block // 8 + plane // 2, 2)
        to_plane = lax.rem(block // 4 + plane, 2)
        to_side = lax.rem(block // 2 + side, 2)
        to_core = lax.rem(block + core, 2)
        is_key = core == 0
        at = pl.ds(pl.multiple_of(to_side * rows, rows), rows)
        keep_ref[to_pair, to_core, to_plane, at, :] = jnp.where(is_key, key_part, value_part)
        send_ref[to_pair, 1 - to_core, to_plane, at, :] = jnp.where(
            is_key, value_part, key_part
        ).astype(jnp.bfloat16)
        return carry

    lax.fori_loop(0, total // rows, finish, 0)


def vmem_specs(count):
    return [pl.BlockSpec(memory_space=pltpu.VMEM)] * count


def smem_specs(count):
    return [pl.BlockSpec(memory_space=pltpu.SMEM)] * count


def attention(lengths, position, kept, came, cosine, sine, own, other):
    rows = kept.shape[3]
    total = SEQ * rows
    bf16, f32 = jnp.bfloat16, jnp.float32
    return pl.pallas_call(
        attention_kernel,
        out_shape=(
            jax.ShapeDtypeStruct((PLANES, 2, 2, rows, HD), bf16),
            jax.ShapeDtypeStruct((2, 2, 2, 2 * rows, HD), f32),
            jax.ShapeDtypeStruct((2, 2, 2, 2 * rows, HD), bf16),
        ),
        in_specs=smem_specs(2) + vmem_specs(12),
        out_specs=vmem_specs(3),
        scratch_shapes=[
            pltpu.VMEM((total, HD), bf16),
            pltpu.VMEM((total, HD), bf16),
            pltpu.VMEM((2, total, HD), bf16),
            pltpu.VMEM((HD, total), bf16),
            pltpu.VMEM((REACH, BLK, BLK), f32),
            pltpu.VMEM((REACH, BLK, BLK), f32),
            pltpu.VMEM((total, HD), f32),
            pltpu.VMEM((total, HD), f32),
        ],
        compiler_params=pltpu.CompilerParams(vmem_limit_bytes=40 * 2**20),
        cost_estimate=LIGHT,
    )(lengths, position, kept, came, cosine, sine, *own, *other)


def project_kernel(pos_ref, cos_ref, sin_ref, *refs):
    tok_refs, w_refs, out_ref = refs[:4], refs[4:-1], refs[-1]
    plane, side, core = pos_ref[0], pos_ref[1], pos_ref[2]
    rows = tok_refs[0].shape[0]
    is_key = core == 0
    for half in range(PLANES // 2):
        acc = jnp.zeros((4 * rows, 2 * HD), jnp.float32)
        for o, w_ref in enumerate(w_refs):
            depth = w_ref.shape[0]
            span = pl.ds(pl.multiple_of(pos_ref[3 + o] * depth, HD), depth)
            part = jnp.concatenate([t[:, span] for t in tok_refs], axis=0)
            acc = acc + jnp.dot(
                part,
                w_ref[:, half * 2 * HD : (half + 1) * 2 * HD],
                preferred_element_type=jnp.float32,
            )
        for b in range(2):
            step = lax.rem(2 * half + b + PLANES - plane, PLANES)
            for piece in range(4):
                x = 1 - side if piece % 2 else side
                c = 1 - core if piece // 2 else core
                start = pl.multiple_of((plane * 4 + 2 * x + c) * rows, rows)
                head = acc[piece * rows : (piece + 1) * rows, b * HD : (b + 1) * HD]
                cosine = jnp.where(is_key, cos_ref[pl.ds(start, rows), :], 1.0)
                sine = jnp.where(is_key, sin_ref[pl.ds(start, rows), :], 0.0)
                turned = head * cosine + pltpu.roll(head, HD // 2, 1) * sine
                out_ref[step, piece * rows : (piece + 1) * rows] = turned.astype(jnp.bfloat16)


def project(position, cosine, sine, pieces, weights):
    rows, width = pieces[0].shape
    return pl.pallas_call(
        project_kernel,
        out_shape=jax.ShapeDtypeStruct((PLANES, 4 * rows, HD), jnp.bfloat16),
        in_specs=smem_specs(1) + vmem_specs(6 + len(weights)),
        out_specs=vmem_specs(1)[0],
        compiler_params=pltpu.CompilerParams(vmem_limit_bytes=32 * 2**20),
        cost_estimate=LIGHT,
    )(position, cosine, sine, *pieces, *weights)


def fill_columns(pos_ref, cr, mine_ref, its_ref, near_mine_ref, near_its_ref, grad_s):
    for ar in range(2):
        for br in range(2):
            block = pos_ref[0] ^ (2 * ar + br)
            if br:
                value = (near_its_ref if ar else near_mine_ref)[cr]
            else:
                value = (its_ref if ar else mine_ref)[cr, 0]
            grad_s[:, pl.ds(pl.multiple_of(block * HD, HD), HD)] = value


def other_core_kernel(count, pos_ref, mine_ref, its_ref, near_mine_ref, near_its_ref, *refs):
    w_refs, out_ref, grad_s = refs[:count], refs[-2], refs[-1]
    fill_columns(pos_ref, 1, mine_ref, its_ref, near_mine_ref, near_its_ref, grad_s)
    for o, w_ref in enumerate(w_refs):
        depth = w_ref.shape[0]
        span = pl.ds(pl.multiple_of(pos_ref[3 + o] * depth, HD), depth)
        out_ref[:, span] = lax.dot_general(
            grad_s[...], w_ref[...], (((1,), (1,)), ((), ())), preferred_element_type=jnp.float32
        ).astype(out_ref.dtype)


def same_core_kernel(count, pos_ref, mine_ref, its_ref, near_mine_ref, near_its_ref, came_ref, *refs):
    w_refs, (keep_ref, send_ref, grad_s) = refs[:count], refs[-3:]
    rows = keep_ref.shape[0]
    fill_columns(pos_ref, 0, mine_ref, its_ref, near_mine_ref, near_its_ref, grad_s)
    for o, w_ref in enumerate(w_refs):
        depth = w_ref.shape[0]
        span = pl.ds(pl.multiple_of(pos_ref[3 + o] * depth, HD), depth)
        term = lax.dot_general(
            grad_s[...], w_ref[...], (((1,), (1,)), ((), ())), preferred_element_type=jnp.float32
        ) + came_ref[:, span].astype(jnp.float32)
        keep_ref[:, span] = term[:rows]
        send_ref[:, span] = term[rows:].astype(send_ref.dtype)


def input_terms(position, blocks, weights, earlier, came=None):
    rows = blocks[0].shape[2]
    width = sum(w.shape[0] for w in weights)
    bf16 = jnp.bfloat16
    count = len(weights)
    if came is None:
        kernel, extra = functools.partial(other_core_kernel, count), ()
        shapes = jax.ShapeDtypeStruct((rows, width), bf16)
        out_specs = vmem_specs(1)[0]
    else:
        kernel, extra = functools.partial(same_core_kernel, count), (came,)
        shapes = (
            jax.ShapeDtypeStruct((rows // 2, width), jnp.float32),
            jax.ShapeDtypeStruct((rows // 2, width), bf16),
        )
        out_specs = vmem_specs(2)
    return pl.pallas_call(
        kernel,
        out_shape=shapes,
        in_specs=smem_specs(1)
        + vmem_specs(4 + len(extra) + len(weights))
        + [pl.BlockSpec(memory_space=pl.ANY)] * len(earlier),
        out_specs=out_specs,
        scratch_shapes=[pltpu.VMEM((rows, PLANES * HD), bf16)],
        compiler_params=pltpu.CompilerParams(vmem_limit_bytes=32 * 2**20),
        cost_estimate=LIGHT,
    )(position, *blocks, *extra, *weights, *earlier)


def after(values, *earlier):
    count = len(values)
    anywhere = pl.BlockSpec(memory_space=pl.ANY)
    return pl.pallas_call(
        lambda *refs: None,
        out_shape=tuple(jax.ShapeDtypeStruct(v.shape, v.dtype) for v in values),
        in_specs=[anywhere] * (count + len(earlier)),
        out_specs=(anywhere,) * count,
        input_output_aliases={i: i for i in range(count)},
    )(*values, *earlier)


def simple_kernel(kernel, shapes, scalars, arrays, earlier=()):
    anywhere = pl.BlockSpec(memory_space=pl.ANY)
    return pl.pallas_call(
        kernel,
        out_shape=shapes,
        in_specs=smem_specs(1) + vmem_specs(len(arrays)) + [anywhere] * len(earlier),
        out_specs=jax.tree.map(lambda _: vmem_specs(1)[0], shapes),
        compiler_params=pltpu.CompilerParams(vmem_limit_bytes=32 * 2**20),
        cost_estimate=LIGHT,
    )(scalars, *arrays, *earlier)


def split_cores_kernel(pos_ref, q_ref, d_ref, _, kept_ref, send_ref):
    for out_ref, c in ((kept_ref, pos_ref[2]), (send_ref, 1 - pos_ref[2])):
        for at in range(PLANES):
            for x in range(2):
                head = 8 * (at // 2) + 4 * x + 2 * (at % 2) + c
                span = pl.ds(pl.multiple_of(head * HD, HD), HD)
                for i, ref in enumerate((q_ref, d_ref)):
                    out_ref[i, :, (2 * at + x) * HD : (2 * at + x + 1) * HD] = ref[:, span]


def split_planes_kernel(pos_ref, same_ref, other_ref, *out_refs):
    for step, out_ref in enumerate(out_refs):
        at = lax.rem(pos_ref[0] + step, PLANES)
        span = pl.ds(pl.multiple_of(at * 2 * HD, 2 * HD), 2 * HD)
        out_ref[0] = same_ref[:, :, span]
        out_ref[1] = other_ref[:, :, span]


def split_sides_kernel(pos_ref, zero_ref, one_ref, two_ref, three_ref, kept_ref, send_ref):
    for out_ref, x in ((kept_ref, pos_ref[1]), (send_ref, 1 - pos_ref[1])):
        span = pl.ds(pl.multiple_of(x * HD, HD), HD)
        for step, ref in enumerate((zero_ref, one_ref, two_ref, three_ref)):
            out_ref[step] = ref[:, :, :, span]


def add_kernel(pos_ref, keep_ref, came_ref, mine_ref, theirs_ref, mine_next_ref, theirs_next_ref):
    outs = ((mine_ref, mine_next_ref), (theirs_ref, theirs_next_ref))
    for pair, (all_ref, next_ref) in enumerate(outs):
        for cr in range(2):
            for pr in range(2):
                total = keep_ref[pair, cr, pr] + came_ref[pair, cr, pr].astype(jnp.float32)
                total = total.astype(all_ref.dtype)
                all_ref[cr, pr] = total
                if pr:
                    next_ref[cr] = total


def tokens_kernel(pos_ref, *refs):
    pieces, outs = refs[:4], refs[5:]
    for o, out_ref in enumerate(outs):
        depth = out_ref.shape[1]
        at = lax.rem(pos_ref[3] + o, len(outs))
        span = pl.ds(pl.multiple_of(at * depth, HD), depth)
        for i, piece in enumerate(pieces):
            rows = piece.shape[0]
            out_ref[i * rows : (i + 1) * rows] = piece[:, span]


def weight_kernel(pos_ref, *refs):
    out_refs, ins = refs[-2:], refs[:-2]
    seqs = len(ins) // 4
    tok_refs, grad_refs = ins[: 2 * seqs], ins[2 * seqs :]
    half = tok_refs[0].shape[0]
    acc = 0.0
    for o in range(seqs):
        for cr in range(2):
            part = jnp.concatenate(
                [grad_refs[ar * seqs + o][cr].reshape(half, HD) for ar in range(2)], axis=1
            )
            part = part.astype(jnp.float32).T.astype(jnp.bfloat16)
            acc = acc + jnp.dot(
                part, tok_refs[cr * seqs + o][...], preferred_element_type=jnp.float32
            )
    for ar in range(2):
        out_refs[ar][...] = acc[ar * HD : (ar + 1) * HD].astype(out_refs[ar].dtype)


def finish_kernel(pos_ref, one_ref, two_ref, out_ref):
    total = one_ref[...].astype(jnp.float32) + two_ref[...].astype(jnp.float32)
    out_ref[...] = total.T


def out_cores_kernel(pos_ref, zero_ref, one_ref, two_ref, three_ref, *refs):
    kept_ref, send_ref = refs[-2:]
    for step, ref in enumerate((zero_ref, one_ref, two_ref, three_ref)):
        kept_ref[step] = ref[0]
        send_ref[step] = ref[1]


def place_kernel(pos_ref, kept_ref, came_ref, far_ref, out_ref):
    plane, side, core = pos_ref[0], pos_ref[1], pos_ref[2]
    for step in range(PLANES):
        home = lax.rem(plane + (PLANES - step), PLANES)
        for hx in range(2):
            for hc in range(2):
                x = 1 - side if hx else side
                c = 1 - core if hc else core
                head = 8 * (home // 2) + 4 * x + 2 * lax.rem(home, 2) + c
                at = pl.ds(pl.multiple_of(head * HD, HD), HD)
                if hx:
                    out_ref[:, at] = far_ref[hc, step]
                else:
                    out_ref[:, at] = (came_ref if hc else kept_ref)[step, 0]


def out_sides_kernel(pos_ref, kept_ref, came_ref, out_ref):
    out_ref[0] = kept_ref[:, 1]
    out_ref[1] = came_ref[:, 1]


def on_device(inputs, queries, w_kv, doc_lengths, grad_out):
    bf16, f32 = jnp.bfloat16, jnp.float32
    tokens = inputs[0]
    query_rows = queries[0]
    cotangent = grad_out[0]
    lengths = doc_lengths[0]
    rows, width = tokens.shape
    total = SEQ * rows
    half_kv = KVH * HD
    seqs = lax.axis_size("fsdp")
    depth = w_kv.shape[0]
    here = lax.axis_index("seq")
    own_seq = lax.axis_index("fsdp")
    plane, side, core = here >> 2, (here >> 1) & 1, here & 1
    origins = [(own_seq - o) % seqs for o in range(seqs)]

    first = core * half_kv + side * 256
    w_own = jnp.concatenate(
        [columns(w_kv, first, 256), columns(w_kv, first + half_kv // 2, 256)], axis=1
    )
    w_parts = [w_own] + [shift_rows(w_own, o) for o in range(1, seqs)]
    if depth % HD:
        w_full = jnp.zeros((width, PLANES * HD), bf16)
        for o in range(seqs):
            w_full = lax.dynamic_update_slice_in_dim(w_full, w_parts[o], origins[o] * depth, 0)
        w_parts, places_of = [w_full], [jnp.int32(0)]
    else:
        places_of = origins
    position = jnp.stack([plane, side, core] + places_of).astype(jnp.int32)
    seq_first = jnp.stack([plane, side, core, own_seq]).astype(jnp.int32)

    crossed = swap(tokens, 2)
    pieces = [tokens, crossed, swap(tokens, 1), swap(crossed, 1)]

    def bf16s(*shape):
        return jax.ShapeDtypeStruct(shape, bf16)

    same_core, for_other = simple_kernel(
        split_cores_kernel,
        (bf16s(2, rows, 8 * HD),) * 2,
        position,
        (query_rows, cotangent),
        (w_own,),
    )
    by_planes = simple_kernel(
        split_planes_kernel,
        (bf16s(2, 2, rows, 2 * HD),) * PLANES,
        position,
        (same_core, swap_cores(for_other)),
    )
    by_planes = [shift_planes(p, k) if k else p for k, p in enumerate(by_planes)]
    kept, for_side = simple_kernel(
        split_sides_kernel, (bf16s(PLANES, 2, 2, rows, HD),) * 2, position, by_planes
    )
    came = swap_sides(for_side)
    (tokens_later,) = after((tokens,), by_planes[1])
    beside = swap(tokens_later, 4)

    places = jnp.arange(total, dtype=jnp.int32)
    doc_ends = jnp.cumsum(lengths)
    ended = doc_ends[None, :] <= places[:, None]
    within = places - jnp.sum(jnp.where(ended, lengths[None, :], 0), axis=1)
    exponent = jnp.arange(HD // 2, dtype=f32) * (2.0 / HD)
    rate = jnp.power(ROPE_BASE, -exponent)
    angles = within.astype(f32)[:, None] * rate[None, :]
    cos_half, sin_half = jnp.cos(angles), jnp.sin(angles)
    cosine = jnp.concatenate([cos_half, cos_half], axis=1)
    sine = jnp.concatenate([-sin_half, sin_half], axis=1)

    kv_blocks = project(position, cosine, sine, pieces, w_parts)
    own = [kv_blocks[0]] + [shift_planes(kv_blocks[k], k) for k in range(1, PLANES)]
    other = [swap_cores(part) for part in own]

    near = (pieces[0], pieces[1], beside, swap(beside, 2))
    if depth % HD:
        near = jnp.concatenate(near, axis=0)
        for_seqs = [columns(near, ((own_seq + o) % seqs) * depth, depth) for o in range(seqs)]
    else:
        for_seqs = simple_kernel(
            tokens_kernel, (bf16s(4 * rows, depth),) * seqs, seq_first, near, (own[3],)
        )
    from_seqs = [shift_rows(part, o) if o else part for o, part in enumerate(for_seqs)]

    out_parts, keep, send = attention(
        lengths, position, kept, came, cosine, sine, own, other
    )

    mine, theirs, mine_next, theirs_next = simple_kernel(
        add_kernel,
        (bf16s(2, 2, 2 * rows, HD),) * 2 + (bf16s(2, 2 * rows, HD),) * 2,
        position,
        (keep, swap_cores(send)),
    )
    its = swap(theirs, 8)
    blocks = (mine, its, swap(mine_next, 4), swap(theirs_next, 12))
    mine_seqs = [mine] + [shift_rows(mine, o) for o in range(1, seqs)]
    from_seqs = after(from_seqs, blocks[2], *mine_seqs)
    token_parts = [*from_seqs, *(swap_cores(part) for part in from_seqs)]
    its_seqs = [its] + [shift_rows(its, o) for o in range(1, seqs)]

    outs = [out_parts[0], *after([out_parts[k] for k in range(1, PLANES)], its)]
    outs = [shift_planes(part, k) if k else part for k, part in enumerate(outs)]

    for_core = input_terms(position, blocks, w_parts, mine_seqs[1:])
    for_self, for_side = input_terms(
        position, blocks, w_parts, its_seqs[1:], swap_cores(for_core)
    )
    from_side = swap_sides(for_side)

    terms = simple_kernel(
        weight_kernel, (bf16s(HD, depth),) * 2, position, (*token_parts, *mine_seqs, *its_seqs)
    )
    sums = []
    for ar, term in enumerate(terms):
        pairs = []
        for s in range(SEQ):
            half = (s // 8 + ar) % 2
            pairs.append((s, (2 * (s % 2) + half) * 4 + (s & 2) + (s // 4) % 2))
        sums.append(lax.ppermute(term, "seq", pairs))

    kept_out, out_send = simple_kernel(
        out_cores_kernel, (bf16s(4, 2, rows, HD),) * 2, position, outs, (for_side, terms[0])
    )
    came_out = swap_cores(out_send)
    far_send = simple_kernel(
        out_sides_kernel, bf16s(2, 4, rows, HD), position, (kept_out, came_out)
    )
    out_rows = simple_kernel(
        place_kernel,
        bf16s(rows, QH * HD),
        position,
        (kept_out, came_out, swap_sides(far_send)),
    )
    grad_rows = (for_self + from_side.astype(f32)).astype(bf16)
    finished = simple_kernel(
        finish_kernel, jax.ShapeDtypeStruct((depth, HD), f32), position, sums
    )
    return (out_rows[None], grad_rows[None], finished)


def solution(mesh):
    in_specs = (
        P("fsdp", "seq", None),
        P("fsdp", "seq", None),
        P("fsdp", None),
        P("fsdp", None),
        P("fsdp", "seq", None),
    )
    out_specs = (P("fsdp", "seq", None), P("fsdp", "seq", None), P("fsdp", "seq"))
    return jax.shard_map(
        on_device, mesh=mesh, in_specs=in_specs, out_specs=out_specs, check_vma=False
    )
```

```python
import functools

import jax
import jax.numpy as jnp
from jax import lax
from jax.experimental import pallas as pl
from jax.experimental.pallas import tpu as pltpu
from jax.sharding import PartitionSpec as P

QH = 16
KVH = 8
HD = 128
WIN = 1024
G = 2

SOFT_CAP = 50.0
QUERY_SCALE = 1.0 / 12.0
ROPE_BASE = 10000.0

SEQ = 16
PLANES = 4
BLK = 256
REACH = WIN // BLK + 1


def cost(flops, *arrays):
    moved = sum(a.size * a.dtype.itemsize for a in arrays)
    return pl.CostEstimate(flops=flops, bytes_accessed=2 * moved, transcendentals=0)


def swap(value, mask):
    return lax.ppermute(value, "seq", [(s, s ^ mask) for s in range(SEQ)])


def swap_sides(value):
    return swap(value, 2)


def swap_cores(value):
    return swap(value, 1)


def shift_rows(value, steps):
    count = lax.axis_size("fsdp")
    return lax.ppermute(value, "fsdp", [(i, (i + steps) % count) for i in range(count)])


def columns(value, start, size):
    return lax.dynamic_slice_in_dim(value, start, size, value.ndim - 1)


def rotation(table):
    swapped = pltpu.roll(table, HD // 2, 1)
    first = lax.broadcasted_iota(jnp.int32, table.shape, 1) < HD // 2
    return jnp.where(first, table, swapped), jnp.where(first, -swapped, table)


def attention_kernel(
    len_ref, pos_ref, heads_ref, turn_ref, own_ref, oth_ref,
    out_ref, keep_ref, send_ref,
    kv_s, vt_s, e_s, t_s, dk_s, dv_s,
):
    plane, side, core = pos_ref[0], pos_ref[1], pos_ref[2]
    rows = out_ref.shape[1]
    total = dk_s.shape[0]
    f32 = jnp.float32
    nt = (((1,), (1,)), ((), ()))

    def flipped(bit, flip):
        return 1 - bit if flip else bit

    for at in range(PLANES):
        for xr in range(2):
            for cr in range(2):
                base = at * (4 * rows) + flipped(side, xr) * (2 * rows)
                mine = pl.multiple_of(base + flipped(core, cr) * rows, rows)
                theirs = pl.multiple_of(base + flipped(core, 1 - cr) * rows, rows)
                piece = pl.ds((2 * cr + xr) * rows, rows)
                kv_s[core, pl.ds(mine, rows), :] = own_ref[at, piece, :]
                kv_s[1 - core, pl.ds(theirs, rows), :] = oth_ref[at, piece, :]

    for block in range(total // BLK):
        span = pl.ds(block * BLK, BLK)
        vt_s[:, span] = kv_s[1, span, :].astype(f32).T.astype(jnp.bfloat16)
    dk_s[...] = jnp.zeros_like(dk_s)
    dv_s[...] = jnp.zeros_like(dv_s)

    ends = []
    run = 0
    for j in range(len_ref.shape[0]):
        run = run + len_ref[j]
        ends.append(run)

    def query_block(i, carry):
        base = pl.multiple_of(i * BLK, BLK)
        first_part = i * (BLK // rows)
        qb, db = (
            jnp.concatenate([heads_ref[first_part + j, t] for j in range(BLK // rows)], axis=0)
            for t in range(2)
        )
        p_row = base + lax.broadcasted_iota(jnp.int32, (1, BLK), 1)
        start_row = jnp.zeros((1, BLK), jnp.int32)
        first = jnp.int32(0)
        for end in ends:
            start_row = jnp.where(end <= p_row, end, start_row)
            first = jnp.where(end <= base, end, first)
        low_row = jnp.maximum(start_row, p_row - (WIN - 1))
        low_block = jnp.maximum(first, jnp.maximum(base - (WIN - 1), 0)) // BLK
        count = i - low_block + 1

        def body(n):
            def key_span(j):
                return pl.ds(pl.multiple_of((low_block + j) * BLK, BLK), BLK)

            norm = jnp.zeros((1, BLK), f32)
            out_t = jnp.zeros((HD, BLK), f32)
            for j in range(n):
                keys = key_span(j)
                scores = lax.dot_general(kv_s[0, keys, :], qb, nt, preferred_element_type=f32)
                squashed = jnp.tanh(scores * (QUERY_SCALE / SOFT_CAP))
                weights = jnp.exp(squashed * SOFT_CAP)
                n_col = (low_block + j) * BLK + lax.broadcasted_iota(jnp.int32, (BLK, 1), 0)
                allowed = n_col >= low_row
                if j == n - 1:
                    allowed = allowed & (n_col <= p_row)
                weights = jnp.where(allowed, weights, 0.0)
                t_s[j] = squashed
                e_s[j] = weights
                norm = norm + jnp.sum(weights, axis=0, keepdims=True)
                out_t = out_t + jnp.dot(
                    vt_s[:, keys], weights.astype(jnp.bfloat16), preferred_element_type=f32
                )
            inverse = 1.0 / norm
            out_f = (out_t * inverse).astype(jnp.bfloat16).astype(f32)
            delta = jnp.sum(db.astype(f32).T * out_f, axis=0, keepdims=True)
            out_b = out_f.T.astype(jnp.bfloat16)
            for j in range(BLK // rows):
                out_ref[first_part + j] = out_b[j * rows : (j + 1) * rows]
            for j in range(n):
                keys = key_span(j)
                probs = e_s[j] * inverse
                squashed = t_s[j]
                dv_s[keys, :] += jnp.dot(
                    probs.astype(jnp.bfloat16), db, preferred_element_type=f32
                )
                dprob = lax.dot_general(kv_s[1, keys, :], db, nt, preferred_element_type=f32)
                dscore = probs * (dprob - delta) * (1.0 - squashed * squashed)
                dk_s[keys, :] += jnp.dot(
                    dscore.astype(jnp.bfloat16), qb, preferred_element_type=f32
                )

        for n in range(1, REACH + 1):
            pl.when(count == n)(lambda n=n: body(n))
        return carry

    lax.fori_loop(0, total // BLK, query_block, 0)

    def finish(block, carry):
        span = pl.ds(pl.multiple_of(block * rows, rows), rows)
        key_part = dk_s[span, :] * QUERY_SCALE
        cosine, sine = rotation(turn_ref[span, :])
        key_part = key_part * cosine - pltpu.roll(key_part, HD // 2, 1) * sine
        value_part = dv_s[span, :]
        to_pair = lax.rem(block // 8 + plane // 2, 2)
        to_plane = lax.rem(block // 4 + plane, 2)
        to_side = lax.rem(block // 2 + side, 2)
        to_core = lax.rem(block + core, 2)
        is_key = core == 0
        at = pl.ds(pl.multiple_of(to_side * rows, rows), rows)
        keep_ref[to_pair, to_core, to_plane, at, :] = jnp.where(is_key, key_part, value_part)
        send_ref[to_pair, 1 - to_core, to_plane, at, :] = jnp.where(
            is_key, value_part, key_part
        ).astype(jnp.bfloat16)
        return carry

    lax.fori_loop(0, total // rows, finish, 0)


def vmem_specs(count):
    return [pl.BlockSpec(memory_space=pltpu.VMEM)] * count


def smem_specs(count):
    return [pl.BlockSpec(memory_space=pltpu.SMEM)] * count


def attention(lengths, position, heads, turns, own, other):
    rows = heads.shape[2]
    total = SEQ * rows
    bf16, f32 = jnp.bfloat16, jnp.float32
    return pl.pallas_call(
        attention_kernel,
        out_shape=(
            jax.ShapeDtypeStruct((SEQ, rows, HD), bf16),
            jax.ShapeDtypeStruct((2, 2, 2, 2 * rows, HD), f32),
            jax.ShapeDtypeStruct((2, 2, 2, 2 * rows, HD), bf16),
        ),
        in_specs=smem_specs(2) + vmem_specs(4),
        out_specs=vmem_specs(3),
        scratch_shapes=[
            pltpu.VMEM((2, total, HD), bf16),
            pltpu.VMEM((HD, total), bf16),
            pltpu.VMEM((REACH, BLK, BLK), f32),
            pltpu.VMEM((REACH, BLK, BLK), f32),
            pltpu.VMEM((total, HD), f32),
            pltpu.VMEM((total, HD), f32),
        ],
        compiler_params=pltpu.CompilerParams(vmem_limit_bytes=32 * 2**20),
        cost_estimate=cost(300 * BLK * BLK * HD, heads, own, other, turns),
    )(lengths, position, heads, turns, own, other)


def project_kernel(count, pos_ref, turn_ref, *refs):
    tok_refs, w_refs, out_ref = refs[:4], refs[4 : 4 + count], refs[-1]
    plane, side, core = pos_ref[0], pos_ref[1], pos_ref[2]
    rows = tok_refs[0].shape[0]
    is_key = core == 0
    for half in range(PLANES // 2):
        acc = jnp.zeros((4 * rows, 2 * HD), jnp.float32)
        for o, w_ref in enumerate(w_refs):
            depth = w_ref.shape[0]
            span = pl.ds(pl.multiple_of(pos_ref[3 + o] * depth, HD), depth)
            part = jnp.concatenate([t[:, span] for t in tok_refs], axis=0)
            acc = acc + jnp.dot(
                part,
                w_ref[:, half * 2 * HD : (half + 1) * 2 * HD],
                preferred_element_type=jnp.float32,
            )
        for b in range(2):
            at = 2 * half + b
            for piece in range(4):
                x = 1 - side if piece % 2 else side
                c = 1 - core if piece // 2 else core
                start = pl.multiple_of((plane * 4 + 2 * x + c) * rows, rows)
                head = acc[piece * rows : (piece + 1) * rows, b * HD : (b + 1) * HD]
                cosine, sine = rotation(turn_ref[pl.ds(start, rows), :])
                cosine, sine = jnp.where(is_key, cosine, 1.0), jnp.where(is_key, sine, 0.0)
                turned = head * cosine + pltpu.roll(head, HD // 2, 1) * sine
                out_ref[at, piece * rows : (piece + 1) * rows] = turned.astype(jnp.bfloat16)


def project(position, turns, pieces, weights, *earlier):
    rows, width = pieces[0].shape
    return pl.pallas_call(
        functools.partial(project_kernel, len(weights)),
        out_shape=jax.ShapeDtypeStruct((PLANES, 4 * rows, HD), jnp.bfloat16),
        in_specs=smem_specs(1)
        + vmem_specs(5 + len(weights))
        + [pl.BlockSpec(memory_space=pl.ANY)] * len(earlier),
        out_specs=vmem_specs(1)[0],
        compiler_params=pltpu.CompilerParams(vmem_limit_bytes=32 * 2**20),
        cost_estimate=cost(8 * rows * width * PLANES * HD, *pieces, *weights),
    )(position, turns, *pieces, *weights, *earlier)


def fill_columns(pos_ref, cr, mine_ref, its_ref, near_mine_ref, near_its_ref, grad_s):
    for ar in range(2):
        for br in range(2):
            block = pos_ref[0] ^ (2 * ar + br)
            if br:
                value = (near_its_ref if ar else near_mine_ref)[cr]
            else:
                value = (its_ref if ar else mine_ref)[cr, 0]
            grad_s[:, pl.ds(pl.multiple_of(block * HD, HD), HD)] = value


def other_core_kernel(count, pos_ref, mine_ref, its_ref, near_mine_ref, near_its_ref, *refs):
    w_refs, out_ref, grad_s = refs[:count], refs[-2], refs[-1]
    fill_columns(pos_ref, 1, mine_ref, its_ref, near_mine_ref, near_its_ref, grad_s)
    for o, w_ref in enumerate(w_refs):
        depth = w_ref.shape[0]
        span = pl.ds(pl.multiple_of(pos_ref[3 + o] * depth, HD), depth)
        out_ref[:, span] = lax.dot_general(
            grad_s[...], w_ref[...], (((1,), (1,)), ((), ())), preferred_element_type=jnp.float32
        ).astype(out_ref.dtype)


def same_core_kernel(count, pos_ref, mine_ref, its_ref, near_mine_ref, near_its_ref, came_ref, *refs):
    w_refs, (keep_ref, send_ref, grad_s) = refs[:count], refs[-3:]
    rows = keep_ref.shape[0]
    fill_columns(pos_ref, 0, mine_ref, its_ref, near_mine_ref, near_its_ref, grad_s)
    for o, w_ref in enumerate(w_refs):
        depth = w_ref.shape[0]
        span = pl.ds(pl.multiple_of(pos_ref[3 + o] * depth, HD), depth)
        term = lax.dot_general(
            grad_s[...], w_ref[...], (((1,), (1,)), ((), ())), preferred_element_type=jnp.float32
        ) + came_ref[:, span].astype(jnp.float32)
        keep_ref[:, span] = term[:rows]
        send_ref[:, span] = term[rows:].astype(send_ref.dtype)


def input_terms(position, blocks, weights, earlier, came=None):
    rows = blocks[0].shape[2]
    width = sum(w.shape[0] for w in weights)
    bf16 = jnp.bfloat16
    count = len(weights)
    if came is None:
        kernel, extra = functools.partial(other_core_kernel, count), ()
        shapes = jax.ShapeDtypeStruct((rows, width), bf16)
        out_specs = vmem_specs(1)[0]
    else:
        kernel, extra = functools.partial(same_core_kernel, count), (came,)
        shapes = (
            jax.ShapeDtypeStruct((rows // 2, width), jnp.float32),
            jax.ShapeDtypeStruct((rows // 2, width), bf16),
        )
        out_specs = vmem_specs(2)
    return pl.pallas_call(
        kernel,
        out_shape=shapes,
        in_specs=smem_specs(1)
        + vmem_specs(4 + len(extra) + len(weights))
        + [pl.BlockSpec(memory_space=pl.ANY)] * len(earlier),
        out_specs=out_specs,
        scratch_shapes=[pltpu.VMEM((rows, PLANES * HD), bf16)],
        compiler_params=pltpu.CompilerParams(vmem_limit_bytes=32 * 2**20),
        cost_estimate=cost(2 * rows * width * PLANES * HD, *weights),
    )(position, *blocks, *extra, *weights, *earlier)


def after(values, *earlier):
    count = len(values)
    anywhere = pl.BlockSpec(memory_space=pl.ANY)
    return pl.pallas_call(
        lambda *refs: None,
        out_shape=tuple(jax.ShapeDtypeStruct(v.shape, v.dtype) for v in values),
        in_specs=[anywhere] * (count + len(earlier)),
        out_specs=(anywhere,) * count,
        input_output_aliases={i: i for i in range(count)},
    )(*values, *earlier)


def simple_kernel(kernel, shapes, scalars, arrays, earlier=()):
    anywhere = pl.BlockSpec(memory_space=pl.ANY)
    return pl.pallas_call(
        kernel,
        out_shape=shapes,
        in_specs=smem_specs(1) + vmem_specs(len(arrays)) + [anywhere] * len(earlier),
        out_specs=jax.tree.map(lambda _: vmem_specs(1)[0], shapes),
        compiler_params=pltpu.CompilerParams(vmem_limit_bytes=32 * 2**20),
        cost_estimate=cost(0, *arrays),
    )(scalars, *arrays, *earlier)


def head_of(device):
    plane, side, core = device // 4, (device // 2) % 2, device % 2
    return 8 * (plane // 2) + 4 * side + 2 * (plane % 2) + core


def split_heads_kernel(pos_ref, q_ref, d_ref, _, out_ref):
    for device in range(SEQ):
        head = head_of(device)
        for i, ref in enumerate((q_ref, d_ref)):
            out_ref[device, i] = ref[:, head * HD : (head + 1) * HD]


def join_heads_kernel(pos_ref, in_ref, out_ref):
    for device in range(SEQ):
        head = head_of(device)
        out_ref[:, head * HD : (head + 1) * HD] = in_ref[device]


def add_kernel(pos_ref, keep_ref, came_ref, mine_ref, theirs_ref, mine_next_ref, theirs_next_ref):
    outs = ((mine_ref, mine_next_ref), (theirs_ref, theirs_next_ref))
    for pair, (all_ref, next_ref) in enumerate(outs):
        for cr in range(2):
            for pr in range(2):
                total = keep_ref[pair, cr, pr] + came_ref[pair, cr, pr].astype(jnp.float32)
                total = total.astype(all_ref.dtype)
                all_ref[cr, pr] = total
                if pr:
                    next_ref[cr] = total


def weight_kernel(count, pos_ref, grad_ref, *refs):
    tok_refs, out_refs = refs[:8], refs[8 : 8 + count]
    for o, out_ref in enumerate(out_refs):
        depth = out_ref.shape[1]
        at = lax.rem(pos_ref[3] + o, count)
        span = pl.ds(pl.multiple_of(at * depth, HD), depth)
        acc = jnp.zeros(out_ref.shape, jnp.float32)
        for cr in range(2):
            for pr in range(2):
                grad = grad_ref[cr, pr].astype(jnp.float32).T.astype(jnp.bfloat16)
                first = 4 * cr + 2 * pr
                part = jnp.concatenate([t[:, span] for t in tok_refs[first : first + 2]], axis=0)
                acc = acc + jnp.dot(grad, part, preferred_element_type=jnp.float32)
        out_ref[...] = acc.astype(out_ref.dtype)


def sum_kernel(count, pos_ref, *refs):
    total = sum(r[...].astype(jnp.float32) for r in refs[:count])
    refs[-1][...] = total.astype(refs[-1].dtype)


def finish_kernel(pos_ref, one_ref, two_ref, _, out_ref):
    total = one_ref[...].astype(jnp.float32) + two_ref[...].astype(jnp.float32)
    out_ref[...] = total.T


def exchange(value, groups=None):
    return lax.all_to_all(value, "seq", 0, 0, axis_index_groups=groups, tiled=True)


def on_device(inputs, queries, w_kv, doc_lengths, grad_out):
    bf16, f32 = jnp.bfloat16, jnp.float32
    tokens = inputs[0]
    query_rows = queries[0]
    cotangent = grad_out[0]
    lengths = doc_lengths[0]
    rows, width = tokens.shape
    total = SEQ * rows
    half_kv = KVH * HD
    seqs = lax.axis_size("fsdp")
    depth = w_kv.shape[0]
    here = lax.axis_index("seq")
    own_seq = lax.axis_index("fsdp")
    plane, side, core = here >> 2, (here >> 1) & 1, here & 1
    origins = [(own_seq - o) % seqs for o in range(seqs)]

    first = core * half_kv + side * 256
    w_own = jnp.concatenate(
        [columns(w_kv, first, 256), columns(w_kv, first + half_kv // 2, 256)], axis=1
    )
    w_parts = [w_own] + [shift_rows(w_own, o) for o in range(1, seqs)]
    if depth % HD:
        w_full = jnp.zeros((width, PLANES * HD), bf16)
        for o in range(seqs):
            w_full = lax.dynamic_update_slice_in_dim(w_full, w_parts[o], origins[o] * depth, 0)
        w_parts, places_of = [w_full], [jnp.int32(0)]
    else:
        places_of = origins
    position = jnp.stack([plane, side, core] + places_of).astype(jnp.int32)
    seq_first = jnp.stack([plane, side, core, own_seq]).astype(jnp.int32)

    crossed = swap(tokens, 2)
    pieces = [tokens, crossed, swap(tokens, 1), swap(crossed, 1)]

    def bf16s(*shape):
        return jax.ShapeDtypeStruct(shape, bf16)

    heads = exchange(
        simple_kernel(
            split_heads_kernel,
            bf16s(SEQ, 2, rows, HD),
            position,
            (query_rows, cotangent),
            (w_own,),
        )
    )

    places = jnp.arange(total, dtype=jnp.int32)
    doc_ends = jnp.cumsum(lengths)
    ended = doc_ends[None, :] <= places[:, None]
    within = places - jnp.sum(jnp.where(ended, lengths[None, :], 0), axis=1)
    exponent = jnp.arange(HD // 2, dtype=f32) * (2.0 / HD)
    rate = jnp.power(ROPE_BASE, -exponent)
    angles = within.astype(f32)[:, None] * jnp.concatenate([rate, rate])[None, :]
    quarter = jnp.where(jnp.arange(HD) < HD // 2, jnp.float32(jnp.pi / 2), jnp.float32(0.0))
    turns = jnp.sin(angles + quarter[None, :])

    kv_blocks = project(position, turns, pieces, w_parts, heads)
    own = exchange(kv_blocks, [[r + 4 * p for p in range(PLANES)] for r in range(4)])
    other = swap_cores(own)

    (tokens_later,) = after((tokens,), own)
    beside = swap(tokens_later, 4)
    beside_crossed = swap(beside, 2)

    out_parts, keep, send = attention(
        lengths, position, heads, turns, own, other
    )

    mine, theirs, mine_next, theirs_next = simple_kernel(
        add_kernel,
        (bf16s(2, 2, 2 * rows, HD),) * 2 + (bf16s(2, 2 * rows, HD),) * 2,
        position,
        (keep, swap_cores(send)),
    )
    its = swap(theirs, 8)
    blocks = (mine, its, swap(mine_next, 4), swap(theirs_next, 12))
    pair_tokens = [*pieces[:2], beside, beside_crossed]
    pair_tokens += [*pieces[2:], swap_cores(beside), swap_cores(beside_crossed)]

    def weight_sum(grad, *earlier):
        cuts = 1 if depth % HD else seqs
        terms = simple_kernel(
            functools.partial(weight_kernel, cuts),
            (bf16s(HD, width // cuts),) * cuts,
            seq_first,
            (grad, *pair_tokens),
        )
        if cuts < seqs:
            terms = [columns(terms[0], ((own_seq + o) % seqs) * depth, depth) for o in range(seqs)]
        terms = [shift_rows(t, o) if o else t for o, t in enumerate(terms)]
        return simple_kernel(
            functools.partial(sum_kernel, seqs), bf16s(HD, depth), position, terms, earlier
        )

    for_core = input_terms(position, blocks, w_parts, ())
    for_self, for_side = input_terms(position, blocks, w_parts, (), swap_cores(for_core))
    from_side = swap_sides(for_side)

    terms = [weight_sum(mine), weight_sum(its, for_side)]

    sums = []
    for ar, term in enumerate(terms):
        pairs = []
        for s in range(SEQ):
            half = (s // 8 + ar) % 2
            pairs.append((s, (2 * (s % 2) + half) * 4 + (s & 2) + (s // 4) % 2))
        sums.append(lax.ppermute(term, "seq", pairs))

    outs = exchange(after((out_parts,), for_side, terms[1])[0])
    out_rows = simple_kernel(
        join_heads_kernel, bf16s(rows, QH * HD), position, (outs,)
    )
    grad_rows = (for_self + from_side.astype(f32)).astype(bf16)
    finished = simple_kernel(
        finish_kernel, jax.ShapeDtypeStruct((depth, HD), f32), position, sums, (outs,)
    )
    return (out_rows[None], grad_rows[None], finished)


def solution(mesh):
    in_specs = (
        P("fsdp", "seq", None),
        P("fsdp", "seq", None),
        P("fsdp", None),
        P("fsdp", None),
        P("fsdp", "seq", None),
    )
    out_specs = (P("fsdp", "seq", None), P("fsdp", "seq", None), P("fsdp", "seq"))
    return jax.shard_map(
        on_device, mesh=mesh, in_specs=in_specs, out_specs=out_specs, check_vma=False
    )
```

```python
import functools

import jax
import jax.numpy as jnp
from jax import lax
from jax.experimental import pallas as pl
from jax.experimental.pallas import tpu as pltpu
from jax.sharding import PartitionSpec as P

QH = 16
KVH = 8
HD = 128
WIN = 1024
G = 2

SOFT_CAP = 50.0
QUERY_SCALE = 1.0 / 12.0
ROPE_BASE = 10000.0

SEQ = 16
PLANES = 4
BLK = 256
REACH = WIN // BLK + 1


def cost(flops, *arrays):
    moved = sum(a.size * a.dtype.itemsize for a in arrays)
    return pl.CostEstimate(flops=flops, bytes_accessed=2 * moved, transcendentals=0)


def swap(value, mask):
    return lax.ppermute(value, "seq", [(s, s ^ mask) for s in range(SEQ)])


def swap_sides(value):
    return swap(value, 2)


def swap_cores(value):
    return swap(value, 1)


def shift_rows(value, steps):
    count = lax.axis_size("fsdp")
    return lax.ppermute(value, "fsdp", [(i, (i + steps) % count) for i in range(count)])


def columns(value, start, size):
    return lax.dynamic_slice_in_dim(value, start, size, value.ndim - 1)


def rotation(table):
    swapped = pltpu.roll(table, HD // 2, 1)
    first = lax.broadcasted_iota(jnp.int32, table.shape, 1) < HD // 2
    return jnp.where(first, table, swapped), jnp.where(first, -swapped, table)


def attention_kernel(
    len_ref, pos_ref, heads_ref, turn_ref, own_ref, oth_ref, *refs
):
    out_ref, keep_ref, send_ref, kv_s, vt_s, e_s, t_s, dk_s, dv_s = refs[-9:]
    plane, side, core = pos_ref[0], pos_ref[1], pos_ref[2]
    rows = out_ref.shape[1]
    total = dk_s.shape[0]
    f32 = jnp.float32
    nt = (((1,), (1,)), ((), ()))

    def flipped(bit, flip):
        return 1 - bit if flip else bit

    for at in range(PLANES):
        for xr in range(2):
            for cr in range(2):
                base = at * (4 * rows) + flipped(side, xr) * (2 * rows)
                mine = pl.multiple_of(base + flipped(core, cr) * rows, rows)
                theirs = pl.multiple_of(base + flipped(core, 1 - cr) * rows, rows)
                piece = pl.ds((2 * cr + xr) * rows, rows)
                kv_s[core, pl.ds(mine, rows), :] = own_ref[at, piece, :]
                kv_s[1 - core, pl.ds(theirs, rows), :] = oth_ref[at, piece, :]

    for block in range(total // BLK):
        span = pl.ds(block * BLK, BLK)
        vt_s[:, span] = kv_s[1, span, :].astype(f32).T.astype(jnp.bfloat16)
    dk_s[...] = jnp.zeros_like(dk_s)
    dv_s[...] = jnp.zeros_like(dv_s)

    ends = []
    run = 0
    for j in range(len_ref.shape[0]):
        run = run + len_ref[j]
        ends.append(run)

    def query_block(i, carry):
        base = pl.multiple_of(i * BLK, BLK)
        first_part = i * (BLK // rows)
        qb, db = (
            jnp.concatenate([heads_ref[first_part + j, t] for j in range(BLK // rows)], axis=0)
            for t in range(2)
        )
        p_row = base + lax.broadcasted_iota(jnp.int32, (1, BLK), 1)
        start_row = jnp.zeros((1, BLK), jnp.int32)
        first = jnp.int32(0)
        for end in ends:
            start_row = jnp.where(end <= p_row, end, start_row)
            first = jnp.where(end <= base, end, first)
        low_row = jnp.maximum(start_row, p_row - (WIN - 1))
        low_block = jnp.maximum(first, jnp.maximum(base - (WIN - 1), 0)) // BLK
        count = i - low_block + 1

        def body(n):
            def key_span(j):
                return pl.ds(pl.multiple_of((low_block + j) * BLK, BLK), BLK)

            norm = jnp.zeros((1, BLK), f32)
            out_t = jnp.zeros((HD, BLK), f32)
            for j in range(n):
                keys = key_span(j)
                scores = lax.dot_general(kv_s[0, keys, :], qb, nt, preferred_element_type=f32)
                squashed = jnp.tanh(scores * (QUERY_SCALE / SOFT_CAP))
                weights = jnp.exp(squashed * SOFT_CAP)
                n_col = (low_block + j) * BLK + lax.broadcasted_iota(jnp.int32, (BLK, 1), 0)
                allowed = n_col >= low_row
                if j == n - 1:
                    allowed = allowed & (n_col <= p_row)
                weights = jnp.where(allowed, weights, 0.0)
                t_s[j] = squashed
                e_s[j] = weights
                norm = norm + jnp.sum(weights, axis=0, keepdims=True)
                out_t = out_t + jnp.dot(
                    vt_s[:, keys], weights.astype(jnp.bfloat16), preferred_element_type=f32
                )
            inverse = 1.0 / norm
            out_f = (out_t * inverse).astype(jnp.bfloat16).astype(f32)
            delta = jnp.sum(db.astype(f32).T * out_f, axis=0, keepdims=True)
            out_b = out_f.T.astype(jnp.bfloat16)
            for j in range(BLK // rows):
                out_ref[first_part + j] = out_b[j * rows : (j + 1) * rows]
            for j in range(n):
                keys = key_span(j)
                probs = e_s[j] * inverse
                squashed = t_s[j]
                dv_s[keys, :] += jnp.dot(
                    probs.astype(jnp.bfloat16), db, preferred_element_type=f32
                )
                dprob = lax.dot_general(kv_s[1, keys, :], db, nt, preferred_element_type=f32)
                dscore = probs * (dprob - delta) * (1.0 - squashed * squashed)
                dk_s[keys, :] += jnp.dot(
                    dscore.astype(jnp.bfloat16), qb, preferred_element_type=f32
                )

        for n in range(1, REACH + 1):
            pl.when(count == n)(lambda n=n: body(n))
        return carry

    lax.fori_loop(0, total // BLK, query_block, 0)

    def finish(block, carry):
        span = pl.ds(pl.multiple_of(block * rows, rows), rows)
        key_part = dk_s[span, :] * QUERY_SCALE
        cosine, sine = rotation(turn_ref[span, :])
        key_part = key_part * cosine - pltpu.roll(key_part, HD // 2, 1) * sine
        value_part = dv_s[span, :]
        to_pair = lax.rem(block // 8 + plane // 2, 2)
        to_plane = lax.rem(block // 4 + plane, 2)
        to_side = lax.rem(block // 2 + side, 2)
        to_core = lax.rem(block + core, 2)
        is_key = core == 0
        at = pl.ds(pl.multiple_of(to_side * rows, rows), rows)
        keep_ref[to_pair, to_core, to_plane, at, :] = jnp.where(is_key, key_part, value_part)
        send_ref[to_pair, 1 - to_core, to_plane, at, :] = jnp.where(
            is_key, value_part, key_part
        ).astype(jnp.bfloat16)
        return carry

    lax.fori_loop(0, total // rows, finish, 0)


def vmem_specs(count):
    return [pl.BlockSpec(memory_space=pltpu.VMEM)] * count


def smem_specs(count):
    return [pl.BlockSpec(memory_space=pltpu.SMEM)] * count


def attention(lengths, position, heads, turns, own, other, *earlier):
    rows = heads.shape[2]
    total = SEQ * rows
    bf16, f32 = jnp.bfloat16, jnp.float32
    return pl.pallas_call(
        attention_kernel,
        out_shape=(
            jax.ShapeDtypeStruct((SEQ, rows, HD), bf16),
            jax.ShapeDtypeStruct((2, 2, 2, 2 * rows, HD), f32),
            jax.ShapeDtypeStruct((2, 2, 2, 2 * rows, HD), bf16),
        ),
        in_specs=smem_specs(2)
        + vmem_specs(4)
        + [pl.BlockSpec(memory_space=pl.ANY)] * len(earlier),
        out_specs=vmem_specs(3),
        scratch_shapes=[
            pltpu.VMEM((2, total, HD), bf16),
            pltpu.VMEM((HD, total), bf16),
            pltpu.VMEM((REACH, BLK, BLK), f32),
            pltpu.VMEM((REACH, BLK, BLK), f32),
            pltpu.VMEM((total, HD), f32),
            pltpu.VMEM((total, HD), f32),
        ],
        compiler_params=pltpu.CompilerParams(vmem_limit_bytes=22 * 2**20),
        cost_estimate=cost(300 * BLK * BLK * HD, heads, own, other, turns),
    )(lengths, position, heads, turns, own, other, *earlier)


def project_kernel(count, pos_ref, turn_ref, *refs):
    tok_refs, w_refs, out_ref = refs[:4], refs[4 : 4 + count], refs[-1]
    plane, side, core = pos_ref[0], pos_ref[1], pos_ref[2]
    rows = tok_refs[0].shape[0]
    is_key = core == 0
    for half in range(PLANES // 2):
        acc = jnp.zeros((4 * rows, 2 * HD), jnp.float32)
        for o, w_ref in enumerate(w_refs):
            depth = w_ref.shape[0]
            span = pl.ds(pl.multiple_of(pos_ref[3 + o] * depth, HD), depth)
            part = jnp.concatenate([t[:, span] for t in tok_refs], axis=0)
            acc = acc + jnp.dot(
                part,
                w_ref[:, half * 2 * HD : (half + 1) * 2 * HD],
                preferred_element_type=jnp.float32,
            )
        for b in range(2):
            at = 2 * half + b
            for piece in range(4):
                x = 1 - side if piece % 2 else side
                c = 1 - core if piece // 2 else core
                start = pl.multiple_of((plane * 4 + 2 * x + c) * rows, rows)
                head = acc[piece * rows : (piece + 1) * rows, b * HD : (b + 1) * HD]
                cosine, sine = rotation(turn_ref[pl.ds(start, rows), :])
                cosine, sine = jnp.where(is_key, cosine, 1.0), jnp.where(is_key, sine, 0.0)
                turned = head * cosine + pltpu.roll(head, HD // 2, 1) * sine
                out_ref[at, piece * rows : (piece + 1) * rows] = turned.astype(jnp.bfloat16)


def project(position, turns, pieces, weights, *earlier):
    rows, width = pieces[0].shape
    return pl.pallas_call(
        functools.partial(project_kernel, len(weights)),
        out_shape=jax.ShapeDtypeStruct((PLANES, 4 * rows, HD), jnp.bfloat16),
        in_specs=smem_specs(1)
        + vmem_specs(5 + len(weights))
        + [pl.BlockSpec(memory_space=pl.ANY)] * len(earlier),
        out_specs=vmem_specs(1)[0],
        compiler_params=pltpu.CompilerParams(vmem_limit_bytes=20 * 2**20),
        cost_estimate=cost(8 * rows * width * PLANES * HD, *pieces, *weights),
    )(position, turns, *pieces, *weights, *earlier)


def fill_columns(pos_ref, cr, mine_ref, its_ref, near_mine_ref, near_its_ref, grad_s):
    for ar in range(2):
        for br in range(2):
            block = pos_ref[0] ^ (2 * ar + br)
            if br:
                value = (near_its_ref if ar else near_mine_ref)[cr]
            else:
                value = (its_ref if ar else mine_ref)[cr, 0]
            grad_s[:, pl.ds(pl.multiple_of(block * HD, HD), HD)] = value


def other_core_kernel(count, pos_ref, mine_ref, its_ref, near_mine_ref, near_its_ref, *refs):
    w_refs, out_ref, grad_s = refs[:count], refs[-2], refs[-1]
    fill_columns(pos_ref, 1, mine_ref, its_ref, near_mine_ref, near_its_ref, grad_s)
    for o, w_ref in enumerate(w_refs):
        depth = w_ref.shape[0]
        span = pl.ds(pl.multiple_of(pos_ref[3 + o] * depth, HD), depth)
        out_ref[:, span] = lax.dot_general(
            grad_s[...], w_ref[...], (((1,), (1,)), ((), ())), preferred_element_type=jnp.float32
        ).astype(out_ref.dtype)


def same_core_kernel(count, pos_ref, mine_ref, its_ref, near_mine_ref, near_its_ref, came_ref, *refs):
    w_refs, (keep_ref, send_ref, grad_s) = refs[:count], refs[-3:]
    rows = keep_ref.shape[0]
    fill_columns(pos_ref, 0, mine_ref, its_ref, near_mine_ref, near_its_ref, grad_s)
    for o, w_ref in enumerate(w_refs):
        depth = w_ref.shape[0]
        span = pl.ds(pl.multiple_of(pos_ref[3 + o] * depth, HD), depth)
        term = lax.dot_general(
            grad_s[...], w_ref[...], (((1,), (1,)), ((), ())), preferred_element_type=jnp.float32
        ) + came_ref[:, span].astype(jnp.float32)
        keep_ref[:, span] = term[:rows]
        send_ref[:, span] = term[rows:].astype(send_ref.dtype)


def input_terms(position, blocks, weights, earlier, came=None):
    rows = blocks[0].shape[2]
    width = sum(w.shape[0] for w in weights)
    bf16 = jnp.bfloat16
    count = len(weights)
    if came is None:
        kernel, extra = functools.partial(other_core_kernel, count), ()
        shapes = jax.ShapeDtypeStruct((rows, width), bf16)
        out_specs = vmem_specs(1)[0]
    else:
        kernel, extra = functools.partial(same_core_kernel, count), (came,)
        shapes = (
            jax.ShapeDtypeStruct((rows // 2, width), jnp.float32),
            jax.ShapeDtypeStruct((rows // 2, width), bf16),
        )
        out_specs = vmem_specs(2)
    return pl.pallas_call(
        kernel,
        out_shape=shapes,
        in_specs=smem_specs(1)
        + vmem_specs(4 + len(extra) + len(weights))
        + [pl.BlockSpec(memory_space=pl.ANY)] * len(earlier),
        out_specs=out_specs,
        scratch_shapes=[pltpu.VMEM((rows, PLANES * HD), bf16)],
        compiler_params=pltpu.CompilerParams(vmem_limit_bytes=16 * 2**20),
        cost_estimate=cost(2 * rows * width * PLANES * HD, *weights),
    )(position, *blocks, *extra, *weights, *earlier)


def after(values, *earlier):
    count = len(values)
    anywhere = pl.BlockSpec(memory_space=pl.ANY)
    return pl.pallas_call(
        lambda *refs: None,
        out_shape=tuple(jax.ShapeDtypeStruct(v.shape, v.dtype) for v in values),
        in_specs=[anywhere] * (count + len(earlier)),
        out_specs=(anywhere,) * count,
        input_output_aliases={i: i for i in range(count)},
    )(*values, *earlier)


def simple_kernel(kernel, shapes, scalars, arrays, earlier=()):
    anywhere = pl.BlockSpec(memory_space=pl.ANY)
    return pl.pallas_call(
        kernel,
        out_shape=shapes,
        in_specs=smem_specs(1) + vmem_specs(len(arrays)) + [anywhere] * len(earlier),
        out_specs=jax.tree.map(lambda _: vmem_specs(1)[0], shapes),
        compiler_params=pltpu.CompilerParams(vmem_limit_bytes=16 * 2**20),
        cost_estimate=cost(0, *arrays),
    )(scalars, *arrays, *earlier)


def head_of(device):
    plane, side, core = device // 4, (device // 2) % 2, device % 2
    return 8 * (plane // 2) + 4 * side + 2 * (plane % 2) + core


def split_heads_kernel(pos_ref, q_ref, d_ref, *refs):
    out_ref = refs[-1]
    for device in range(SEQ):
        head = head_of(device)
        for i, ref in enumerate((q_ref, d_ref)):
            out_ref[device, i] = ref[:, head * HD : (head + 1) * HD]


def join_heads_kernel(pos_ref, in_ref, out_ref):
    for device in range(SEQ):
        head = head_of(device)
        out_ref[:, head * HD : (head + 1) * HD] = in_ref[device]


def add_kernel(pos_ref, keep_ref, came_ref, mine_ref, theirs_ref, mine_next_ref, theirs_next_ref):
    outs = ((mine_ref, mine_next_ref), (theirs_ref, theirs_next_ref))
    for pair, (all_ref, next_ref) in enumerate(outs):
        for cr in range(2):
            for pr in range(2):
                total = keep_ref[pair, cr, pr] + came_ref[pair, cr, pr].astype(jnp.float32)
                total = total.astype(all_ref.dtype)
                all_ref[cr, pr] = total
                if pr:
                    next_ref[cr] = total


def weight_kernel(count, pos_ref, grad_ref, *refs):
    tok_refs, out_refs = refs[:8], refs[8 : 8 + count]
    for o, out_ref in enumerate(out_refs):
        depth = out_ref.shape[1]
        at = lax.rem(pos_ref[3] + o, count)
        span = pl.ds(pl.multiple_of(at * depth, HD), depth)
        acc = jnp.zeros(out_ref.shape, jnp.float32)
        for cr in range(2):
            for pr in range(2):
                grad = grad_ref[cr, pr].astype(jnp.float32).T.astype(jnp.bfloat16)
                first = 4 * cr + 2 * pr
                part = jnp.concatenate([t[:, span] for t in tok_refs[first : first + 2]], axis=0)
                acc = acc + jnp.dot(grad, part, preferred_element_type=jnp.float32)
        out_ref[...] = acc.astype(out_ref.dtype)


def sum_kernel(count, pos_ref, *refs):
    total = sum(r[...].astype(jnp.float32) for r in refs[:count])
    refs[-1][...] = total.astype(refs[-1].dtype)


def finish_kernel(pos_ref, one_ref, two_ref, _, out_ref):
    total = one_ref[...].astype(jnp.float32) + two_ref[...].astype(jnp.float32)
    out_ref[...] = total.T


def exchange(value, groups=None):
    return lax.all_to_all(value, "seq", 0, 0, axis_index_groups=groups, tiled=True)


def on_device(inputs, queries, w_kv, doc_lengths, grad_out):
    bf16, f32 = jnp.bfloat16, jnp.float32
    tokens = inputs[0]
    query_rows = queries[0]
    cotangent = grad_out[0]
    lengths = doc_lengths[0]
    rows, width = tokens.shape
    total = SEQ * rows
    half_kv = KVH * HD
    seqs = lax.axis_size("fsdp")
    depth = w_kv.shape[0]
    here = lax.axis_index("seq")
    own_seq = lax.axis_index("fsdp")
    plane, side, core = here >> 2, (here >> 1) & 1, here & 1
    origins = [(own_seq - o) % seqs for o in range(seqs)]

    first = core * half_kv + side * 256
    w_own = jnp.concatenate(
        [columns(w_kv, first, 256), columns(w_kv, first + half_kv // 2, 256)], axis=1
    )
    w_parts = [w_own] + [shift_rows(w_own, o) for o in range(1, seqs)]
    if depth % HD:
        w_full = jnp.zeros((width, PLANES * HD), bf16)
        for o in range(seqs):
            w_full = lax.dynamic_update_slice_in_dim(w_full, w_parts[o], origins[o] * depth, 0)
        w_parts, places_of = [w_full], [jnp.int32(0)]
    else:
        places_of = origins
    position = jnp.stack([plane, side, core] + places_of).astype(jnp.int32)
    seq_first = jnp.stack([plane, side, core, own_seq]).astype(jnp.int32)

    crossed, beside = swap(tokens, 2), swap(tokens, 4)
    beside_crossed = swap(beside, 2)
    pieces = [tokens, crossed, swap(tokens, 1), swap(crossed, 1)]
    pieces_beside = [beside, beside_crossed, swap(beside, 1), swap(beside_crossed, 1)]

    places = jnp.arange(total, dtype=jnp.int32)
    doc_ends = jnp.cumsum(lengths)
    ended = doc_ends[None, :] <= places[:, None]
    within = places - jnp.sum(jnp.where(ended, lengths[None, :], 0), axis=1)
    exponent = jnp.arange(HD // 2, dtype=f32) * (2.0 / HD)
    rate = jnp.power(ROPE_BASE, -exponent)
    angles = within.astype(f32)[:, None] * jnp.concatenate([rate, rate])[None, :]
    quarter = jnp.where(jnp.arange(HD) < HD // 2, jnp.float32(jnp.pi / 2), jnp.float32(0.0))
    turns = jnp.sin(angles + quarter[None, :])

    def bf16s(*shape):
        return jax.ShapeDtypeStruct(shape, bf16)

    heads = exchange(
        simple_kernel(
            split_heads_kernel,
            bf16s(SEQ, 2, rows, HD),
            position,
            (query_rows, cotangent),
            (w_own, turns),
        )
    )

    kv_blocks = project(position, turns, pieces, w_parts, heads)
    own = exchange(kv_blocks, [[r + 4 * p for p in range(PLANES)] for r in range(4)])
    other = swap_cores(own)

    out_parts, keep, send = attention(
        lengths, position, heads, turns, own, other, *pieces_beside
    )

    mine, theirs, mine_next, theirs_next = simple_kernel(
        add_kernel,
        (bf16s(2, 2, 2 * rows, HD),) * 2 + (bf16s(2, 2 * rows, HD),) * 2,
        position,
        (keep, swap_cores(send)),
    )
    its = swap(theirs, 8)
    blocks = (mine, its, swap(mine_next, 4), swap(theirs_next, 12))
    pair_tokens = [*pieces[:2], *pieces_beside[:2], *pieces[2:], *pieces_beside[2:]]

    def weight_terms(grad):
        cuts = 1 if depth % HD else seqs
        terms = simple_kernel(
            functools.partial(weight_kernel, cuts),
            (bf16s(HD, width // cuts),) * cuts,
            seq_first,
            (grad, *pair_tokens),
        )
        if cuts < seqs:
            terms = [columns(terms[0], ((own_seq + o) % seqs) * depth, depth) for o in range(seqs)]
        return terms

    def weight_sum(terms, *earlier):
        terms = [shift_rows(t, o) if o else t for o, t in enumerate(terms)]
        return simple_kernel(
            functools.partial(sum_kernel, seqs), bf16s(HD, depth), position, terms, earlier
        )

    mine_terms, its_terms = weight_terms(mine), weight_terms(its)

    for_core = input_terms(position, blocks, w_parts, mine_terms[:1])
    for_self, for_side = input_terms(position, blocks, w_parts, (), swap_cores(for_core))
    from_side = swap_sides(for_side)

    terms = [weight_sum(mine_terms), weight_sum(its_terms, for_side)]

    sums = []
    for ar, term in enumerate(terms):
        pairs = []
        for s in range(SEQ):
            half = (s // 8 + ar) % 2
            pairs.append((s, (2 * (s % 2) + half) * 4 + (s & 2) + (s // 4) % 2))
        sums.append(lax.ppermute(term, "seq", pairs))

    outs = exchange(after((out_parts,), for_side, *terms)[0])
    out_rows = simple_kernel(
        join_heads_kernel, bf16s(rows, QH * HD), position, (outs,)
    )
    grad_rows = (for_self + from_side.astype(f32)).astype(bf16)
    finished = simple_kernel(
        finish_kernel, jax.ShapeDtypeStruct((depth, HD), f32), position, sums, (outs,)
    )
    return (out_rows[None], grad_rows[None], finished)


def solution(mesh):
    in_specs = (
        P("fsdp", "seq", None),
        P("fsdp", "seq", None),
        P("fsdp", None),
        P("fsdp", None),
        P("fsdp", "seq", None),
    )
    out_specs = (P("fsdp", "seq", None), P("fsdp", "seq", None), P("fsdp", "seq"))
    return jax.shard_map(
        on_device, mesh=mesh, in_specs=in_specs, out_specs=out_specs, check_vma=False
    )
```

```python
import functools

import jax
import jax.numpy as jnp
from jax import lax
from jax.experimental import pallas as pl
from jax.experimental.pallas import tpu as pltpu
from jax.sharding import PartitionSpec as P

QH = 16
KVH = 8
HD = 128
WIN = 1024
G = 2

SOFT_CAP = 50.0
QUERY_SCALE = 1.0 / 12.0
ROPE_BASE = 10000.0

SEQ = 16
PLANES = 4
BLK = 256
REACH = WIN // BLK + 1


def cost(flops, *arrays):
    moved = sum(a.size * a.dtype.itemsize for a in arrays)
    return pl.CostEstimate(flops=flops, bytes_accessed=2 * moved, transcendentals=0)


def swap(value, mask):
    return lax.ppermute(value, "seq", [(s, s ^ mask) for s in range(SEQ)])


def swap_sides(value):
    return swap(value, 2)


def swap_cores(value):
    return swap(value, 1)


def shift_rows(value, steps):
    count = lax.axis_size("fsdp")
    return lax.ppermute(value, "fsdp", [(i, (i + steps) % count) for i in range(count)])


def columns(value, start, size):
    return lax.dynamic_slice_in_dim(value, start, size, value.ndim - 1)


def rotation(table):
    swapped = pltpu.roll(table, HD // 2, 1)
    first = lax.broadcasted_iota(jnp.int32, table.shape, 1) < HD // 2
    return jnp.where(first, table, swapped), jnp.where(first, -swapped, table)


def attention_kernel(
    len_ref, pos_ref, heads_ref, turn_ref, own_ref, oth_ref, *refs
):
    out_ref, keep_ref, send_ref, kv_s, vt_s, e_s, t_s, dk_s, dv_s = refs[-9:]
    plane, side, core = pos_ref[0], pos_ref[1], pos_ref[2]
    rows = out_ref.shape[1]
    total = dk_s.shape[0]
    f32 = jnp.float32
    nt = (((1,), (1,)), ((), ()))

    def flipped(bit, flip):
        return 1 - bit if flip else bit

    for at in range(PLANES):
        for xr in range(2):
            for cr in range(2):
                base = at * (4 * rows) + flipped(side, xr) * (2 * rows)
                mine = pl.multiple_of(base + flipped(core, cr) * rows, rows)
                theirs = pl.multiple_of(base + flipped(core, 1 - cr) * rows, rows)
                piece = pl.ds((2 * cr + xr) * rows, rows)
                kv_s[core, pl.ds(mine, rows), :] = own_ref[at, piece, :]
                kv_s[1 - core, pl.ds(theirs, rows), :] = oth_ref[at, piece, :]

    for block in range(total // BLK):
        span = pl.ds(block * BLK, BLK)
        vt_s[:, span] = kv_s[1, span, :].astype(f32).T.astype(jnp.bfloat16)
    dk_s[...] = jnp.zeros_like(dk_s)
    dv_s[...] = jnp.zeros_like(dv_s)

    ends = []
    run = 0
    for j in range(len_ref.shape[0]):
        run = run + len_ref[j]
        ends.append(run)

    def query_block(i, carry):
        base = pl.multiple_of(i * BLK, BLK)
        first_part = i * (BLK // rows)
        qb, db = (
            jnp.concatenate([heads_ref[first_part + j, t] for j in range(BLK // rows)], axis=0)
            for t in range(2)
        )
        p_row = base + lax.broadcasted_iota(jnp.int32, (1, BLK), 1)
        start_row = jnp.zeros((1, BLK), jnp.int32)
        first = jnp.int32(0)
        for end in ends:
            start_row = jnp.where(end <= p_row, end, start_row)
            first = jnp.where(end <= base, end, first)
        low_row = jnp.maximum(start_row, p_row - (WIN - 1))
        low_block = jnp.maximum(first, jnp.maximum(base - (WIN - 1), 0)) // BLK
        count = i - low_block + 1

        def body(n):
            def key_span(j):
                return pl.ds(pl.multiple_of((low_block + j) * BLK, BLK), BLK)

            norm = jnp.zeros((1, BLK), f32)
            out_t = jnp.zeros((HD, BLK), f32)
            for j in range(n):
                keys = key_span(j)
                scores = lax.dot_general(kv_s[0, keys, :], qb, nt, preferred_element_type=f32)
                squashed = jnp.tanh(scores * (QUERY_SCALE / SOFT_CAP))
                weights = jnp.exp(squashed * SOFT_CAP)
                n_col = (low_block + j) * BLK + lax.broadcasted_iota(jnp.int32, (BLK, 1), 0)
                allowed = n_col >= low_row
                if j == n - 1:
                    allowed = allowed & (n_col <= p_row)
                weights = jnp.where(allowed, weights, 0.0)
                t_s[j] = squashed
                e_s[j] = weights
                norm = norm + jnp.sum(weights, axis=0, keepdims=True)
                out_t = out_t + jnp.dot(
                    vt_s[:, keys], weights.astype(jnp.bfloat16), preferred_element_type=f32
                )
            inverse = 1.0 / norm
            out_f = (out_t * inverse).astype(jnp.bfloat16).astype(f32)
            delta = jnp.sum(db.astype(f32).T * out_f, axis=0, keepdims=True)
            out_b = out_f.T.astype(jnp.bfloat16)
            for j in range(BLK // rows):
                out_ref[first_part + j] = out_b[j * rows : (j + 1) * rows]
            for j in range(n):
                keys = key_span(j)
                probs = e_s[j] * inverse
                squashed = t_s[j]
                dv_s[keys, :] += jnp.dot(
                    probs.astype(jnp.bfloat16), db, preferred_element_type=f32
                )
                dprob = lax.dot_general(kv_s[1, keys, :], db, nt, preferred_element_type=f32)
                dscore = probs * (dprob - delta) * (1.0 - squashed * squashed)
                dk_s[keys, :] += jnp.dot(
                    dscore.astype(jnp.bfloat16), qb, preferred_element_type=f32
                )

        for n in range(1, REACH + 1):
            pl.when(count == n)(lambda n=n: body(n))
        return carry

    lax.fori_loop(0, total // BLK, query_block, 0)

    def finish(block, carry):
        span = pl.ds(pl.multiple_of(block * rows, rows), rows)
        key_part = dk_s[span, :] * QUERY_SCALE
        cosine, sine = rotation(turn_ref[span, :])
        key_part = key_part * cosine - pltpu.roll(key_part, HD // 2, 1) * sine
        value_part = dv_s[span, :]
        to_pair = lax.rem(block // 8 + plane // 2, 2)
        to_plane = lax.rem(block // 4 + plane, 2)
        to_side = lax.rem(block // 2 + side, 2)
        to_core = lax.rem(block + core, 2)
        is_key = core == 0
        at = pl.ds(pl.multiple_of(to_side * rows, rows), rows)
        keep_ref[to_pair, to_core, to_plane, at, :] = jnp.where(is_key, key_part, value_part)
        send_ref[to_pair, 1 - to_core, to_plane, at, :] = jnp.where(
            is_key, value_part, key_part
        ).astype(jnp.bfloat16)
        return carry

    lax.fori_loop(0, total // rows, finish, 0)


def vmem_specs(count):
    return [pl.BlockSpec(memory_space=pltpu.VMEM)] * count


def smem_specs(count):
    return [pl.BlockSpec(memory_space=pltpu.SMEM)] * count


def attention(lengths, position, heads, turns, own, other, *earlier):
    rows = heads.shape[2]
    total = SEQ * rows
    bf16, f32 = jnp.bfloat16, jnp.float32
    return pl.pallas_call(
        attention_kernel,
        out_shape=(
            jax.ShapeDtypeStruct((SEQ, rows, HD), bf16),
            jax.ShapeDtypeStruct((2, 2, 2, 2 * rows, HD), f32),
            jax.ShapeDtypeStruct((2, 2, 2, 2 * rows, HD), bf16),
        ),
        in_specs=smem_specs(2)
        + vmem_specs(4)
        + [pl.BlockSpec(memory_space=pl.ANY)] * len(earlier),
        out_specs=vmem_specs(3),
        scratch_shapes=[
            pltpu.VMEM((2, total, HD), bf16),
            pltpu.VMEM((HD, total), bf16),
            pltpu.VMEM((REACH, BLK, BLK), f32),
            pltpu.VMEM((REACH, BLK, BLK), f32),
            pltpu.VMEM((total, HD), f32),
            pltpu.VMEM((total, HD), f32),
        ],
        compiler_params=pltpu.CompilerParams(vmem_limit_bytes=22 * 2**20),
        cost_estimate=cost(300 * BLK * BLK * HD, heads, own, other, turns),
    )(lengths, position, heads, turns, own, other, *earlier)


def project_kernel(count, pos_ref, turn_ref, *refs):
    tok_refs, w_refs, out_ref = refs[:4], refs[4 : 4 + count], refs[-1]
    plane, side, core = pos_ref[0], pos_ref[1], pos_ref[2]
    rows = tok_refs[0].shape[0]
    is_key = core == 0
    for half in range(PLANES // 2):
        acc = jnp.zeros((4 * rows, 2 * HD), jnp.float32)
        for o, w_ref in enumerate(w_refs):
            depth = w_ref.shape[0]
            span = pl.ds(pl.multiple_of(pos_ref[3 + o] * depth, HD), depth)
            part = jnp.concatenate([t[:, span] for t in tok_refs], axis=0)
            acc = acc + jnp.dot(
                part,
                w_ref[:, half * 2 * HD : (half + 1) * 2 * HD],
                preferred_element_type=jnp.float32,
            )
        for b in range(2):
            at = 2 * half + b
            for piece in range(4):
                x = 1 - side if piece % 2 else side
                c = 1 - core if piece // 2 else core
                start = pl.multiple_of((plane * 4 + 2 * x + c) * rows, rows)
                head = acc[piece * rows : (piece + 1) * rows, b * HD : (b + 1) * HD]
                cosine, sine = rotation(turn_ref[pl.ds(start, rows), :])
                cosine, sine = jnp.where(is_key, cosine, 1.0), jnp.where(is_key, sine, 0.0)
                turned = head * cosine + pltpu.roll(head, HD // 2, 1) * sine
                out_ref[at, piece * rows : (piece + 1) * rows] = turned.astype(jnp.bfloat16)


def project(position, turns, pieces, weights, *earlier):
    rows, width = pieces[0].shape
    return pl.pallas_call(
        functools.partial(project_kernel, len(weights)),
        out_shape=jax.ShapeDtypeStruct((PLANES, 4 * rows, HD), jnp.bfloat16),
        in_specs=smem_specs(1)
        + vmem_specs(5 + len(weights))
        + [pl.BlockSpec(memory_space=pl.ANY)] * len(earlier),
        out_specs=vmem_specs(1)[0],
        compiler_params=pltpu.CompilerParams(vmem_limit_bytes=40 * 2**20),
        cost_estimate=cost(8 * rows * width * PLANES * HD, *pieces, *weights),
    )(position, turns, *pieces, *weights, *earlier)


def fill_columns(pos_ref, cr, mine_ref, its_ref, near_mine_ref, near_its_ref, grad_s):
    for ar in range(2):
        for br in range(2):
            block = pos_ref[0] ^ (2 * ar + br)
            if br:
                value = (near_its_ref if ar else near_mine_ref)[cr]
            else:
                value = (its_ref if ar else mine_ref)[cr, 0]
            grad_s[:, pl.ds(pl.multiple_of(block * HD, HD), HD)] = value


def other_core_kernel(count, pos_ref, mine_ref, its_ref, near_mine_ref, near_its_ref, *refs):
    w_refs, out_ref, grad_s = refs[:count], refs[-2], refs[-1]
    fill_columns(pos_ref, 1, mine_ref, its_ref, near_mine_ref, near_its_ref, grad_s)
    for o, w_ref in enumerate(w_refs):
        depth = w_ref.shape[0]
        span = pl.ds(pl.multiple_of(pos_ref[3 + o] * depth, HD), depth)
        out_ref[:, span] = lax.dot_general(
            grad_s[...], w_ref[...], (((1,), (1,)), ((), ())), preferred_element_type=jnp.float32
        ).astype(out_ref.dtype)


def same_core_kernel(count, pos_ref, mine_ref, its_ref, near_mine_ref, near_its_ref, came_ref, *refs):
    w_refs, (keep_ref, send_ref, grad_s) = refs[:count], refs[-3:]
    rows = keep_ref.shape[0]
    fill_columns(pos_ref, 0, mine_ref, its_ref, near_mine_ref, near_its_ref, grad_s)
    for o, w_ref in enumerate(w_refs):
        depth = w_ref.shape[0]
        span = pl.ds(pl.multiple_of(pos_ref[3 + o] * depth, HD), depth)
        term = lax.dot_general(
            grad_s[...], w_ref[...], (((1,), (1,)), ((), ())), preferred_element_type=jnp.float32
        ) + came_ref[:, span].astype(jnp.float32)
        keep_ref[:, span] = term[:rows]
        send_ref[:, span] = term[rows:].astype(send_ref.dtype)


def input_terms(position, blocks, weights, earlier, came=None):
    rows = blocks[0].shape[2]
    width = sum(w.shape[0] for w in weights)
    bf16 = jnp.bfloat16
    count = len(weights)
    if came is None:
        kernel, extra = functools.partial(other_core_kernel, count), ()
        shapes = jax.ShapeDtypeStruct((rows, width), bf16)
        out_specs = vmem_specs(1)[0]
    else:
        kernel, extra = functools.partial(same_core_kernel, count), (came,)
        shapes = (
            jax.ShapeDtypeStruct((rows // 2, width), jnp.float32),
            jax.ShapeDtypeStruct((rows // 2, width), bf16),
        )
        out_specs = vmem_specs(2)
    return pl.pallas_call(
        kernel,
        out_shape=shapes,
        in_specs=smem_specs(1)
        + vmem_specs(4 + len(extra) + len(weights))
        + [pl.BlockSpec(memory_space=pl.ANY)] * len(earlier),
        out_specs=out_specs,
        scratch_shapes=[pltpu.VMEM((rows, PLANES * HD), bf16)],
        compiler_params=pltpu.CompilerParams(vmem_limit_bytes=16 * 2**20),
        cost_estimate=cost(2 * rows * width * PLANES * HD, *weights),
    )(position, *blocks, *extra, *weights, *earlier)


def after(values, *earlier):
    count = len(values)
    anywhere = pl.BlockSpec(memory_space=pl.ANY)
    return pl.pallas_call(
        lambda *refs: None,
        out_shape=tuple(jax.ShapeDtypeStruct(v.shape, v.dtype) for v in values),
        in_specs=[anywhere] * (count + len(earlier)),
        out_specs=(anywhere,) * count,
        input_output_aliases={i: i for i in range(count)},
    )(*values, *earlier)


def simple_kernel(kernel, shapes, scalars, arrays, earlier=()):
    anywhere = pl.BlockSpec(memory_space=pl.ANY)
    return pl.pallas_call(
        kernel,
        out_shape=shapes,
        in_specs=smem_specs(1) + vmem_specs(len(arrays)) + [anywhere] * len(earlier),
        out_specs=jax.tree.map(lambda _: vmem_specs(1)[0], shapes),
        compiler_params=pltpu.CompilerParams(vmem_limit_bytes=16 * 2**20),
        cost_estimate=cost(0, *arrays),
    )(scalars, *arrays, *earlier)


def head_of(device):
    plane, side, core = device // 4, (device // 2) % 2, device % 2
    return 8 * (plane // 2) + 4 * side + 2 * (plane % 2) + core


def split_heads_kernel(pos_ref, q_ref, d_ref, *refs):
    out_ref = refs[-1]
    for device in range(SEQ):
        head = head_of(device)
        for i, ref in enumerate((q_ref, d_ref)):
            out_ref[device, i] = ref[:, head * HD : (head + 1) * HD]


def join_heads_kernel(pos_ref, in_ref, out_ref):
    for device in range(SEQ):
        head = head_of(device)
        out_ref[:, head * HD : (head + 1) * HD] = in_ref[device]


def add_kernel(pos_ref, keep_ref, came_ref, mine_ref, theirs_ref, mine_next_ref, theirs_next_ref):
    outs = ((mine_ref, mine_next_ref), (theirs_ref, theirs_next_ref))
    for pair, (all_ref, next_ref) in enumerate(outs):
        for cr in range(2):
            for pr in range(2):
                total = keep_ref[pair, cr, pr] + came_ref[pair, cr, pr].astype(jnp.float32)
                total = total.astype(all_ref.dtype)
                all_ref[cr, pr] = total
                if pr:
                    next_ref[cr] = total


def weight_kernel(count, pos_ref, grad_ref, *refs):
    tok_refs, out_refs = refs[:8], refs[8 : 8 + count]
    for o, out_ref in enumerate(out_refs):
        depth = out_ref.shape[1]
        at = lax.rem(pos_ref[3] + o, count)
        span = pl.ds(pl.multiple_of(at * depth, HD), depth)
        acc = jnp.zeros(out_ref.shape, jnp.float32)
        for cr in range(2):
            for pr in range(2):
                grad = grad_ref[cr, pr].astype(jnp.float32).T.astype(jnp.bfloat16)
                first = 4 * cr + 2 * pr
                part = jnp.concatenate([t[:, span] for t in tok_refs[first : first + 2]], axis=0)
                acc = acc + jnp.dot(grad, part, preferred_element_type=jnp.float32)
        out_ref[...] = acc.astype(out_ref.dtype)


def sum_kernel(count, pos_ref, *refs):
    total = sum(r[...].astype(jnp.float32) for r in refs[:count])
    refs[-1][...] = total.astype(refs[-1].dtype)


def finish_kernel(pos_ref, one_ref, two_ref, _, out_ref):
    total = one_ref[...].astype(jnp.float32) + two_ref[...].astype(jnp.float32)
    out_ref[...] = total.T


def exchange(value, groups=None):
    return lax.all_to_all(value, "seq", 0, 0, axis_index_groups=groups, tiled=True)


def on_device(inputs, queries, w_kv, doc_lengths, grad_out):
    bf16, f32 = jnp.bfloat16, jnp.float32
    tokens = inputs[0]
    query_rows = queries[0]
    cotangent = grad_out[0]
    lengths = doc_lengths[0]
    rows, width = tokens.shape
    total = SEQ * rows
    half_kv = KVH * HD
    seqs = lax.axis_size("fsdp")
    depth = w_kv.shape[0]
    here = lax.axis_index("seq")
    own_seq = lax.axis_index("fsdp")
    plane, side, core = here >> 2, (here >> 1) & 1, here & 1
    origins = [(own_seq - o) % seqs for o in range(seqs)]

    first = core * half_kv + side * 256
    w_own = jnp.concatenate(
        [columns(w_kv, first, 256), columns(w_kv, first + half_kv // 2, 256)], axis=1
    )
    w_parts = [w_own] + [shift_rows(w_own, o) for o in range(1, seqs)]
    if depth % HD:
        w_full = jnp.zeros((width, PLANES * HD), bf16)
        for o in range(seqs):
            w_full = lax.dynamic_update_slice_in_dim(w_full, w_parts[o], origins[o] * depth, 0)
        w_parts, places_of = [w_full], [jnp.int32(0)]
    else:
        places_of = origins
    position = jnp.stack([plane, side, core] + places_of).astype(jnp.int32)
    seq_first = jnp.stack([plane, side, core, own_seq]).astype(jnp.int32)

    crossed, beside = swap(tokens, 2), swap(tokens, 4)
    beside_crossed = swap(beside, 2)
    pieces = [tokens, crossed, swap(tokens, 1), swap(crossed, 1)]
    pieces_beside = [beside, beside_crossed, swap(beside, 1), swap(beside_crossed, 1)]

    places = jnp.arange(total, dtype=jnp.int32)
    doc_ends = jnp.cumsum(lengths)
    ended = doc_ends[None, :] <= places[:, None]
    within = places - jnp.sum(jnp.where(ended, lengths[None, :], 0), axis=1)
    exponent = jnp.arange(HD // 2, dtype=f32) * (2.0 / HD)
    rate = jnp.power(ROPE_BASE, -exponent)
    angles = within.astype(f32)[:, None] * jnp.concatenate([rate, rate])[None, :]
    quarter = jnp.where(jnp.arange(HD) < HD // 2, jnp.float32(jnp.pi / 2), jnp.float32(0.0))
    turns = jnp.sin(angles + quarter[None, :])

    def bf16s(*shape):
        return jax.ShapeDtypeStruct(shape, bf16)

    heads = exchange(
        simple_kernel(
            split_heads_kernel,
            bf16s(SEQ, 2, rows, HD),
            position,
            (query_rows, cotangent),
            (w_own, turns),
        )
    )

    kv_blocks = project(position, turns, pieces, w_parts, beside)
    (kv_blocks,) = after((kv_blocks,), heads, beside_crossed)
    own = exchange(kv_blocks, [[r + 4 * p for p in range(PLANES)] for r in range(4)])
    other = swap_cores(own)

    out_parts, keep, send = attention(
        lengths, position, heads, turns, own, other, *pieces_beside
    )

    mine, theirs, mine_next, theirs_next = simple_kernel(
        add_kernel,
        (bf16s(2, 2, 2 * rows, HD),) * 2 + (bf16s(2, 2 * rows, HD),) * 2,
        position,
        (keep, swap_cores(send)),
    )
    its = swap(theirs, 8)
    blocks = (mine, its, swap(mine_next, 4), swap(theirs_next, 12))
    pair_tokens = [*pieces[:2], *pieces_beside[:2], *pieces[2:], *pieces_beside[2:]]

    def weight_terms(grad):
        cuts = 1 if depth % HD else seqs
        terms = simple_kernel(
            functools.partial(weight_kernel, cuts),
            (bf16s(HD, width // cuts),) * cuts,
            seq_first,
            (grad, *pair_tokens),
        )
        if cuts < seqs:
            terms = [columns(terms[0], ((own_seq + o) % seqs) * depth, depth) for o in range(seqs)]
        return terms

    def weight_sum(terms, *earlier):
        terms = [shift_rows(t, o) if o else t for o, t in enumerate(terms)]
        return simple_kernel(
            functools.partial(sum_kernel, seqs), bf16s(HD, depth), position, terms, earlier
        )

    mine_sum = weight_sum(weight_terms(mine))
    its_terms = weight_terms(its)

    outs = exchange(after((out_parts,), its, blocks[3])[0])

    for_core = input_terms(position, blocks, w_parts, (mine_sum,))
    for_self, for_side = input_terms(position, blocks, w_parts, (), swap_cores(for_core))
    from_side = swap_sides(for_side)

    terms = [mine_sum, weight_sum(its_terms, for_side)]

    sums = []
    for ar, term in enumerate(terms):
        pairs = []
        for s in range(SEQ):
            half = (s // 8 + ar) % 2
            pairs.append((s, (2 * (s % 2) + half) * 4 + (s & 2) + (s // 4) % 2))
        sums.append(lax.ppermute(term, "seq", pairs))

    out_rows = simple_kernel(
        join_heads_kernel, bf16s(rows, QH * HD), position, (outs,)
    )
    grad_rows = (for_self + from_side.astype(f32)).astype(bf16)
    finished = simple_kernel(
        finish_kernel, jax.ShapeDtypeStruct((depth, HD), f32), position, sums, (outs,)
    )
    return (out_rows[None], grad_rows[None], finished)


def solution(mesh):
    in_specs = (
        P("fsdp", "seq", None),
        P("fsdp", "seq", None),
        P("fsdp", None),
        P("fsdp", None),
        P("fsdp", "seq", None),
    )
    out_specs = (P("fsdp", "seq", None), P("fsdp", "seq", None), P("fsdp", "seq"))
    return jax.shard_map(
        on_device, mesh=mesh, in_specs=in_specs, out_specs=out_specs, check_vma=False
    )
```

```python
import functools

import jax
import jax.numpy as jnp
from jax import lax
from jax.experimental import pallas as pl
from jax.experimental.pallas import tpu as pltpu
from jax.sharding import PartitionSpec as P

QH = 16
KVH = 8
HD = 128
WIN = 1024
G = 2

SOFT_CAP = 50.0
QUERY_SCALE = 1.0 / 12.0
ROPE_BASE = 10000.0

SEQ = 16
PLANES = 4
BLK = 256
REACH = WIN // BLK + 1


def cost(flops, *arrays):
    moved = sum(a.size * a.dtype.itemsize for a in arrays)
    return pl.CostEstimate(flops=flops, bytes_accessed=2 * moved, transcendentals=0)


def shift_planes(value, steps):
    pairs = [(s, (s + 4 * steps) % SEQ) for s in range(SEQ)]
    return lax.ppermute(value, "seq", pairs)


def swap(value, mask):
    return lax.ppermute(value, "seq", [(s, s ^ mask) for s in range(SEQ)])


def swap_sides(value):
    return swap(value, 2)


def swap_cores(value):
    return swap(value, 1)


def shift_rows(value, steps):
    count = lax.axis_size("fsdp")
    return lax.ppermute(value, "fsdp", [(i, (i + steps) % count) for i in range(count)])


def columns(value, start, size):
    return lax.dynamic_slice_in_dim(value, start, size, value.ndim - 1)


def rotation(table):
    swapped = pltpu.roll(table, HD // 2, 1)
    first = lax.broadcasted_iota(jnp.int32, table.shape, 1) < HD // 2
    return jnp.where(first, table, swapped), jnp.where(first, -swapped, table)


def attention_kernel(
    len_ref, pos_ref, kept_ref, came_ref, turn_ref, own_ref, oth_ref, *refs
):
    out_ref, keep_ref, send_ref, q_s, d_s, kv_s, vt_s, e_s, t_s, dk_s, dv_s = refs[-11:]
    plane, side, core = pos_ref[0], pos_ref[1], pos_ref[2]
    rows = out_ref.shape[1]
    total = dk_s.shape[0]
    f32 = jnp.float32
    nt = (((1,), (1,)), ((), ()))

    def flipped(bit, flip):
        return 1 - bit if flip else bit

    for step in range(PLANES):
        home = lax.rem(plane + (PLANES - step), PLANES)
        for xr in range(2):
            for cr in range(2):
                base = home * (4 * rows) + flipped(side, xr) * (2 * rows)
                base = pl.multiple_of(base + flipped(core, cr) * rows, rows)
                source = came_ref if cr else kept_ref
                q_s[pl.ds(base, rows), :] = source[xr, step, 0]
                d_s[pl.ds(base, rows), :] = source[xr, step, 1]

    for at in range(PLANES):
        for xr in range(2):
            for cr in range(2):
                base = at * (4 * rows) + flipped(side, xr) * (2 * rows)
                mine = pl.multiple_of(base + flipped(core, cr) * rows, rows)
                theirs = pl.multiple_of(base + flipped(core, 1 - cr) * rows, rows)
                piece = pl.ds((2 * cr + xr) * rows, rows)
                kv_s[core, pl.ds(mine, rows), :] = own_ref[at, piece, :]
                kv_s[1 - core, pl.ds(theirs, rows), :] = oth_ref[at, piece, :]

    for block in range(total // BLK):
        span = pl.ds(block * BLK, BLK)
        vt_s[:, span] = kv_s[1, span, :].astype(f32).T.astype(jnp.bfloat16)
    dk_s[...] = jnp.zeros_like(dk_s)
    dv_s[...] = jnp.zeros_like(dv_s)

    ends = []
    run = 0
    for j in range(len_ref.shape[0]):
        run = run + len_ref[j]
        ends.append(run)

    def query_block(i, carry):
        base = pl.multiple_of(i * BLK, BLK)
        first_part = i * (BLK // rows)
        qb, db = q_s[pl.ds(base, BLK), :], d_s[pl.ds(base, BLK), :]
        p_row = base + lax.broadcasted_iota(jnp.int32, (1, BLK), 1)
        start_row = jnp.zeros((1, BLK), jnp.int32)
        first = jnp.int32(0)
        for end in ends:
            start_row = jnp.where(end <= p_row, end, start_row)
            first = jnp.where(end <= base, end, first)
        low_row = jnp.maximum(start_row, p_row - (WIN - 1))
        low_block = jnp.maximum(first, jnp.maximum(base - (WIN - 1), 0)) // BLK
        count = i - low_block + 1

        def body(n):
            def key_span(j):
                return pl.ds(pl.multiple_of((low_block + j) * BLK, BLK), BLK)

            norm = jnp.zeros((1, BLK), f32)
            out_t = jnp.zeros((HD, BLK), f32)
            for j in range(n):
                keys = key_span(j)
                scores = lax.dot_general(kv_s[0, keys, :], qb, nt, preferred_element_type=f32)
                squashed = jnp.tanh(scores * (QUERY_SCALE / SOFT_CAP))
                weights = jnp.exp(squashed * SOFT_CAP)
                n_col = (low_block + j) * BLK + lax.broadcasted_iota(jnp.int32, (BLK, 1), 0)
                allowed = n_col >= low_row
                if j == n - 1:
                    allowed = allowed & (n_col <= p_row)
                weights = jnp.where(allowed, weights, 0.0)
                t_s[j] = squashed
                e_s[j] = weights
                norm = norm + jnp.sum(weights, axis=0, keepdims=True)
                out_t = out_t + jnp.dot(
                    vt_s[:, keys], weights.astype(jnp.bfloat16), preferred_element_type=f32
                )
            inverse = 1.0 / norm
            out_f = (out_t * inverse).astype(jnp.bfloat16).astype(f32)
            delta = jnp.sum(db.astype(f32).T * out_f, axis=0, keepdims=True)
            out_b = out_f.T.astype(jnp.bfloat16)
            for j in range(BLK // rows):
                out_ref[first_part + j] = out_b[j * rows : (j + 1) * rows]
            for j in range(n):
                keys = key_span(j)
                probs = e_s[j] * inverse
                squashed = t_s[j]
                dv_s[keys, :] += jnp.dot(
                    probs.astype(jnp.bfloat16), db, preferred_element_type=f32
                )
                dprob = lax.dot_general(kv_s[1, keys, :], db, nt, preferred_element_type=f32)
                dscore = probs * (dprob - delta) * (1.0 - squashed * squashed)
                dk_s[keys, :] += jnp.dot(
                    dscore.astype(jnp.bfloat16), qb, preferred_element_type=f32
                )

        for n in range(1, REACH + 1):
            pl.when(count == n)(lambda n=n: body(n))
        return carry

    lax.fori_loop(0, total // BLK, query_block, 0)

    def finish(block, carry):
        span = pl.ds(pl.multiple_of(block * rows, rows), rows)
        key_part = dk_s[span, :] * QUERY_SCALE
        cosine, sine = rotation(turn_ref[span, :])
        key_part = key_part * cosine - pltpu.roll(key_part, HD // 2, 1) * sine
        value_part = dv_s[span, :]
        to_pair = lax.rem(block // 8 + plane // 2, 2)
        to_plane = lax.rem(block // 4 + plane, 2)
        to_side = lax.rem(block // 2 + side, 2)
        to_core = lax.rem(block + core, 2)
        is_key = core == 0
        at = pl.ds(pl.multiple_of(to_side * rows, rows), rows)
        keep_ref[to_pair, to_core, to_plane, at, :] = jnp.where(is_key, key_part, value_part)
        send_ref[to_pair, 1 - to_core, to_plane, at, :] = jnp.where(
            is_key, value_part, key_part
        ).astype(jnp.bfloat16)
        return carry

    lax.fori_loop(0, total // rows, finish, 0)


def vmem_specs(count):
    return [pl.BlockSpec(memory_space=pltpu.VMEM)] * count


def smem_specs(count):
    return [pl.BlockSpec(memory_space=pltpu.SMEM)] * count


def attention(lengths, position, kept, came, turns, own, other, *earlier):
    rows = kept.shape[3]
    total = SEQ * rows
    bf16, f32 = jnp.bfloat16, jnp.float32
    return pl.pallas_call(
        attention_kernel,
        out_shape=(
            jax.ShapeDtypeStruct((SEQ, rows, HD), bf16),
            jax.ShapeDtypeStruct((2, 2, 2, 2 * rows, HD), f32),
            jax.ShapeDtypeStruct((2, 2, 2, 2 * rows, HD), bf16),
        ),
        in_specs=smem_specs(2)
        + vmem_specs(5)
        + [pl.BlockSpec(memory_space=pl.ANY)] * len(earlier),
        out_specs=vmem_specs(3),
        scratch_shapes=[
            pltpu.VMEM((total, HD), bf16),
            pltpu.VMEM((total, HD), bf16),
            pltpu.VMEM((2, total, HD), bf16),
            pltpu.VMEM((HD, total), bf16),
            pltpu.VMEM((REACH, BLK, BLK), f32),
            pltpu.VMEM((REACH, BLK, BLK), f32),
            pltpu.VMEM((total, HD), f32),
            pltpu.VMEM((total, HD), f32),
        ],
        compiler_params=pltpu.CompilerParams(vmem_limit_bytes=22 * 2**20),
        cost_estimate=cost(300 * BLK * BLK * HD, kept, came, own, other, turns),
    )(lengths, position, kept, came, turns, own, other, *earlier)


def project_kernel(count, pos_ref, turn_ref, *refs):
    tok_refs, w_refs, out_ref = refs[:4], refs[4 : 4 + count], refs[-1]
    plane, side, core = pos_ref[0], pos_ref[1], pos_ref[2]
    rows = tok_refs[0].shape[0]
    is_key = core == 0
    for half in range(PLANES // 2):
        acc = jnp.zeros((4 * rows, 2 * HD), jnp.float32)
        for o, w_ref in enumerate(w_refs):
            depth = w_ref.shape[0]
            span = pl.ds(pl.multiple_of(pos_ref[3 + o] * depth, HD), depth)
            part = jnp.concatenate([t[:, span] for t in tok_refs], axis=0)
            acc = acc + jnp.dot(
                part,
                w_ref[:, half * 2 * HD : (half + 1) * 2 * HD],
                preferred_element_type=jnp.float32,
            )
        for b in range(2):
            at = 2 * half + b
            for piece in range(4):
                x = 1 - side if piece % 2 else side
                c = 1 - core if piece // 2 else core
                start = pl.multiple_of((plane * 4 + 2 * x + c) * rows, rows)
                head = acc[piece * rows : (piece + 1) * rows, b * HD : (b + 1) * HD]
                cosine, sine = rotation(turn_ref[pl.ds(start, rows), :])
                cosine, sine = jnp.where(is_key, cosine, 1.0), jnp.where(is_key, sine, 0.0)
                turned = head * cosine + pltpu.roll(head, HD // 2, 1) * sine
                out_ref[at, piece * rows : (piece + 1) * rows] = turned.astype(jnp.bfloat16)


def project(position, turns, pieces, weights, *earlier):
    rows, width = pieces[0].shape
    return pl.pallas_call(
        functools.partial(project_kernel, len(weights)),
        out_shape=jax.ShapeDtypeStruct((PLANES, 4 * rows, HD), jnp.bfloat16),
        in_specs=smem_specs(1)
        + vmem_specs(5 + len(weights))
        + [pl.BlockSpec(memory_space=pl.ANY)] * len(earlier),
        out_specs=vmem_specs(1)[0],
        compiler_params=pltpu.CompilerParams(vmem_limit_bytes=40 * 2**20),
        cost_estimate=cost(8 * rows * width * PLANES * HD, *pieces, *weights),
    )(position, turns, *pieces, *weights, *earlier)


def fill_columns(pos_ref, cr, mine_ref, its_ref, near_mine_ref, near_its_ref, grad_s):
    for ar in range(2):
        for br in range(2):
            block = pos_ref[0] ^ (2 * ar + br)
            if br:
                value = (near_its_ref if ar else near_mine_ref)[cr]
            else:
                value = (its_ref if ar else mine_ref)[cr, 0]
            grad_s[:, pl.ds(pl.multiple_of(block * HD, HD), HD)] = value


def other_core_kernel(count, pos_ref, mine_ref, its_ref, near_mine_ref, near_its_ref, *refs):
    w_refs, out_ref, grad_s = refs[:count], refs[-2], refs[-1]
    fill_columns(pos_ref, 1, mine_ref, its_ref, near_mine_ref, near_its_ref, grad_s)
    for o, w_ref in enumerate(w_refs):
        depth = w_ref.shape[0]
        span = pl.ds(pl.multiple_of(pos_ref[3 + o] * depth, HD), depth)
        out_ref[:, span] = lax.dot_general(
            grad_s[...], w_ref[...], (((1,), (1,)), ((), ())), preferred_element_type=jnp.float32
        ).astype(out_ref.dtype)


def same_core_kernel(count, pos_ref, mine_ref, its_ref, near_mine_ref, near_its_ref, came_ref, *refs):
    w_refs, (keep_ref, send_ref, grad_s) = refs[:count], refs[-3:]
    rows = keep_ref.shape[0]
    fill_columns(pos_ref, 0, mine_ref, its_ref, near_mine_ref, near_its_ref, grad_s)
    for o, w_ref in enumerate(w_refs):
        depth = w_ref.shape[0]
        span = pl.ds(pl.multiple_of(pos_ref[3 + o] * depth, HD), depth)
        term = lax.dot_general(
            grad_s[...], w_ref[...], (((1,), (1,)), ((), ())), preferred_element_type=jnp.float32
        ) + came_ref[:, span].astype(jnp.float32)
        keep_ref[:, span] = term[:rows]
        send_ref[:, span] = term[rows:].astype(send_ref.dtype)


def input_terms(position, blocks, weights, earlier, came=None):
    rows = blocks[0].shape[2]
    width = sum(w.shape[0] for w in weights)
    bf16 = jnp.bfloat16
    count = len(weights)
    if came is None:
        kernel, extra = functools.partial(other_core_kernel, count), ()
        shapes = jax.ShapeDtypeStruct((rows, width), bf16)
        out_specs = vmem_specs(1)[0]
    else:
        kernel, extra = functools.partial(same_core_kernel, count), (came,)
        shapes = (
            jax.ShapeDtypeStruct((rows // 2, width), jnp.float32),
            jax.ShapeDtypeStruct((rows // 2, width), bf16),
        )
        out_specs = vmem_specs(2)
    return pl.pallas_call(
        kernel,
        out_shape=shapes,
        in_specs=smem_specs(1)
        + vmem_specs(4 + len(extra) + len(weights))
        + [pl.BlockSpec(memory_space=pl.ANY)] * len(earlier),
        out_specs=out_specs,
        scratch_shapes=[pltpu.VMEM((rows, PLANES * HD), bf16)],
        compiler_params=pltpu.CompilerParams(vmem_limit_bytes=16 * 2**20),
        cost_estimate=cost(2 * rows * width * PLANES * HD, *weights),
    )(position, *blocks, *extra, *weights, *earlier)


def after(values, *earlier):
    count = len(values)
    anywhere = pl.BlockSpec(memory_space=pl.ANY)
    return pl.pallas_call(
        lambda *refs: None,
        out_shape=tuple(jax.ShapeDtypeStruct(v.shape, v.dtype) for v in values),
        in_specs=[anywhere] * (count + len(earlier)),
        out_specs=(anywhere,) * count,
        input_output_aliases={i: i for i in range(count)},
    )(*values, *earlier)


def simple_kernel(kernel, shapes, scalars, arrays, earlier=()):
    anywhere = pl.BlockSpec(memory_space=pl.ANY)
    return pl.pallas_call(
        kernel,
        out_shape=shapes,
        in_specs=smem_specs(1) + vmem_specs(len(arrays)) + [anywhere] * len(earlier),
        out_specs=jax.tree.map(lambda _: vmem_specs(1)[0], shapes),
        compiler_params=pltpu.CompilerParams(vmem_limit_bytes=16 * 2**20),
        cost_estimate=cost(0, *arrays),
    )(scalars, *arrays, *earlier)


def head_of(device):
    plane, side, core = device // 4, (device // 2) % 2, device % 2
    return 8 * (plane // 2) + 4 * side + 2 * (plane % 2) + core


def join_heads_kernel(pos_ref, in_ref, out_ref):
    for device in range(SEQ):
        head = head_of(device)
        out_ref[:, head * HD : (head + 1) * HD] = in_ref[device]


def head_columns(at):
    return (at // 2) * 1024 + lax.rem(at, 2) * 256


def planes_kernel(pos_ref, q_ref, d_ref, _, *out_refs):
    for step, out_ref in enumerate(out_refs, 1):
        start = pl.multiple_of(head_columns(lax.rem(pos_ref[0] + step, PLANES)), 256)
        for i, ref in enumerate((q_ref, d_ref)):
            out_ref[i, :, :256] = ref[:, pl.ds(start, 256)]
            out_ref[i, :, 256:] = ref[:, pl.ds(start + 512, 256)]


def sides_kernel(pos_ref, q_ref, d_ref, one_ref, two_ref, three_ref, _, kept_ref, send_ref):
    plane, side = pos_ref[0], pos_ref[1]
    for out_ref, x in ((kept_ref, side), (send_ref, 1 - side)):
        start = pl.multiple_of(head_columns(plane) + 512 * x, 256)
        for i, ref in enumerate((q_ref, d_ref)):
            out_ref[0, i] = ref[:, pl.ds(start, 256)]
        for step, ref in enumerate((one_ref, two_ref, three_ref), 1):
            out_ref[step] = ref[:, :, pl.ds(pl.multiple_of(256 * x, 256), 256)]


def cores_kernel(pos_ref, same_ref, other_ref, tok_ref, _, kept_ref, send_ref, copy_ref):
    copy_ref[...] = tok_ref[...]
    core = pos_ref[2]
    for out_ref, c in ((kept_ref, core), (send_ref, 1 - core)):
        span = pl.ds(pl.multiple_of(HD * c, HD), HD)
        out_ref[0] = same_ref[:, :, :, span]
        out_ref[1] = other_ref[:, :, :, span]


def add_kernel(pos_ref, keep_ref, came_ref, mine_ref, theirs_ref, mine_next_ref, theirs_next_ref):
    outs = ((mine_ref, mine_next_ref), (theirs_ref, theirs_next_ref))
    for pair, (all_ref, next_ref) in enumerate(outs):
        for cr in range(2):
            for pr in range(2):
                total = keep_ref[pair, cr, pr] + came_ref[pair, cr, pr].astype(jnp.float32)
                total = total.astype(all_ref.dtype)
                all_ref[cr, pr] = total
                if pr:
                    next_ref[cr] = total


def weight_kernel(count, pos_ref, grad_ref, *refs):
    tok_refs, out_refs = refs[:8], refs[-count:]
    for o, out_ref in enumerate(out_refs):
        depth = out_ref.shape[1]
        at = lax.rem(pos_ref[3] + o, count)
        span = pl.ds(pl.multiple_of(at * depth, HD), depth)
        acc = jnp.zeros(out_ref.shape, jnp.float32)
        for cr in range(2):
            for pr in range(2):
                grad = grad_ref[cr, pr].astype(jnp.float32).T.astype(jnp.bfloat16)
                first = 4 * cr + 2 * pr
                part = jnp.concatenate([t[:, span] for t in tok_refs[first : first + 2]], axis=0)
                acc = acc + jnp.dot(grad, part, preferred_element_type=jnp.float32)
        out_ref[...] = acc.astype(out_ref.dtype)


def sum_kernel(count, pos_ref, *refs):
    total = sum(r[...].astype(jnp.float32) for r in refs[:count])
    refs[-1][...] = total.astype(refs[-1].dtype)


def finish_kernel(pos_ref, one_ref, two_ref, _, out_ref):
    total = one_ref[...].astype(jnp.float32) + two_ref[...].astype(jnp.float32)
    out_ref[...] = total.T


def exchange(value, groups=None):
    return lax.all_to_all(value, "seq", 0, 0, axis_index_groups=groups, tiled=True)


def on_device(inputs, queries, w_kv, doc_lengths, grad_out):
    bf16, f32 = jnp.bfloat16, jnp.float32
    tokens = inputs[0]
    query_rows = queries[0]
    cotangent = grad_out[0]
    lengths = doc_lengths[0]
    rows, width = tokens.shape
    total = SEQ * rows
    half_kv = KVH * HD
    seqs = lax.axis_size("fsdp")
    depth = w_kv.shape[0]
    here = lax.axis_index("seq")
    own_seq = lax.axis_index("fsdp")
    plane, side, core = here >> 2, (here >> 1) & 1, here & 1
    origins = [(own_seq - o) % seqs for o in range(seqs)]

    first = core * half_kv + side * 256
    w_own = jnp.concatenate(
        [columns(w_kv, first, 256), columns(w_kv, first + half_kv // 2, 256)], axis=1
    )
    w_parts = [w_own] + [shift_rows(w_own, o) for o in range(1, seqs)]
    if depth % HD:
        w_full = jnp.zeros((width, PLANES * HD), bf16)
        for o in range(seqs):
            w_full = lax.dynamic_update_slice_in_dim(w_full, w_parts[o], origins[o] * depth, 0)
        w_parts, places_of = [w_full], [jnp.int32(0)]
    else:
        places_of = origins
    position = jnp.stack([plane, side, core] + places_of).astype(jnp.int32)
    seq_first = jnp.stack([plane, side, core, own_seq]).astype(jnp.int32)

    crossed = swap(tokens, 2)
    pieces = [tokens, crossed, swap(tokens, 1), swap(crossed, 1)]

    places = jnp.arange(total, dtype=jnp.int32)
    doc_ends = jnp.cumsum(lengths)
    ended = doc_ends[None, :] <= places[:, None]
    within = places - jnp.sum(jnp.where(ended, lengths[None, :], 0), axis=1)
    exponent = jnp.arange(HD // 2, dtype=f32) * (2.0 / HD)
    rate = jnp.power(ROPE_BASE, -exponent)
    angles = within.astype(f32)[:, None] * jnp.concatenate([rate, rate])[None, :]
    quarter = jnp.where(jnp.arange(HD) < HD // 2, jnp.float32(jnp.pi / 2), jnp.float32(0.0))
    turns = jnp.sin(angles + quarter[None, :])

    def bf16s(*shape):
        return jax.ShapeDtypeStruct(shape, bf16)

    for_planes = simple_kernel(
        planes_kernel, (bf16s(2, rows, 512),) * 3, position, (query_rows, cotangent), (w_own,)
    )
    from_planes = [shift_planes(part, k) for k, part in enumerate(for_planes, 1)]
    same_side, for_side = simple_kernel(
        sides_kernel,
        (bf16s(4, 2, rows, 256),) * 2,
        position,
        (query_rows, cotangent, *from_planes),
        (crossed,),
    )
    from_side = swap_sides(for_side)

    kv_blocks = project(position, turns, pieces, w_parts)
    own = exchange(kv_blocks, [[r + 4 * p for p in range(PLANES)] for r in range(4)])
    other = swap_cores(own)
    kept, for_other, tokens_later = simple_kernel(
        cores_kernel,
        (bf16s(2, 4, 2, rows, HD),) * 2 + (bf16s(rows, width),),
        position,
        (same_side, from_side, tokens),
        (own,),
    )
    came = swap_cores(for_other)

    beside = swap(tokens_later, 4)

    out_parts, keep, send = attention(
        lengths, position, kept, came, turns, own, other
    )

    (beside,) = after((beside,), send)
    beside_crossed = swap(beside, 2)
    pieces_beside = [beside, beside_crossed, swap(beside, 1), swap(beside_crossed, 1)]

    mine, theirs, mine_next, theirs_next = simple_kernel(
        add_kernel,
        (bf16s(2, 2, 2 * rows, HD),) * 2 + (bf16s(2, 2 * rows, HD),) * 2,
        position,
        (keep, swap_cores(send)),
    )
    its = swap(theirs, 8)
    blocks = (mine, its, swap(mine_next, 4), swap(theirs_next, 12))
    pair_tokens = [*pieces[:2], *pieces_beside[:2], *pieces[2:], *pieces_beside[2:]]

    def weight_terms(grad, *earlier):
        cuts = 1 if depth % HD else seqs
        terms = simple_kernel(
            functools.partial(weight_kernel, cuts),
            (bf16s(HD, width // cuts),) * cuts,
            seq_first,
            (grad, *pair_tokens),
            earlier,
        )
        if cuts < seqs:
            terms = [columns(terms[0], ((own_seq + o) % seqs) * depth, depth) for o in range(seqs)]
        return terms

    def weight_sum(terms, *earlier):
        terms = [shift_rows(t, o) if o else t for o, t in enumerate(terms)]
        return simple_kernel(
            functools.partial(sum_kernel, seqs), bf16s(HD, depth), position, terms, earlier
        )

    mine_sum = weight_sum(weight_terms(mine, blocks[2]))
    its_terms = weight_terms(its)

    outs = exchange(after((out_parts,), its, blocks[3])[0])

    for_core = input_terms(position, blocks, w_parts, ())
    for_self, for_side = input_terms(
        position, blocks, w_parts, (mine_sum,), swap_cores(for_core)
    )
    from_side = swap_sides(for_side)

    terms = [mine_sum, weight_sum(its_terms, for_side)]

    sums = []
    for ar, term in enumerate(terms):
        pairs = []
        for s in range(SEQ):
            half = (s // 8 + ar) % 2
            pairs.append((s, (2 * (s % 2) + half) * 4 + (s & 2) + (s // 4) % 2))
        sums.append(lax.ppermute(term, "seq", pairs))

    out_rows = simple_kernel(
        join_heads_kernel, bf16s(rows, QH * HD), position, (outs,)
    )
    grad_rows = (for_self + from_side.astype(f32)).astype(bf16)
    finished = simple_kernel(
        finish_kernel, jax.ShapeDtypeStruct((depth, HD), f32), position, sums, (outs,)
    )
    return (out_rows[None], grad_rows[None], finished)


def solution(mesh):
    in_specs = (
        P("fsdp", "seq", None),
        P("fsdp", "seq", None),
        P("fsdp", None),
        P("fsdp", None),
        P("fsdp", "seq", None),
    )
    out_specs = (P("fsdp", "seq", None), P("fsdp", "seq", None), P("fsdp", "seq"))
    return jax.shard_map(
        on_device, mesh=mesh, in_specs=in_specs, out_specs=out_specs, check_vma=False
    )
```

```python
import functools

import jax
import jax.numpy as jnp
from jax import lax
from jax.experimental import pallas as pl
from jax.experimental.pallas import tpu as pltpu
from jax.sharding import PartitionSpec as P

QH = 16
KVH = 8
HD = 128
WIN = 1024
G = 2

SOFT_CAP = 50.0
QUERY_SCALE = 1.0 / 12.0
ROPE_BASE = 10000.0

SEQ = 16
PLANES = 4
BLK = 256
REACH = WIN // BLK + 1


def cost(flops, *arrays):
    moved = sum(a.size * a.dtype.itemsize for a in arrays)
    return pl.CostEstimate(flops=flops, bytes_accessed=2 * moved, transcendentals=0)


def shift_planes(value, steps):
    pairs = [(s, (s + 4 * steps) % SEQ) for s in range(SEQ)]
    return lax.ppermute(value, "seq", pairs)


def swap(value, mask):
    return lax.ppermute(value, "seq", [(s, s ^ mask) for s in range(SEQ)])


def swap_sides(value):
    return swap(value, 2)


def swap_cores(value):
    return swap(value, 1)


def shift_rows(value, steps):
    count = lax.axis_size("fsdp")
    return lax.ppermute(value, "fsdp", [(i, (i + steps) % count) for i in range(count)])


def columns(value, start, size):
    return lax.dynamic_slice_in_dim(value, start, size, value.ndim - 1)


def rotation(table):
    swapped = pltpu.roll(table, HD // 2, 1)
    first = lax.broadcasted_iota(jnp.int32, table.shape, 1) < HD // 2
    return jnp.where(first, table, swapped), jnp.where(first, -swapped, table)


def attention_kernel(
    len_ref, pos_ref, kept_ref, came_ref, turn_ref, own_ref, oth_ref, *refs
):
    out_ref, keep_ref, send_ref, q_s, d_s, kv_s, vt_s, e_s, t_s, dk_s, dv_s = refs[-11:]
    plane, side, core = pos_ref[0], pos_ref[1], pos_ref[2]
    rows = out_ref.shape[1]
    total = dk_s.shape[0]
    f32 = jnp.float32
    nt = (((1,), (1,)), ((), ()))

    def flipped(bit, flip):
        return 1 - bit if flip else bit

    for step in range(PLANES):
        home = lax.rem(plane + (PLANES - step), PLANES)
        for xr in range(2):
            for cr in range(2):
                base = home * (4 * rows) + flipped(side, xr) * (2 * rows)
                base = pl.multiple_of(base + flipped(core, cr) * rows, rows)
                source = came_ref if cr else kept_ref
                q_s[pl.ds(base, rows), :] = source[xr, step, 0]
                d_s[pl.ds(base, rows), :] = source[xr, step, 1]

    for at in range(PLANES):
        for xr in range(2):
            for cr in range(2):
                base = at * (4 * rows) + flipped(side, xr) * (2 * rows)
                mine = pl.multiple_of(base + flipped(core, cr) * rows, rows)
                theirs = pl.multiple_of(base + flipped(core, 1 - cr) * rows, rows)
                piece = pl.ds((2 * cr + xr) * rows, rows)
                kv_s[core, pl.ds(mine, rows), :] = own_ref[at, piece, :]
                kv_s[1 - core, pl.ds(theirs, rows), :] = oth_ref[at, piece, :]

    for block in range(total // BLK):
        span = pl.ds(block * BLK, BLK)
        vt_s[:, span] = kv_s[1, span, :].astype(f32).T.astype(jnp.bfloat16)
    dk_s[...] = jnp.zeros_like(dk_s)
    dv_s[...] = jnp.zeros_like(dv_s)

    ends = []
    run = 0
    for j in range(len_ref.shape[0]):
        run = run + len_ref[j]
        ends.append(run)

    def query_block(i, carry):
        base = pl.multiple_of(i * BLK, BLK)
        first_part = i * (BLK // rows)
        qb, db = q_s[pl.ds(base, BLK), :], d_s[pl.ds(base, BLK), :]
        p_row = base + lax.broadcasted_iota(jnp.int32, (1, BLK), 1)
        start_row = jnp.zeros((1, BLK), jnp.int32)
        first = jnp.int32(0)
        for end in ends:
            start_row = jnp.where(end <= p_row, end, start_row)
            first = jnp.where(end <= base, end, first)
        low_row = jnp.maximum(start_row, p_row - (WIN - 1))
        low_block = jnp.maximum(first, jnp.maximum(base - (WIN - 1), 0)) // BLK
        count = i - low_block + 1

        def body(n):
            def key_span(j):
                return pl.ds(pl.multiple_of((low_block + j) * BLK, BLK), BLK)

            norm = jnp.zeros((1, BLK), f32)
            out_t = jnp.zeros((HD, BLK), f32)
            for j in range(n):
                keys = key_span(j)
                scores = lax.dot_general(kv_s[0, keys, :], qb, nt, preferred_element_type=f32)
                squashed = jnp.tanh(scores * (QUERY_SCALE / SOFT_CAP))
                weights = jnp.exp(squashed * SOFT_CAP)
                n_col = (low_block + j) * BLK + lax.broadcasted_iota(jnp.int32, (BLK, 1), 0)
                allowed = n_col >= low_row
                if j == n - 1:
                    allowed = allowed & (n_col <= p_row)
                weights = jnp.where(allowed, weights, 0.0)
                t_s[j] = squashed
                e_s[j] = weights
                norm = norm + jnp.sum(weights, axis=0, keepdims=True)
                out_t = out_t + jnp.dot(
                    vt_s[:, keys], weights.astype(jnp.bfloat16), preferred_element_type=f32
                )
            inverse = 1.0 / norm
            out_f = (out_t * inverse).astype(jnp.bfloat16).astype(f32)
            delta = jnp.sum(db.astype(f32).T * out_f, axis=0, keepdims=True)
            out_b = out_f.T.astype(jnp.bfloat16)
            for j in range(BLK // rows):
                out_ref[first_part + j] = out_b[j * rows : (j + 1) * rows]
            for j in range(n):
                keys = key_span(j)
                probs = e_s[j] * inverse
                squashed = t_s[j]
                dv_s[keys, :] += jnp.dot(
                    probs.astype(jnp.bfloat16), db, preferred_element_type=f32
                )
                dprob = lax.dot_general(kv_s[1, keys, :], db, nt, preferred_element_type=f32)
                dscore = probs * (dprob - delta) * (1.0 - squashed * squashed)
                dk_s[keys, :] += jnp.dot(
                    dscore.astype(jnp.bfloat16), qb, preferred_element_type=f32
                )

        for n in range(1, REACH + 1):
            pl.when(count == n)(lambda n=n: body(n))
        return carry

    lax.fori_loop(0, total // BLK, query_block, 0)

    def finish(block, carry):
        span = pl.ds(pl.multiple_of(block * rows, rows), rows)
        key_part = dk_s[span, :] * QUERY_SCALE
        cosine, sine = rotation(turn_ref[span, :])
        key_part = key_part * cosine - pltpu.roll(key_part, HD // 2, 1) * sine
        value_part = dv_s[span, :]
        to_pair = lax.rem(block // 8 + plane // 2, 2)
        to_plane = lax.rem(block // 4 + plane, 2)
        to_side = lax.rem(block // 2 + side, 2)
        to_core = lax.rem(block + core, 2)
        is_key = core == 0
        at = pl.ds(pl.multiple_of(to_side * rows, rows), rows)
        keep_ref[to_pair, to_core, to_plane, at, :] = jnp.where(is_key, key_part, value_part)
        send_ref[to_pair, 1 - to_core, to_plane, at, :] = jnp.where(
            is_key, value_part, key_part
        ).astype(jnp.bfloat16)
        return carry

    lax.fori_loop(0, total // rows, finish, 0)


def vmem_specs(count):
    return [pl.BlockSpec(memory_space=pltpu.VMEM)] * count


def smem_specs(count):
    return [pl.BlockSpec(memory_space=pltpu.SMEM)] * count


def attention(lengths, position, kept, came, turns, own, other, *earlier):
    rows = kept.shape[3]
    total = SEQ * rows
    bf16, f32 = jnp.bfloat16, jnp.float32
    return pl.pallas_call(
        attention_kernel,
        out_shape=(
            jax.ShapeDtypeStruct((SEQ, rows, HD), bf16),
            jax.ShapeDtypeStruct((2, 2, 2, 2 * rows, HD), f32),
            jax.ShapeDtypeStruct((2, 2, 2, 2 * rows, HD), bf16),
        ),
        in_specs=smem_specs(2)
        + vmem_specs(5)
        + [pl.BlockSpec(memory_space=pl.ANY)] * len(earlier),
        out_specs=vmem_specs(3),
        scratch_shapes=[
            pltpu.VMEM((total, HD), bf16),
            pltpu.VMEM((total, HD), bf16),
            pltpu.VMEM((2, total, HD), bf16),
            pltpu.VMEM((HD, total), bf16),
            pltpu.VMEM((REACH, BLK, BLK), f32),
            pltpu.VMEM((REACH, BLK, BLK), f32),
            pltpu.VMEM((total, HD), f32),
            pltpu.VMEM((total, HD), f32),
        ],
        compiler_params=pltpu.CompilerParams(vmem_limit_bytes=22 * 2**20),
        cost_estimate=cost(300 * BLK * BLK * HD, kept, came, own, other, turns),
    )(lengths, position, kept, came, turns, own, other, *earlier)


def project_kernel(count, pos_ref, turn_ref, *refs):
    tok_refs, w_refs, out_ref = refs[:4], refs[4 : 4 + count], refs[-1]
    plane, side, core = pos_ref[0], pos_ref[1], pos_ref[2]
    rows = tok_refs[0].shape[0]
    is_key = core == 0
    for half in range(PLANES // 2):
        acc = jnp.zeros((4 * rows, 2 * HD), jnp.float32)
        for o, w_ref in enumerate(w_refs):
            depth = w_ref.shape[0]
            span = pl.ds(pl.multiple_of(pos_ref[3 + o] * depth, HD), depth)
            part = jnp.concatenate([t[:, span] for t in tok_refs], axis=0)
            acc = acc + jnp.dot(
                part,
                w_ref[:, half * 2 * HD : (half + 1) * 2 * HD],
                preferred_element_type=jnp.float32,
            )
        for b in range(2):
            at = 2 * half + b
            for piece in range(4):
                x = 1 - side if piece % 2 else side
                c = 1 - core if piece // 2 else core
                start = pl.multiple_of((plane * 4 + 2 * x + c) * rows, rows)
                head = acc[piece * rows : (piece + 1) * rows, b * HD : (b + 1) * HD]
                cosine, sine = rotation(turn_ref[pl.ds(start, rows), :])
                cosine, sine = jnp.where(is_key, cosine, 1.0), jnp.where(is_key, sine, 0.0)
                turned = head * cosine + pltpu.roll(head, HD // 2, 1) * sine
                out_ref[at, piece * rows : (piece + 1) * rows] = turned.astype(jnp.bfloat16)


def project(position, turns, pieces, weights, *earlier):
    rows, width = pieces[0].shape
    return pl.pallas_call(
        functools.partial(project_kernel, len(weights)),
        out_shape=jax.ShapeDtypeStruct((PLANES, 4 * rows, HD), jnp.bfloat16),
        in_specs=smem_specs(1)
        + vmem_specs(5 + len(weights))
        + [pl.BlockSpec(memory_space=pl.ANY)] * len(earlier),
        out_specs=vmem_specs(1)[0],
        compiler_params=pltpu.CompilerParams(vmem_limit_bytes=40 * 2**20),
        cost_estimate=cost(8 * rows * width * PLANES * HD, *pieces, *weights),
    )(position, turns, *pieces, *weights, *earlier)


def fill_columns(pos_ref, cr, mine_ref, its_ref, near_mine_ref, near_its_ref, grad_s):
    for ar in range(2):
        for br in range(2):
            block = pos_ref[0] ^ (2 * ar + br)
            if br:
                value = (near_its_ref if ar else near_mine_ref)[cr]
            else:
                value = (its_ref if ar else mine_ref)[cr, 0]
            grad_s[:, pl.ds(pl.multiple_of(block * HD, HD), HD)] = value


def other_core_kernel(count, pos_ref, mine_ref, its_ref, near_mine_ref, near_its_ref, *refs):
    w_refs, out_ref, grad_s = refs[:count], refs[-2], refs[-1]
    fill_columns(pos_ref, 1, mine_ref, its_ref, near_mine_ref, near_its_ref, grad_s)
    for o, w_ref in enumerate(w_refs):
        depth = w_ref.shape[0]
        span = pl.ds(pl.multiple_of(pos_ref[3 + o] * depth, HD), depth)
        out_ref[:, span] = lax.dot_general(
            grad_s[...], w_ref[...], (((1,), (1,)), ((), ())), preferred_element_type=jnp.float32
        ).astype(out_ref.dtype)


def same_core_kernel(count, pos_ref, mine_ref, its_ref, near_mine_ref, near_its_ref, came_ref, *refs):
    w_refs, (keep_ref, send_ref, grad_s) = refs[:count], refs[-3:]
    rows = keep_ref.shape[0]
    fill_columns(pos_ref, 0, mine_ref, its_ref, near_mine_ref, near_its_ref, grad_s)
    for o, w_ref in enumerate(w_refs):
        depth = w_ref.shape[0]
        span = pl.ds(pl.multiple_of(pos_ref[3 + o] * depth, HD), depth)
        term = lax.dot_general(
            grad_s[...], w_ref[...], (((1,), (1,)), ((), ())), preferred_element_type=jnp.float32
        ) + came_ref[:, span].astype(jnp.float32)
        keep_ref[:, span] = term[:rows]
        send_ref[:, span] = term[rows:].astype(send_ref.dtype)


def input_terms(position, blocks, weights, earlier, came=None):
    rows = blocks[0].shape[2]
    width = sum(w.shape[0] for w in weights)
    bf16 = jnp.bfloat16
    count = len(weights)
    if came is None:
        kernel, extra = functools.partial(other_core_kernel, count), ()
        shapes = jax.ShapeDtypeStruct((rows, width), bf16)
        out_specs = vmem_specs(1)[0]
    else:
        kernel, extra = functools.partial(same_core_kernel, count), (came,)
        shapes = (
            jax.ShapeDtypeStruct((rows // 2, width), jnp.float32),
            jax.ShapeDtypeStruct((rows // 2, width), bf16),
        )
        out_specs = vmem_specs(2)
    return pl.pallas_call(
        kernel,
        out_shape=shapes,
        in_specs=smem_specs(1)
        + vmem_specs(4 + len(extra) + len(weights))
        + [pl.BlockSpec(memory_space=pl.ANY)] * len(earlier),
        out_specs=out_specs,
        scratch_shapes=[pltpu.VMEM((rows, PLANES * HD), bf16)],
        compiler_params=pltpu.CompilerParams(vmem_limit_bytes=16 * 2**20),
        cost_estimate=cost(2 * rows * width * PLANES * HD, *weights),
    )(position, *blocks, *extra, *weights, *earlier)


def after(values, *earlier):
    count = len(values)
    anywhere = pl.BlockSpec(memory_space=pl.ANY)
    return pl.pallas_call(
        lambda *refs: None,
        out_shape=tuple(jax.ShapeDtypeStruct(v.shape, v.dtype) for v in values),
        in_specs=[anywhere] * (count + len(earlier)),
        out_specs=(anywhere,) * count,
        input_output_aliases={i: i for i in range(count)},
    )(*values, *earlier)


def simple_kernel(kernel, shapes, scalars, arrays, earlier=()):
    anywhere = pl.BlockSpec(memory_space=pl.ANY)
    return pl.pallas_call(
        kernel,
        out_shape=shapes,
        in_specs=smem_specs(1) + vmem_specs(len(arrays)) + [anywhere] * len(earlier),
        out_specs=jax.tree.map(lambda _: vmem_specs(1)[0], shapes),
        compiler_params=pltpu.CompilerParams(vmem_limit_bytes=16 * 2**20),
        cost_estimate=cost(0, *arrays),
    )(scalars, *arrays, *earlier)


def head_of(device):
    plane, side, core = device // 4, (device // 2) % 2, device % 2
    return 8 * (plane // 2) + 4 * side + 2 * (plane % 2) + core


def join_heads_kernel(pos_ref, in_ref, out_ref):
    for device in range(SEQ):
        head = head_of(device)
        out_ref[:, head * HD : (head + 1) * HD] = in_ref[device]


def head_columns(at):
    return (at // 2) * 1024 + lax.rem(at, 2) * 256


def planes_kernel(pos_ref, q_ref, d_ref, _, *out_refs):
    for step, out_ref in enumerate(out_refs, 1):
        start = pl.multiple_of(head_columns(lax.rem(pos_ref[0] + step, PLANES)), 256)
        for i, ref in enumerate((q_ref, d_ref)):
            out_ref[i, :, :256] = ref[:, pl.ds(start, 256)]
            out_ref[i, :, 256:] = ref[:, pl.ds(start + 512, 256)]


def sides_kernel(pos_ref, q_ref, d_ref, one_ref, two_ref, three_ref, _, kept_ref, send_ref):
    plane, side = pos_ref[0], pos_ref[1]
    for out_ref, x in ((kept_ref, side), (send_ref, 1 - side)):
        start = pl.multiple_of(head_columns(plane) + 512 * x, 256)
        for i, ref in enumerate((q_ref, d_ref)):
            out_ref[0, i] = ref[:, pl.ds(start, 256)]
        for step, ref in enumerate((one_ref, two_ref, three_ref), 1):
            out_ref[step] = ref[:, :, pl.ds(pl.multiple_of(256 * x, 256), 256)]


def cores_kernel(pos_ref, same_ref, other_ref, tok_ref, _, kept_ref, send_ref, copy_ref):
    copy_ref[...] = tok_ref[...]
    core = pos_ref[2]
    for out_ref, c in ((kept_ref, core), (send_ref, 1 - core)):
        span = pl.ds(pl.multiple_of(HD * c, HD), HD)
        out_ref[0] = same_ref[:, :, :, span]
        out_ref[1] = other_ref[:, :, :, span]


def add_kernel(pos_ref, keep_ref, came_ref, mine_ref, theirs_ref, next_ref):
    for pair, out_ref in enumerate((mine_ref, theirs_ref)):
        for cr in range(2):
            for pr in range(2):
                total = keep_ref[pair, cr, pr] + came_ref[pair, cr, pr].astype(jnp.float32)
                total = total.astype(out_ref.dtype)
                out_ref[cr, pr] = total
                if pr and not pair:
                    next_ref[cr] = total


def weight_kernel(count, pos_ref, grad_ref, *refs):
    tok_refs, out_refs = refs[:8], refs[-count:]
    for o, out_ref in enumerate(out_refs):
        depth = out_ref.shape[1]
        at = lax.rem(pos_ref[3] + o, count)
        span = pl.ds(pl.multiple_of(at * depth, HD), depth)
        acc = jnp.zeros(out_ref.shape, jnp.float32)
        for cr in range(2):
            for pr in range(2):
                grad = grad_ref[cr, pr].astype(jnp.float32).T.astype(jnp.bfloat16)
                first = 4 * cr + 2 * pr
                part = jnp.concatenate([t[:, span] for t in tok_refs[first : first + 2]], axis=0)
                acc = acc + jnp.dot(grad, part, preferred_element_type=jnp.float32)
        out_ref[...] = acc.astype(out_ref.dtype)


def sum_kernel(count, pos_ref, *refs):
    total = sum(r[...].astype(jnp.float32) for r in refs[:count])
    refs[-1][...] = total.astype(refs[-1].dtype)


def finish_kernel(pos_ref, one_ref, two_ref, _, out_ref):
    total = one_ref[...].astype(jnp.float32) + two_ref[...].astype(jnp.float32)
    out_ref[...] = total.T


def exchange(value, groups=None):
    return lax.all_to_all(value, "seq", 0, 0, axis_index_groups=groups, tiled=True)


def on_device(inputs, queries, w_kv, doc_lengths, grad_out):
    bf16, f32 = jnp.bfloat16, jnp.float32
    tokens = inputs[0]
    query_rows = queries[0]
    cotangent = grad_out[0]
    lengths = doc_lengths[0]
    rows, width = tokens.shape
    total = SEQ * rows
    half_kv = KVH * HD
    seqs = lax.axis_size("fsdp")
    depth = w_kv.shape[0]
    here = lax.axis_index("seq")
    own_seq = lax.axis_index("fsdp")
    plane, side, core = here >> 2, (here >> 1) & 1, here & 1
    origins = [(own_seq - o) % seqs for o in range(seqs)]

    first = core * half_kv + side * 256
    w_own = jnp.concatenate(
        [columns(w_kv, first, 256), columns(w_kv, first + half_kv // 2, 256)], axis=1
    )
    w_parts = [w_own] + [shift_rows(w_own, o) for o in range(1, seqs)]
    if depth % HD:
        w_full = jnp.zeros((width, PLANES * HD), bf16)
        for o in range(seqs):
            w_full = lax.dynamic_update_slice_in_dim(w_full, w_parts[o], origins[o] * depth, 0)
        w_parts, places_of = [w_full], [jnp.int32(0)]
    else:
        places_of = origins
    position = jnp.stack([plane, side, core] + places_of).astype(jnp.int32)
    seq_first = jnp.stack([plane, side, core, own_seq]).astype(jnp.int32)

    crossed = swap(tokens, 2)
    (tokens_next,) = after((tokens,), crossed)
    pieces = [tokens, crossed, swap(tokens_next, 1), swap(crossed, 1)]

    places = jnp.arange(total, dtype=jnp.int32)
    doc_ends = jnp.cumsum(lengths)
    ended = doc_ends[None, :] <= places[:, None]
    within = places - jnp.sum(jnp.where(ended, lengths[None, :], 0), axis=1)
    exponent = jnp.arange(HD // 2, dtype=f32) * (2.0 / HD)
    rate = jnp.power(ROPE_BASE, -exponent)
    angles = within.astype(f32)[:, None] * jnp.concatenate([rate, rate])[None, :]
    quarter = jnp.where(jnp.arange(HD) < HD // 2, jnp.float32(jnp.pi / 2), jnp.float32(0.0))
    turns = jnp.sin(angles + quarter[None, :])

    def bf16s(*shape):
        return jax.ShapeDtypeStruct(shape, bf16)

    for_planes = simple_kernel(
        planes_kernel, (bf16s(2, rows, 512),) * 3, position, (query_rows, cotangent), (w_own,)
    )
    from_planes = [shift_planes(part, k) for k, part in enumerate(for_planes, 1)]
    same_side, for_side = simple_kernel(
        sides_kernel,
        (bf16s(4, 2, rows, 256),) * 2,
        position,
        (query_rows, cotangent, *from_planes),
        (crossed,),
    )
    from_side = swap_sides(for_side)

    kv_blocks = project(position, turns, pieces, w_parts, for_side)
    own = exchange(kv_blocks, [[r + 4 * p for p in range(PLANES)] for r in range(4)])
    other = swap_cores(own)
    kept, for_other, tokens_later = simple_kernel(
        cores_kernel,
        (bf16s(2, 4, 2, rows, HD),) * 2 + (bf16s(rows, width),),
        position,
        (same_side, from_side, tokens),
        (own,),
    )
    came = swap_cores(for_other)

    beside = swap(tokens_later, 4)

    out_parts, keep, send = attention(
        lengths, position, kept, came, turns, own, other
    )

    (beside,) = after((beside,), send)
    beside_crossed = swap(beside, 2)
    pieces_beside = [beside, beside_crossed, swap(beside, 1), swap(beside_crossed, 1)]

    mine, theirs, mine_next = simple_kernel(
        add_kernel,
        (bf16s(2, 2, 2 * rows, HD),) * 2 + (bf16s(2, 2 * rows, HD),),
        position,
        (keep, swap_cores(send)),
    )
    its = swap(theirs, 8)
    blocks = (mine, its, swap(mine_next, 4), swap(its[:, 1], 4))
    pair_tokens = [*pieces[:2], *pieces_beside[:2], *pieces[2:], *pieces_beside[2:]]

    def weight_terms(grad, *earlier):
        cuts = 1 if depth % HD else seqs
        terms = simple_kernel(
            functools.partial(weight_kernel, cuts),
            (bf16s(HD, width // cuts),) * cuts,
            seq_first,
            (grad, *pair_tokens),
            earlier,
        )
        if cuts < seqs:
            terms = [columns(terms[0], ((own_seq + o) % seqs) * depth, depth) for o in range(seqs)]
        return terms

    def weight_sum(terms, *earlier):
        terms = [shift_rows(t, o) if o else t for o, t in enumerate(terms)]
        return simple_kernel(
            functools.partial(sum_kernel, seqs), bf16s(HD, depth), position, terms, earlier
        )

    mine_terms = weight_terms(mine, blocks[2])
    mine_sum = weight_sum(mine_terms)
    its_terms = weight_terms(its)

    for_core = input_terms(position, blocks, w_parts, mine_terms[:1])
    outs = exchange(after((out_parts,), its_terms[0], for_core)[0])

    for_self, for_side = input_terms(
        position, blocks, w_parts, (mine_sum,), swap_cores(for_core)
    )
    from_side = swap_sides(for_side)

    terms = [mine_sum, weight_sum(its_terms, for_side)]

    sums = []
    for ar, term in enumerate(terms):
        pairs = []
        for s in range(SEQ):
            half = (s // 8 + ar) % 2
            pairs.append((s, (2 * (s % 2) + half) * 4 + (s & 2) + (s // 4) % 2))
        sums.append(lax.ppermute(term, "seq", pairs))

    out_rows = simple_kernel(
        join_heads_kernel, bf16s(rows, QH * HD), position, (outs,)
    )
    grad_rows = (for_self + from_side.astype(f32)).astype(bf16)
    finished = simple_kernel(
        finish_kernel, jax.ShapeDtypeStruct((depth, HD), f32), position, sums, (outs,)
    )
    return (out_rows[None], grad_rows[None], finished)


def solution(mesh):
    in_specs = (
        P("fsdp", "seq", None),
        P("fsdp", "seq", None),
        P("fsdp", None),
        P("fsdp", None),
        P("fsdp", "seq", None),
    )
    out_specs = (P("fsdp", "seq", None), P("fsdp", "seq", None), P("fsdp", "seq"))
    return jax.shard_map(
        on_device, mesh=mesh, in_specs=in_specs, out_specs=out_specs, check_vma=False
    )
```

```python
import functools

import jax
import jax.numpy as jnp
from jax import lax
from jax.experimental import pallas as pl
from jax.experimental.pallas import tpu as pltpu
from jax.sharding import PartitionSpec as P

QH = 16
KVH = 8
HD = 128
WIN = 1024
G = 2

SOFT_CAP = 50.0
QUERY_SCALE = 1.0 / 12.0
ROPE_BASE = 10000.0

SEQ = 16
PLANES = 4
BLK = 256
REACH = WIN // BLK + 1


def cost(flops, *arrays):
    moved = sum(a.size * a.dtype.itemsize for a in arrays)
    return pl.CostEstimate(flops=flops, bytes_accessed=2 * moved, transcendentals=0)


def shift_planes(value, steps):
    pairs = [(s, (s + 4 * steps) % SEQ) for s in range(SEQ)]
    return lax.ppermute(value, "seq", pairs)


def swap(value, mask):
    return lax.ppermute(value, "seq", [(s, s ^ mask) for s in range(SEQ)])


def swap_sides(value):
    return swap(value, 2)


def swap_cores(value):
    return swap(value, 1)


def shift_rows(value, steps):
    count = lax.axis_size("fsdp")
    return lax.ppermute(value, "fsdp", [(i, (i + steps) % count) for i in range(count)])


def columns(value, start, size):
    return lax.dynamic_slice_in_dim(value, start, size, value.ndim - 1)


def rotation(table):
    swapped = pltpu.roll(table, HD // 2, 1)
    first = lax.broadcasted_iota(jnp.int32, table.shape, 1) < HD // 2
    return jnp.where(first, table, swapped), jnp.where(first, -swapped, table)


def attention_kernel(
    len_ref, pos_ref, kept_ref, came_ref, turn_ref, own_ref, oth_ref, *refs
):
    out_ref, keep_ref, send_ref, q_s, d_s, kv_s, vt_s, e_s, t_s, dk_s, dv_s = refs[-11:]
    plane, side, core = pos_ref[0], pos_ref[1], pos_ref[2]
    rows = out_ref.shape[1]
    total = dk_s.shape[0]
    f32 = jnp.float32
    nt = (((1,), (1,)), ((), ()))

    def flipped(bit, flip):
        return 1 - bit if flip else bit

    for step in range(PLANES):
        home = lax.rem(plane + (PLANES - step), PLANES)
        for xr in range(2):
            for cr in range(2):
                base = home * (4 * rows) + flipped(side, xr) * (2 * rows)
                base = pl.multiple_of(base + flipped(core, cr) * rows, rows)
                source = came_ref if cr else kept_ref
                q_s[pl.ds(base, rows), :] = source[xr, step, 0]
                d_s[pl.ds(base, rows), :] = source[xr, step, 1]

    for at in range(PLANES):
        for xr in range(2):
            for cr in range(2):
                base = at * (4 * rows) + flipped(side, xr) * (2 * rows)
                mine = pl.multiple_of(base + flipped(core, cr) * rows, rows)
                theirs = pl.multiple_of(base + flipped(core, 1 - cr) * rows, rows)
                piece = pl.ds((2 * cr + xr) * rows, rows)
                kv_s[core, pl.ds(mine, rows), :] = own_ref[at, piece, :]
                kv_s[1 - core, pl.ds(theirs, rows), :] = oth_ref[at, piece, :]

    for block in range(total // BLK):
        span = pl.ds(block * BLK, BLK)
        vt_s[:, span] = kv_s[1, span, :].astype(f32).T.astype(jnp.bfloat16)
    dk_s[...] = jnp.zeros_like(dk_s)
    dv_s[...] = jnp.zeros_like(dv_s)

    ends = []
    run = 0
    for j in range(len_ref.shape[0]):
        run = run + len_ref[j]
        ends.append(run)

    def query_block(i, carry):
        base = pl.multiple_of(i * BLK, BLK)
        first_part = i * (BLK // rows)
        qb, db = q_s[pl.ds(base, BLK), :], d_s[pl.ds(base, BLK), :]
        p_row = base + lax.broadcasted_iota(jnp.int32, (1, BLK), 1)
        start_row = jnp.zeros((1, BLK), jnp.int32)
        first = jnp.int32(0)
        for end in ends:
            start_row = jnp.where(end <= p_row, end, start_row)
            first = jnp.where(end <= base, end, first)
        low_row = jnp.maximum(start_row, p_row - (WIN - 1))
        low_block = jnp.maximum(first, jnp.maximum(base - (WIN - 1), 0)) // BLK
        count = i - low_block + 1

        def body(n):
            def key_span(j):
                return pl.ds(pl.multiple_of((low_block + j) * BLK, BLK), BLK)

            norm = jnp.zeros((1, BLK), f32)
            out_t = jnp.zeros((HD, BLK), f32)
            for j in range(n):
                keys = key_span(j)
                scores = lax.dot_general(kv_s[0, keys, :], qb, nt, preferred_element_type=f32)
                squashed = jnp.tanh(scores * (QUERY_SCALE / SOFT_CAP))
                weights = jnp.exp(squashed * SOFT_CAP)
                n_col = (low_block + j) * BLK + lax.broadcasted_iota(jnp.int32, (BLK, 1), 0)
                allowed = n_col >= low_row
                if j == n - 1:
                    allowed = allowed & (n_col <= p_row)
                weights = jnp.where(allowed, weights, 0.0)
                t_s[j] = squashed
                e_s[j] = weights
                norm = norm + jnp.sum(weights, axis=0, keepdims=True)
                out_t = out_t + jnp.dot(
                    vt_s[:, keys], weights.astype(jnp.bfloat16), preferred_element_type=f32
                )
            inverse = 1.0 / norm
            out_f = (out_t * inverse).astype(jnp.bfloat16).astype(f32)
            delta = jnp.sum(db.astype(f32).T * out_f, axis=0, keepdims=True)
            out_b = out_f.T.astype(jnp.bfloat16)
            for j in range(BLK // rows):
                out_ref[first_part + j] = out_b[j * rows : (j + 1) * rows]
            for j in range(n):
                keys = key_span(j)
                probs = e_s[j] * inverse
                squashed = t_s[j]
                dv_s[keys, :] += jnp.dot(
                    probs.astype(jnp.bfloat16), db, preferred_element_type=f32
                )
                dprob = lax.dot_general(kv_s[1, keys, :], db, nt, preferred_element_type=f32)
                dscore = probs * (dprob - delta) * (1.0 - squashed * squashed)
                dk_s[keys, :] += jnp.dot(
                    dscore.astype(jnp.bfloat16), qb, preferred_element_type=f32
                )

        for n in range(1, REACH + 1):
            pl.when(count == n)(lambda n=n: body(n))
        return carry

    lax.fori_loop(0, total // BLK, query_block, 0)

    def finish(block, carry):
        span = pl.ds(pl.multiple_of(block * rows, rows), rows)
        key_part = dk_s[span, :] * QUERY_SCALE
        cosine, sine = rotation(turn_ref[span, :])
        key_part = key_part * cosine - pltpu.roll(key_part, HD // 2, 1) * sine
        value_part = dv_s[span, :]
        to_pair = lax.rem(block // 8 + plane // 2, 2)
        to_plane = lax.rem(block // 4 + plane, 2)
        to_side = lax.rem(block // 2 + side, 2)
        to_core = lax.rem(block + core, 2)
        is_key = core == 0
        at = pl.ds(pl.multiple_of(to_side * rows, rows), rows)
        keep_ref[to_pair, to_core, to_plane, at, :] = jnp.where(is_key, key_part, value_part)
        send_ref[to_pair, 1 - to_core, to_plane, at, :] = jnp.where(
            is_key, value_part, key_part
        ).astype(jnp.bfloat16)
        return carry

    lax.fori_loop(0, total // rows, finish, 0)


def vmem_specs(count):
    return [pl.BlockSpec(memory_space=pltpu.VMEM)] * count


def smem_specs(count):
    return [pl.BlockSpec(memory_space=pltpu.SMEM)] * count


def attention(lengths, position, kept, came, turns, own, other, *earlier):
    rows = kept.shape[3]
    total = SEQ * rows
    bf16, f32 = jnp.bfloat16, jnp.float32
    return pl.pallas_call(
        attention_kernel,
        out_shape=(
            jax.ShapeDtypeStruct((SEQ, rows, HD), bf16),
            jax.ShapeDtypeStruct((2, 2, 2, 2 * rows, HD), f32),
            jax.ShapeDtypeStruct((2, 2, 2, 2 * rows, HD), bf16),
        ),
        in_specs=smem_specs(2)
        + vmem_specs(5)
        + [pl.BlockSpec(memory_space=pl.ANY)] * len(earlier),
        out_specs=vmem_specs(3),
        scratch_shapes=[
            pltpu.VMEM((total, HD), bf16),
            pltpu.VMEM((total, HD), bf16),
            pltpu.VMEM((2, total, HD), bf16),
            pltpu.VMEM((HD, total), bf16),
            pltpu.VMEM((REACH, BLK, BLK), f32),
            pltpu.VMEM((REACH, BLK, BLK), f32),
            pltpu.VMEM((total, HD), f32),
            pltpu.VMEM((total, HD), f32),
        ],
        compiler_params=pltpu.CompilerParams(vmem_limit_bytes=22 * 2**20),
        cost_estimate=cost(300 * BLK * BLK * HD, kept, came, own, other, turns),
    )(lengths, position, kept, came, turns, own, other, *earlier)


def project_kernel(count, pos_ref, turn_ref, *refs):
    tok_refs, w_refs, out_ref = refs[:4], refs[4 : 4 + count], refs[-1]
    plane, side, core = pos_ref[0], pos_ref[1], pos_ref[2]
    rows = tok_refs[0].shape[0]
    is_key = core == 0
    for half in range(PLANES // 2):
        acc = jnp.zeros((4 * rows, 2 * HD), jnp.float32)
        for o, w_ref in enumerate(w_refs):
            depth = w_ref.shape[0]
            span = pl.ds(pl.multiple_of(pos_ref[3 + o] * depth, HD), depth)
            part = jnp.concatenate([t[:, span] for t in tok_refs], axis=0)
            acc = acc + jnp.dot(
                part,
                w_ref[:, half * 2 * HD : (half + 1) * 2 * HD],
                preferred_element_type=jnp.float32,
            )
        for b in range(2):
            at = 2 * half + b
            for piece in range(4):
                x = 1 - side if piece % 2 else side
                c = 1 - core if piece // 2 else core
                start = pl.multiple_of((plane * 4 + 2 * x + c) * rows, rows)
                head = acc[piece * rows : (piece + 1) * rows, b * HD : (b + 1) * HD]
                cosine, sine = rotation(turn_ref[pl.ds(start, rows), :])
                cosine, sine = jnp.where(is_key, cosine, 1.0), jnp.where(is_key, sine, 0.0)
                turned = head * cosine + pltpu.roll(head, HD // 2, 1) * sine
                out_ref[at, piece * rows : (piece + 1) * rows] = turned.astype(jnp.bfloat16)


def project(position, turns, pieces, weights, *earlier):
    rows, width = pieces[0].shape
    return pl.pallas_call(
        functools.partial(project_kernel, len(weights)),
        out_shape=jax.ShapeDtypeStruct((PLANES, 4 * rows, HD), jnp.bfloat16),
        in_specs=smem_specs(1)
        + vmem_specs(5 + len(weights))
        + [pl.BlockSpec(memory_space=pl.ANY)] * len(earlier),
        out_specs=vmem_specs(1)[0],
        compiler_params=pltpu.CompilerParams(vmem_limit_bytes=40 * 2**20),
        cost_estimate=cost(8 * rows * width * PLANES * HD, *pieces, *weights),
    )(position, turns, *pieces, *weights, *earlier)


def fill_columns(pos_ref, cr, mine_ref, its_ref, near_mine_ref, near_its_ref, grad_s):
    for ar in range(2):
        for br in range(2):
            block = pos_ref[0] ^ (2 * ar + br)
            if br:
                value = (near_its_ref if ar else near_mine_ref)[cr]
            else:
                value = (its_ref if ar else mine_ref)[cr, 0]
            grad_s[:, pl.ds(pl.multiple_of(block * HD, HD), HD)] = value


def other_core_kernel(count, pos_ref, mine_ref, its_ref, near_mine_ref, near_its_ref, *refs):
    w_refs, out_ref, grad_s = refs[:count], refs[-2], refs[-1]
    fill_columns(pos_ref, 1, mine_ref, its_ref, near_mine_ref, near_its_ref, grad_s)
    for o, w_ref in enumerate(w_refs):
        depth = w_ref.shape[0]
        span = pl.ds(pl.multiple_of(pos_ref[3 + o] * depth, HD), depth)
        out_ref[:, span] = lax.dot_general(
            grad_s[...], w_ref[...], (((1,), (1,)), ((), ())), preferred_element_type=jnp.float32
        ).astype(out_ref.dtype)


def same_core_kernel(count, pos_ref, mine_ref, its_ref, near_mine_ref, near_its_ref, came_ref, *refs):
    w_refs, (keep_ref, send_ref, grad_s) = refs[:count], refs[-3:]
    rows = keep_ref.shape[0]
    fill_columns(pos_ref, 0, mine_ref, its_ref, near_mine_ref, near_its_ref, grad_s)
    for o, w_ref in enumerate(w_refs):
        depth = w_ref.shape[0]
        span = pl.ds(pl.multiple_of(pos_ref[3 + o] * depth, HD), depth)
        term = lax.dot_general(
            grad_s[...], w_ref[...], (((1,), (1,)), ((), ())), preferred_element_type=jnp.float32
        ) + came_ref[:, span].astype(jnp.float32)
        keep_ref[:, span] = term[:rows]
        send_ref[:, span] = term[rows:].astype(send_ref.dtype)


def input_terms(position, blocks, weights, earlier, came=None):
    rows = blocks[0].shape[2]
    width = sum(w.shape[0] for w in weights)
    bf16 = jnp.bfloat16
    count = len(weights)
    if came is None:
        kernel, extra = functools.partial(other_core_kernel, count), ()
        shapes = jax.ShapeDtypeStruct((rows, width), bf16)
        out_specs = vmem_specs(1)[0]
    else:
        kernel, extra = functools.partial(same_core_kernel, count), (came,)
        shapes = (
            jax.ShapeDtypeStruct((rows // 2, width), jnp.float32),
            jax.ShapeDtypeStruct((rows // 2, width), bf16),
        )
        out_specs = vmem_specs(2)
    return pl.pallas_call(
        kernel,
        out_shape=shapes,
        in_specs=smem_specs(1)
        + vmem_specs(4 + len(extra) + len(weights))
        + [pl.BlockSpec(memory_space=pl.ANY)] * len(earlier),
        out_specs=out_specs,
        scratch_shapes=[pltpu.VMEM((rows, PLANES * HD), bf16)],
        compiler_params=pltpu.CompilerParams(vmem_limit_bytes=16 * 2**20),
        cost_estimate=cost(2 * rows * width * PLANES * HD, *weights),
    )(position, *blocks, *extra, *weights, *earlier)


def after(values, *earlier):
    count = len(values)
    anywhere = pl.BlockSpec(memory_space=pl.ANY)
    return pl.pallas_call(
        lambda *refs: None,
        out_shape=tuple(jax.ShapeDtypeStruct(v.shape, v.dtype) for v in values),
        in_specs=[anywhere] * (count + len(earlier)),
        out_specs=(anywhere,) * count,
        input_output_aliases={i: i for i in range(count)},
    )(*values, *earlier)


def simple_kernel(kernel, shapes, scalars, arrays, earlier=()):
    anywhere = pl.BlockSpec(memory_space=pl.ANY)
    return pl.pallas_call(
        kernel,
        out_shape=shapes,
        in_specs=smem_specs(1) + vmem_specs(len(arrays)) + [anywhere] * len(earlier),
        out_specs=jax.tree.map(lambda _: vmem_specs(1)[0], shapes),
        compiler_params=pltpu.CompilerParams(vmem_limit_bytes=16 * 2**20),
        cost_estimate=cost(0, *arrays),
    )(scalars, *arrays, *earlier)


def head_of(device):
    plane, side, core = device // 4, (device // 2) % 2, device % 2
    return 8 * (plane // 2) + 4 * side + 2 * (plane % 2) + core


def join_heads_kernel(pos_ref, in_ref, out_ref):
    for device in range(SEQ):
        head = head_of(device)
        out_ref[:, head * HD : (head + 1) * HD] = in_ref[device]


def head_columns(at):
    return (at // 2) * 1024 + lax.rem(at, 2) * 256


def planes_kernel(pos_ref, q_ref, d_ref, _, *out_refs):
    for step, out_ref in enumerate(out_refs, 1):
        start = pl.multiple_of(head_columns(lax.rem(pos_ref[0] + step, PLANES)), 256)
        for i, ref in enumerate((q_ref, d_ref)):
            out_ref[i, :, :256] = ref[:, pl.ds(start, 256)]
            out_ref[i, :, 256:] = ref[:, pl.ds(start + 512, 256)]


def sides_kernel(pos_ref, q_ref, d_ref, one_ref, two_ref, three_ref, _, kept_ref, send_ref):
    plane, side = pos_ref[0], pos_ref[1]
    for out_ref, x in ((kept_ref, side), (send_ref, 1 - side)):
        start = pl.multiple_of(head_columns(plane) + 512 * x, 256)
        for i, ref in enumerate((q_ref, d_ref)):
            out_ref[0, i] = ref[:, pl.ds(start, 256)]
        for step, ref in enumerate((one_ref, two_ref, three_ref), 1):
            out_ref[step] = ref[:, :, pl.ds(pl.multiple_of(256 * x, 256), 256)]


def cores_kernel(pos_ref, same_ref, other_ref, tok_ref, _, kept_ref, send_ref, copy_ref):
    copy_ref[...] = tok_ref[...]
    core = pos_ref[2]
    for out_ref, c in ((kept_ref, core), (send_ref, 1 - core)):
        span = pl.ds(pl.multiple_of(HD * c, HD), HD)
        out_ref[0] = same_ref[:, :, :, span]
        out_ref[1] = other_ref[:, :, :, span]


def add_kernel(pos_ref, keep_ref, came_ref, mine_ref, theirs_ref, next_ref):
    for pair, out_ref in enumerate((mine_ref, theirs_ref)):
        for cr in range(2):
            for pr in range(2):
                total = keep_ref[pair, cr, pr] + came_ref[pair, cr, pr].astype(jnp.float32)
                total = total.astype(out_ref.dtype)
                out_ref[cr, pr] = total
                if pr and not pair:
                    next_ref[cr] = total


def weight_kernel(count, pos_ref, grad_ref, *refs):
    tok_refs, out_refs = refs[:8], refs[-count:]
    for o, out_ref in enumerate(out_refs):
        depth = out_ref.shape[1]
        at = lax.rem(pos_ref[3] + o, count)
        span = pl.ds(pl.multiple_of(at * depth, HD), depth)
        acc = jnp.zeros(out_ref.shape, jnp.float32)
        for cr in range(2):
            for pr in range(2):
                grad = grad_ref[cr, pr].astype(jnp.float32).T.astype(jnp.bfloat16)
                first = 4 * cr + 2 * pr
                part = jnp.concatenate([t[:, span] for t in tok_refs[first : first + 2]], axis=0)
                acc = acc + jnp.dot(grad, part, preferred_element_type=jnp.float32)
        out_ref[...] = acc.astype(out_ref.dtype)


def sum_kernel(count, pos_ref, *refs):
    total = sum(r[...].astype(jnp.float32) for r in refs[:count])
    refs[-1][...] = total.astype(refs[-1].dtype)


def finish_kernel(pos_ref, one_ref, two_ref, _, out_ref):
    total = one_ref[...].astype(jnp.float32) + two_ref[...].astype(jnp.float32)
    out_ref[...] = total.T


def exchange(value, groups=None):
    return lax.all_to_all(value, "seq", 0, 0, axis_index_groups=groups, tiled=True)


def on_device(inputs, queries, w_kv, doc_lengths, grad_out):
    bf16, f32 = jnp.bfloat16, jnp.float32
    tokens = inputs[0]
    query_rows = queries[0]
    cotangent = grad_out[0]
    lengths = doc_lengths[0]
    rows, width = tokens.shape
    total = SEQ * rows
    half_kv = KVH * HD
    seqs = lax.axis_size("fsdp")
    depth = w_kv.shape[0]
    here = lax.axis_index("seq")
    own_seq = lax.axis_index("fsdp")
    plane, side, core = here >> 2, (here >> 1) & 1, here & 1
    origins = [(own_seq - o) % seqs for o in range(seqs)]

    first = core * half_kv + side * 256
    w_own = jnp.concatenate(
        [columns(w_kv, first, 256), columns(w_kv, first + half_kv // 2, 256)], axis=1
    )
    w_parts = [w_own] + [shift_rows(w_own, o) for o in range(1, seqs)]
    if depth % HD:
        w_full = jnp.zeros((width, PLANES * HD), bf16)
        for o in range(seqs):
            w_full = lax.dynamic_update_slice_in_dim(w_full, w_parts[o], origins[o] * depth, 0)
        w_parts, places_of = [w_full], [jnp.int32(0)]
    else:
        places_of = origins
    position = jnp.stack([plane, side, core] + places_of).astype(jnp.int32)
    seq_first = jnp.stack([plane, side, core, own_seq]).astype(jnp.int32)

    crossed = swap(tokens, 2)
    pieces = [tokens, crossed, swap(tokens, 1), swap(crossed, 1)]

    places = jnp.arange(total, dtype=jnp.int32)
    doc_ends = jnp.cumsum(lengths)
    ended = doc_ends[None, :] <= places[:, None]
    within = places - jnp.sum(jnp.where(ended, lengths[None, :], 0), axis=1)
    exponent = jnp.arange(HD // 2, dtype=f32) * (2.0 / HD)
    rate = jnp.power(ROPE_BASE, -exponent)
    angles = within.astype(f32)[:, None] * jnp.concatenate([rate, rate])[None, :]
    quarter = jnp.where(jnp.arange(HD) < HD // 2, jnp.float32(jnp.pi / 2), jnp.float32(0.0))
    turns = jnp.sin(angles + quarter[None, :])

    def bf16s(*shape):
        return jax.ShapeDtypeStruct(shape, bf16)

    for_planes = simple_kernel(
        planes_kernel, (bf16s(2, rows, 512),) * 3, position, (query_rows, cotangent), (w_own,)
    )
    from_planes = [shift_planes(part, k) for k, part in enumerate(for_planes, 1)]
    same_side, for_side = simple_kernel(
        sides_kernel,
        (bf16s(4, 2, rows, 256),) * 2,
        position,
        (query_rows, cotangent, *from_planes),
        (crossed,),
    )
    from_side = swap_sides(for_side)

    kv_blocks = project(position, turns, pieces, w_parts, for_side)
    own = exchange(kv_blocks, [[r + 4 * p for p in range(PLANES)] for r in range(4)])
    other = swap_cores(own)
    kept, for_other, tokens_later = simple_kernel(
        cores_kernel,
        (bf16s(2, 4, 2, rows, HD),) * 2 + (bf16s(rows, width),),
        position,
        (same_side, from_side, tokens),
        (own,),
    )
    came = swap_cores(for_other)

    beside = swap(tokens_later, 4)

    out_parts, keep, send = attention(
        lengths, position, kept, came, turns, own, other
    )

    (beside,) = after((beside,), send)
    beside_crossed = swap(beside, 2)
    pieces_beside = [beside, beside_crossed, swap(beside, 1), swap(beside_crossed, 1)]

    mine, theirs, mine_next = simple_kernel(
        add_kernel,
        (bf16s(2, 2, 2 * rows, HD),) * 2 + (bf16s(2, 2 * rows, HD),),
        position,
        (keep, swap_cores(send)),
    )
    its = swap(theirs, 8)

    outs = exchange(after((out_parts,), its)[0])

    blocks = (mine, its, swap(mine_next, 4), swap(its[:, 1], 4))
    pair_tokens = [*pieces[:2], *pieces_beside[:2], *pieces[2:], *pieces_beside[2:]]

    def weight_terms(grad, *earlier):
        cuts = 1 if depth % HD else seqs
        terms = simple_kernel(
            functools.partial(weight_kernel, cuts),
            (bf16s(HD, width // cuts),) * cuts,
            seq_first,
            (grad, *pair_tokens),
            earlier,
        )
        if cuts < seqs:
            terms = [columns(terms[0], ((own_seq + o) % seqs) * depth, depth) for o in range(seqs)]
        return terms

    def weight_sum(terms, *earlier):
        terms = [shift_rows(t, o) if o else t for o, t in enumerate(terms)]
        return simple_kernel(
            functools.partial(sum_kernel, seqs), bf16s(HD, depth), position, terms, earlier
        )

    mine_terms = weight_terms(mine, blocks[2])
    mine_sum = weight_sum(mine_terms)
    its_terms = weight_terms(its)

    for_core = input_terms(position, blocks, w_parts, mine_terms[:1])
    for_self, for_side = input_terms(
        position, blocks, w_parts, (mine_sum,), swap_cores(for_core)
    )
    from_side = swap_sides(for_side)

    terms = [mine_sum, weight_sum(its_terms, for_side)]

    sums = []
    for ar, term in enumerate(terms):
        pairs = []
        for s in range(SEQ):
            half = (s // 8 + ar) % 2
            pairs.append((s, (2 * (s % 2) + half) * 4 + (s & 2) + (s // 4) % 2))
        sums.append(lax.ppermute(term, "seq", pairs))

    out_rows = simple_kernel(
        join_heads_kernel, bf16s(rows, QH * HD), position, (outs,)
    )
    grad_rows = (for_self + from_side.astype(f32)).astype(bf16)
    finished = simple_kernel(
        finish_kernel, jax.ShapeDtypeStruct((depth, HD), f32), position, sums, (outs,)
    )
    return (out_rows[None], grad_rows[None], finished)


def solution(mesh):
    in_specs = (
        P("fsdp", "seq", None),
        P("fsdp", "seq", None),
        P("fsdp", None),
        P("fsdp", None),
        P("fsdp", "seq", None),
    )
    out_specs = (P("fsdp", "seq", None), P("fsdp", "seq", None), P("fsdp", "seq"))
    return jax.shard_map(
        on_device, mesh=mesh, in_specs=in_specs, out_specs=out_specs, check_vma=False
    )
```

```python
import functools

import jax
import jax.numpy as jnp
from jax import lax
from jax.experimental import pallas as pl
from jax.experimental.pallas import tpu as pltpu
from jax.sharding import PartitionSpec as P

QH = 16
KVH = 8
HD = 128
WIN = 1024
G = 2

SOFT_CAP = 50.0
QUERY_SCALE = 1.0 / 12.0
ROPE_BASE = 10000.0

SEQ = 16
PLANES = 4
BLK = 256
REACH = WIN // BLK + 1


def cost(flops, *arrays):
    moved = sum(a.size * a.dtype.itemsize for a in arrays)
    return pl.CostEstimate(flops=flops, bytes_accessed=2 * moved, transcendentals=0)


def shift_planes(value, steps):
    pairs = [(s, (s + 4 * steps) % SEQ) for s in range(SEQ)]
    return lax.ppermute(value, "seq", pairs)


def swap(value, mask):
    return lax.ppermute(value, "seq", [(s, s ^ mask) for s in range(SEQ)])


def swap_sides(value):
    return swap(value, 2)


def swap_cores(value):
    return swap(value, 1)


def shift_rows(value, steps):
    count = lax.axis_size("fsdp")
    return lax.ppermute(value, "fsdp", [(i, (i + steps) % count) for i in range(count)])


def columns(value, start, size):
    return lax.dynamic_slice_in_dim(value, start, size, value.ndim - 1)


def rotation(table):
    swapped = pltpu.roll(table, HD // 2, 1)
    first = lax.broadcasted_iota(jnp.int32, table.shape, 1) < HD // 2
    return jnp.where(first, table, swapped), jnp.where(first, -swapped, table)


def attention_kernel(
    len_ref, pos_ref, kept_ref, came_ref, turn_ref, own_ref, oth_ref, *refs
):
    out_ref, keep_ref, send_ref, q_s, d_s, kv_s, vt_s, e_s, t_s, dk_s, dv_s = refs[-11:]
    plane, side, core = pos_ref[0], pos_ref[1], pos_ref[2]
    rows = out_ref.shape[1]
    total = dk_s.shape[0]
    f32 = jnp.float32
    nt = (((1,), (1,)), ((), ()))

    def flipped(bit, flip):
        return 1 - bit if flip else bit

    for step in range(PLANES):
        home = lax.rem(plane + (PLANES - step), PLANES)
        for xr in range(2):
            for cr in range(2):
                base = home * (4 * rows) + flipped(side, xr) * (2 * rows)
                base = pl.multiple_of(base + flipped(core, cr) * rows, rows)
                source = came_ref if cr else kept_ref
                q_s[pl.ds(base, rows), :] = source[xr, step, 0]
                d_s[pl.ds(base, rows), :] = source[xr, step, 1]

    for at in range(PLANES):
        for xr in range(2):
            for cr in range(2):
                base = at * (4 * rows) + flipped(side, xr) * (2 * rows)
                mine = pl.multiple_of(base + flipped(core, cr) * rows, rows)
                theirs = pl.multiple_of(base + flipped(core, 1 - cr) * rows, rows)
                piece = pl.ds((2 * cr + xr) * rows, rows)
                kv_s[core, pl.ds(mine, rows), :] = own_ref[at, piece, :]
                kv_s[1 - core, pl.ds(theirs, rows), :] = oth_ref[at, piece, :]

    for block in range(total // BLK):
        span = pl.ds(block * BLK, BLK)
        vt_s[:, span] = kv_s[1, span, :].astype(f32).T.astype(jnp.bfloat16)
    dk_s[...] = jnp.zeros_like(dk_s)
    dv_s[...] = jnp.zeros_like(dv_s)

    ends = []
    run = 0
    for j in range(len_ref.shape[0]):
        run = run + len_ref[j]
        ends.append(run)

    def query_block(i, carry):
        base = pl.multiple_of(i * BLK, BLK)
        first_part = i * (BLK // rows)
        qb, db = q_s[pl.ds(base, BLK), :], d_s[pl.ds(base, BLK), :]
        p_row = base + lax.broadcasted_iota(jnp.int32, (1, BLK), 1)
        start_row = jnp.zeros((1, BLK), jnp.int32)
        first = jnp.int32(0)
        for end in ends:
            start_row = jnp.where(end <= p_row, end, start_row)
            first = jnp.where(end <= base, end, first)
        low_row = jnp.maximum(start_row, p_row - (WIN - 1))
        low_block = jnp.maximum(first, jnp.maximum(base - (WIN - 1), 0)) // BLK
        count = i - low_block + 1

        def body(n):
            def key_span(j):
                return pl.ds(pl.multiple_of((low_block + j) * BLK, BLK), BLK)

            norm = jnp.zeros((1, BLK), f32)
            out_t = jnp.zeros((HD, BLK), f32)
            for j in range(n):
                keys = key_span(j)
                scores = lax.dot_general(kv_s[0, keys, :], qb, nt, preferred_element_type=f32)
                squashed = jnp.tanh(scores * (QUERY_SCALE / SOFT_CAP))
                weights = jnp.exp(squashed * SOFT_CAP)
                n_col = (low_block + j) * BLK + lax.broadcasted_iota(jnp.int32, (BLK, 1), 0)
                allowed = n_col >= low_row
                if j == n - 1:
                    allowed = allowed & (n_col <= p_row)
                weights = jnp.where(allowed, weights, 0.0)
                t_s[j] = squashed
                e_s[j] = weights
                norm = norm + jnp.sum(weights, axis=0, keepdims=True)
                out_t = out_t + jnp.dot(
                    vt_s[:, keys], weights.astype(jnp.bfloat16), preferred_element_type=f32
                )
            inverse = 1.0 / norm
            out_f = (out_t * inverse).astype(jnp.bfloat16).astype(f32)
            delta = jnp.sum(db.astype(f32).T * out_f, axis=0, keepdims=True)
            out_b = out_f.T.astype(jnp.bfloat16)
            for j in range(BLK // rows):
                out_ref[first_part + j] = out_b[j * rows : (j + 1) * rows]
            for j in range(n):
                keys = key_span(j)
                probs = e_s[j] * inverse
                squashed = t_s[j]
                dv_s[keys, :] += jnp.dot(
                    probs.astype(jnp.bfloat16), db, preferred_element_type=f32
                )
                dprob = lax.dot_general(kv_s[1, keys, :], db, nt, preferred_element_type=f32)
                dscore = probs * (dprob - delta) * (1.0 - squashed * squashed)
                dk_s[keys, :] += jnp.dot(
                    dscore.astype(jnp.bfloat16), qb, preferred_element_type=f32
                )

        for n in range(1, REACH + 1):
            pl.when(count == n)(lambda n=n: body(n))
        return carry

    lax.fori_loop(0, total // BLK, query_block, 0)

    def finish(block, carry):
        span = pl.ds(pl.multiple_of(block * rows, rows), rows)
        key_part = dk_s[span, :] * QUERY_SCALE
        cosine, sine = rotation(turn_ref[span, :])
        key_part = key_part * cosine - pltpu.roll(key_part, HD // 2, 1) * sine
        value_part = dv_s[span, :]
        to_pair = lax.rem(block // 8 + plane // 2, 2)
        to_plane = lax.rem(block // 4 + plane, 2)
        to_side = lax.rem(block // 2 + side, 2)
        to_core = lax.rem(block + core, 2)
        is_key = core == 0
        at = pl.ds(pl.multiple_of(to_side * rows, rows), rows)
        keep_ref[to_pair, to_core, to_plane, at, :] = jnp.where(is_key, key_part, value_part)
        send_ref[to_pair, 1 - to_core, to_plane, at, :] = jnp.where(
            is_key, value_part, key_part
        ).astype(jnp.bfloat16)
        return carry

    lax.fori_loop(0, total // rows, finish, 0)


def vmem_specs(count):
    return [pl.BlockSpec(memory_space=pltpu.VMEM)] * count


def smem_specs(count):
    return [pl.BlockSpec(memory_space=pltpu.SMEM)] * count


def attention(lengths, position, kept, came, turns, own, other, *earlier):
    rows = kept.shape[3]
    total = SEQ * rows
    bf16, f32 = jnp.bfloat16, jnp.float32
    return pl.pallas_call(
        attention_kernel,
        out_shape=(
            jax.ShapeDtypeStruct((SEQ, rows, HD), bf16),
            jax.ShapeDtypeStruct((2, 2, 2, 2 * rows, HD), f32),
            jax.ShapeDtypeStruct((2, 2, 2, 2 * rows, HD), bf16),
        ),
        in_specs=smem_specs(2)
        + vmem_specs(5)
        + [pl.BlockSpec(memory_space=pl.ANY)] * len(earlier),
        out_specs=vmem_specs(3),
        scratch_shapes=[
            pltpu.VMEM((total, HD), bf16),
            pltpu.VMEM((total, HD), bf16),
            pltpu.VMEM((2, total, HD), bf16),
            pltpu.VMEM((HD, total), bf16),
            pltpu.VMEM((REACH, BLK, BLK), f32),
            pltpu.VMEM((REACH, BLK, BLK), f32),
            pltpu.VMEM((total, HD), f32),
            pltpu.VMEM((total, HD), f32),
        ],
        compiler_params=pltpu.CompilerParams(vmem_limit_bytes=22 * 2**20),
        cost_estimate=cost(300 * BLK * BLK * HD, kept, came, own, other, turns),
    )(lengths, position, kept, came, turns, own, other, *earlier)


def project_kernel(count, pos_ref, turn_ref, *refs):
    tok_refs, w_refs, out_ref = refs[:4], refs[4 : 4 + count], refs[-1]
    plane, side, core = pos_ref[0], pos_ref[1], pos_ref[2]
    rows = tok_refs[0].shape[0]
    is_key = core == 0
    for half in range(PLANES // 2):
        acc = jnp.zeros((4 * rows, 2 * HD), jnp.float32)
        for o, w_ref in enumerate(w_refs):
            depth = w_ref.shape[0]
            span = pl.ds(pl.multiple_of(pos_ref[3 + o] * depth, HD), depth)
            part = jnp.concatenate([t[:, span] for t in tok_refs], axis=0)
            acc = acc + jnp.dot(
                part,
                w_ref[:, half * 2 * HD : (half + 1) * 2 * HD],
                preferred_element_type=jnp.float32,
            )
        for b in range(2):
            at = 2 * half + b
            for piece in range(4):
                x = 1 - side if piece % 2 else side
                c = 1 - core if piece // 2 else core
                start = pl.multiple_of((plane * 4 + 2 * x + c) * rows, rows)
                head = acc[piece * rows : (piece + 1) * rows, b * HD : (b + 1) * HD]
                cosine, sine = rotation(turn_ref[pl.ds(start, rows), :])
                cosine, sine = jnp.where(is_key, cosine, 1.0), jnp.where(is_key, sine, 0.0)
                turned = head * cosine + pltpu.roll(head, HD // 2, 1) * sine
                out_ref[at, piece * rows : (piece + 1) * rows] = turned.astype(jnp.bfloat16)


def project(position, turns, pieces, weights, *earlier):
    rows, width = pieces[0].shape
    return pl.pallas_call(
        functools.partial(project_kernel, len(weights)),
        out_shape=jax.ShapeDtypeStruct((PLANES, 4 * rows, HD), jnp.bfloat16),
        in_specs=smem_specs(1)
        + vmem_specs(5 + len(weights))
        + [pl.BlockSpec(memory_space=pl.ANY)] * len(earlier),
        out_specs=vmem_specs(1)[0],
        compiler_params=pltpu.CompilerParams(vmem_limit_bytes=40 * 2**20),
        cost_estimate=cost(8 * rows * width * PLANES * HD, *pieces, *weights),
    )(position, turns, *pieces, *weights, *earlier)


def fill_columns(pos_ref, cr, mine_ref, its_ref, near_mine_ref, near_its_ref, grad_s):
    for ar in range(2):
        for br in range(2):
            block = pos_ref[0] ^ (2 * ar + br)
            if br:
                value = (near_its_ref if ar else near_mine_ref)[cr]
            else:
                value = (its_ref if ar else mine_ref)[cr, 0]
            grad_s[:, pl.ds(pl.multiple_of(block * HD, HD), HD)] = value


def other_core_kernel(count, pos_ref, mine_ref, its_ref, near_mine_ref, near_its_ref, *refs):
    w_refs, out_ref, grad_s = refs[:count], refs[-2], refs[-1]
    fill_columns(pos_ref, 1, mine_ref, its_ref, near_mine_ref, near_its_ref, grad_s)
    for o, w_ref in enumerate(w_refs):
        depth = w_ref.shape[0]
        span = pl.ds(pl.multiple_of(pos_ref[3 + o] * depth, HD), depth)
        out_ref[:, span] = lax.dot_general(
            grad_s[...], w_ref[...], (((1,), (1,)), ((), ())), preferred_element_type=jnp.float32
        ).astype(out_ref.dtype)


def same_core_kernel(count, pos_ref, mine_ref, its_ref, near_mine_ref, near_its_ref, came_ref, *refs):
    w_refs, (keep_ref, send_ref, grad_s) = refs[:count], refs[-3:]
    rows = keep_ref.shape[0]
    fill_columns(pos_ref, 0, mine_ref, its_ref, near_mine_ref, near_its_ref, grad_s)
    for o, w_ref in enumerate(w_refs):
        depth = w_ref.shape[0]
        span = pl.ds(pl.multiple_of(pos_ref[3 + o] * depth, HD), depth)
        term = lax.dot_general(
            grad_s[...], w_ref[...], (((1,), (1,)), ((), ())), preferred_element_type=jnp.float32
        ) + came_ref[:, span].astype(jnp.float32)
        keep_ref[:, span] = term[:rows]
        send_ref[:, span] = term[rows:].astype(send_ref.dtype)


def input_terms(position, blocks, weights, earlier, came=None):
    rows = blocks[0].shape[2]
    width = sum(w.shape[0] for w in weights)
    bf16 = jnp.bfloat16
    count = len(weights)
    if came is None:
        kernel, extra = functools.partial(other_core_kernel, count), ()
        shapes = jax.ShapeDtypeStruct((rows, width), bf16)
        out_specs = vmem_specs(1)[0]
    else:
        kernel, extra = functools.partial(same_core_kernel, count), (came,)
        shapes = (
            jax.ShapeDtypeStruct((rows // 2, width), jnp.float32),
            jax.ShapeDtypeStruct((rows // 2, width), bf16),
        )
        out_specs = vmem_specs(2)
    return pl.pallas_call(
        kernel,
        out_shape=shapes,
        in_specs=smem_specs(1)
        + vmem_specs(4 + len(extra) + len(weights))
        + [pl.BlockSpec(memory_space=pl.ANY)] * len(earlier),
        out_specs=out_specs,
        scratch_shapes=[pltpu.VMEM((rows, PLANES * HD), bf16)],
        compiler_params=pltpu.CompilerParams(vmem_limit_bytes=16 * 2**20),
        cost_estimate=cost(2 * rows * width * PLANES * HD, *weights),
    )(position, *blocks, *extra, *weights, *earlier)


def after(values, *earlier):
    count = len(values)
    anywhere = pl.BlockSpec(memory_space=pl.ANY)
    return pl.pallas_call(
        lambda *refs: None,
        out_shape=tuple(jax.ShapeDtypeStruct(v.shape, v.dtype) for v in values),
        in_specs=[anywhere] * (count + len(earlier)),
        out_specs=(anywhere,) * count,
        input_output_aliases={i: i for i in range(count)},
    )(*values, *earlier)


def simple_kernel(kernel, shapes, scalars, arrays, earlier=()):
    anywhere = pl.BlockSpec(memory_space=pl.ANY)
    return pl.pallas_call(
        kernel,
        out_shape=shapes,
        in_specs=smem_specs(1) + vmem_specs(len(arrays)) + [anywhere] * len(earlier),
        out_specs=jax.tree.map(lambda _: vmem_specs(1)[0], shapes),
        compiler_params=pltpu.CompilerParams(vmem_limit_bytes=16 * 2**20),
        cost_estimate=cost(0, *arrays),
    )(scalars, *arrays, *earlier)


def head_of(device):
    plane, side, core = device // 4, (device // 2) % 2, device % 2
    return 8 * (plane // 2) + 4 * side + 2 * (plane % 2) + core


def join_heads_kernel(pos_ref, in_ref, out_ref):
    for device in range(SEQ):
        head = head_of(device)
        out_ref[:, head * HD : (head + 1) * HD] = in_ref[device]


def head_columns(at):
    return (at // 2) * 1024 + lax.rem(at, 2) * 256


def planes_kernel(pos_ref, q_ref, d_ref, _, *out_refs):
    for step, out_ref in enumerate(out_refs, 1):
        start = pl.multiple_of(head_columns(lax.rem(pos_ref[0] + step, PLANES)), 256)
        for i, ref in enumerate((q_ref, d_ref)):
            out_ref[i, :, :256] = ref[:, pl.ds(start, 256)]
            out_ref[i, :, 256:] = ref[:, pl.ds(start + 512, 256)]


def sides_kernel(pos_ref, q_ref, d_ref, one_ref, two_ref, three_ref, _, kept_ref, send_ref):
    plane, side = pos_ref[0], pos_ref[1]
    for out_ref, x in ((kept_ref, side), (send_ref, 1 - side)):
        start = pl.multiple_of(head_columns(plane) + 512 * x, 256)
        for i, ref in enumerate((q_ref, d_ref)):
            out_ref[0, i] = ref[:, pl.ds(start, 256)]
        for step, ref in enumerate((one_ref, two_ref, three_ref), 1):
            out_ref[step] = ref[:, :, pl.ds(pl.multiple_of(256 * x, 256), 256)]


def cores_kernel(pos_ref, same_ref, other_ref, tok_ref, _, kept_ref, send_ref, copy_ref):
    copy_ref[...] = tok_ref[...]
    core = pos_ref[2]
    for out_ref, c in ((kept_ref, core), (send_ref, 1 - core)):
        span = pl.ds(pl.multiple_of(HD * c, HD), HD)
        out_ref[0] = same_ref[:, :, :, span]
        out_ref[1] = other_ref[:, :, :, span]


def add_kernel(pos_ref, keep_ref, came_ref, mine_ref, theirs_ref, next_ref):
    for pair, out_ref in enumerate((mine_ref, theirs_ref)):
        for cr in range(2):
            for pr in range(2):
                total = keep_ref[pair, cr, pr] + came_ref[pair, cr, pr].astype(jnp.float32)
                total = total.astype(out_ref.dtype)
                out_ref[cr, pr] = total
                if pr and not pair:
                    next_ref[cr] = total


def weight_kernel(count, pos_ref, mine_ref, its_ref, *refs):
    tok_refs, out_refs = refs[:8], refs[-count:]
    for o, out_ref in enumerate(out_refs):
        depth = out_ref.shape[1]
        at = lax.rem(pos_ref[3] + o, count)
        span = pl.ds(pl.multiple_of(at * depth, HD), depth)
        acc = jnp.zeros(out_ref.shape, jnp.float32)
        for cr in range(2):
            for pr in range(2):
                grad = jnp.concatenate([mine_ref[cr, pr], its_ref[cr, pr]], axis=1)
                grad = grad.astype(jnp.float32).T.astype(jnp.bfloat16)
                first = 4 * cr + 2 * pr
                part = jnp.concatenate([t[:, span] for t in tok_refs[first : first + 2]], axis=0)
                acc = acc + jnp.dot(grad, part, preferred_element_type=jnp.float32)
        out_ref[...] = acc.astype(out_ref.dtype)


def sum_kernel(count, pos_ref, *refs):
    total = sum(r[...].astype(jnp.float32) for r in refs[:count])
    for ar, out_ref in enumerate(refs[-2:]):
        out_ref[...] = total[ar * HD : (ar + 1) * HD].astype(out_ref.dtype)


def finish_kernel(pos_ref, one_ref, two_ref, _, out_ref):
    total = one_ref[...].astype(jnp.float32) + two_ref[...].astype(jnp.float32)
    out_ref[...] = total.T


def exchange(value, groups=None):
    return lax.all_to_all(value, "seq", 0, 0, axis_index_groups=groups, tiled=True)


def on_device(inputs, queries, w_kv, doc_lengths, grad_out):
    bf16, f32 = jnp.bfloat16, jnp.float32
    tokens = inputs[0]
    query_rows = queries[0]
    cotangent = grad_out[0]
    lengths = doc_lengths[0]
    rows, width = tokens.shape
    total = SEQ * rows
    half_kv = KVH * HD
    seqs = lax.axis_size("fsdp")
    depth = w_kv.shape[0]
    here = lax.axis_index("seq")
    own_seq = lax.axis_index("fsdp")
    plane, side, core = here >> 2, (here >> 1) & 1, here & 1
    origins = [(own_seq - o) % seqs for o in range(seqs)]

    first = core * half_kv + side * 256
    w_own = jnp.concatenate(
        [columns(w_kv, first, 256), columns(w_kv, first + half_kv // 2, 256)], axis=1
    )
    w_parts = [w_own] + [shift_rows(w_own, o) for o in range(1, seqs)]
    if depth % HD:
        w_full = jnp.zeros((width, PLANES * HD), bf16)
        for o in range(seqs):
            w_full = lax.dynamic_update_slice_in_dim(w_full, w_parts[o], origins[o] * depth, 0)
        w_parts, places_of = [w_full], [jnp.int32(0)]
    else:
        places_of = origins
    position = jnp.stack([plane, side, core] + places_of).astype(jnp.int32)
    seq_first = jnp.stack([plane, side, core, own_seq]).astype(jnp.int32)

    crossed = swap(tokens, 2)

    places = jnp.arange(total, dtype=jnp.int32)
    doc_ends = jnp.cumsum(lengths)
    ended = doc_ends[None, :] <= places[:, None]
    within = places - jnp.sum(jnp.where(ended, lengths[None, :], 0), axis=1)
    exponent = jnp.arange(HD // 2, dtype=f32) * (2.0 / HD)
    rate = jnp.power(ROPE_BASE, -exponent)
    angles = within.astype(f32)[:, None] * jnp.concatenate([rate, rate])[None, :]
    quarter = jnp.where(jnp.arange(HD) < HD // 2, jnp.float32(jnp.pi / 2), jnp.float32(0.0))
    turns = jnp.sin(angles + quarter[None, :])

    def bf16s(*shape):
        return jax.ShapeDtypeStruct(shape, bf16)

    for_planes = simple_kernel(
        planes_kernel, (bf16s(2, rows, 512),) * 3, position, (query_rows, cotangent), (w_own,)
    )
    from_planes = [shift_planes(part, k) for k, part in enumerate(for_planes, 1)]
    own_later, crossed_later = after((tokens, crossed), from_planes[0], turns)
    pieces = [own_later, crossed_later, swap(own_later, 1), swap(crossed_later, 1)]
    same_side, for_side = simple_kernel(
        sides_kernel,
        (bf16s(4, 2, rows, 256),) * 2,
        position,
        (query_rows, cotangent, *from_planes),
        (crossed,),
    )
    from_side = swap_sides(for_side)

    kv_blocks = project(position, turns, pieces, w_parts, for_side)
    own = exchange(kv_blocks, [[r + 4 * p for p in range(PLANES)] for r in range(4)])
    other = swap_cores(own)
    kept, for_other, tokens_later = simple_kernel(
        cores_kernel,
        (bf16s(2, 4, 2, rows, HD),) * 2 + (bf16s(rows, width),),
        position,
        (same_side, from_side, own_later),
        (own,),
    )
    came = swap_cores(for_other)

    beside = swap(tokens_later, 4)

    out_parts, keep, send = attention(
        lengths, position, kept, came, turns, own, other
    )

    (beside,) = after((beside,), send)
    beside_crossed = swap(beside, 2)
    pieces_beside = [beside, beside_crossed, swap(beside, 1), swap(beside_crossed, 1)]

    mine, theirs, mine_next = simple_kernel(
        add_kernel,
        (bf16s(2, 2, 2 * rows, HD),) * 2 + (bf16s(2, 2 * rows, HD),),
        position,
        (keep, swap_cores(send)),
    )
    its = swap(theirs, 8)

    outs = exchange(after((out_parts,), its)[0])

    blocks = (mine, its, swap(mine_next, 4), swap(its[:, 1], 4))
    pair_tokens = [*pieces[:2], *pieces_beside[:2], *pieces[2:], *pieces_beside[2:]]

    cuts = 1 if depth % HD else seqs
    terms = simple_kernel(
        functools.partial(weight_kernel, cuts),
        (bf16s(2 * HD, width // cuts),) * cuts,
        seq_first,
        (mine, its, *pair_tokens),
    )
    if cuts < seqs:
        terms = [columns(terms[0], ((own_seq + o) % seqs) * depth, depth) for o in range(seqs)]
    of_seqs = [shift_rows(t, o) if o else t for o, t in enumerate(terms)]

    for_core = input_terms(position, blocks, w_parts, terms[:1])
    for_self, for_side = input_terms(
        position, blocks, w_parts, (), swap_cores(for_core)
    )
    from_side = swap_sides(for_side)

    terms = simple_kernel(
        functools.partial(sum_kernel, seqs),
        (bf16s(HD, depth),) * 2,
        position,
        of_seqs,
        (for_side,),
    )

    sums = []
    for ar, term in enumerate(terms):
        pairs = []
        for s in range(SEQ):
            half = (s // 8 + ar) % 2
            pairs.append((s, (2 * (s % 2) + half) * 4 + (s & 2) + (s // 4) % 2))
        sums.append(lax.ppermute(term, "seq", pairs))

    out_rows = simple_kernel(
        join_heads_kernel, bf16s(rows, QH * HD), position, (outs,)
    )
    grad_rows = (for_self + from_side.astype(f32)).astype(bf16)
    finished = simple_kernel(
        finish_kernel, jax.ShapeDtypeStruct((depth, HD), f32), position, sums, (outs,)
    )
    return (out_rows[None], grad_rows[None], finished)


def solution(mesh):
    in_specs = (
        P("fsdp", "seq", None),
        P("fsdp", "seq", None),
        P("fsdp", None),
        P("fsdp", None),
        P("fsdp", "seq", None),
    )
    out_specs = (P("fsdp", "seq", None), P("fsdp", "seq", None), P("fsdp", "seq"))
    return jax.shard_map(
        on_device, mesh=mesh, in_specs=in_specs, out_specs=out_specs, check_vma=False
    )
```

```python
import functools

import jax
import jax.numpy as jnp
from jax import lax
from jax.experimental import pallas as pl
from jax.experimental.pallas import tpu as pltpu
from jax.sharding import PartitionSpec as P

QH = 16
KVH = 8
HD = 128
WIN = 1024
G = 2

SOFT_CAP = 50.0
QUERY_SCALE = 1.0 / 12.0
ROPE_BASE = 10000.0

SEQ = 16
PLANES = 4
BLK = 256
REACH = WIN // BLK + 1


def cost(flops, *arrays):
    moved = sum(a.size * a.dtype.itemsize for a in arrays)
    return pl.CostEstimate(flops=flops, bytes_accessed=2 * moved, transcendentals=0)


def shift_planes(value, steps):
    pairs = [(s, (s + 4 * steps) % SEQ) for s in range(SEQ)]
    return lax.ppermute(value, "seq", pairs)


def swap(value, mask):
    return lax.ppermute(value, "seq", [(s, s ^ mask) for s in range(SEQ)])


def swap_sides(value):
    return swap(value, 2)


def swap_cores(value):
    return swap(value, 1)


def shift_rows(value, steps):
    count = lax.axis_size("fsdp")
    return lax.ppermute(value, "fsdp", [(i, (i + steps) % count) for i in range(count)])


def columns(value, start, size):
    return lax.dynamic_slice_in_dim(value, start, size, value.ndim - 1)


def rotation(table):
    swapped = pltpu.roll(table, HD // 2, 1)
    first = lax.broadcasted_iota(jnp.int32, table.shape, 1) < HD // 2
    return jnp.where(first, table, swapped), jnp.where(first, -swapped, table)


def attention_kernel(
    len_ref, pos_ref, kept_ref, came_ref, turn_ref, own_ref, oth_ref, *refs
):
    out_ref, keep_ref, send_ref, q_s, d_s, kv_s, vt_s, e_s, t_s, dk_s, dv_s = refs[-11:]
    plane, side, core = pos_ref[0], pos_ref[1], pos_ref[2]
    rows = out_ref.shape[1]
    total = dk_s.shape[0]
    f32 = jnp.float32
    nt = (((1,), (1,)), ((), ()))

    def flipped(bit, flip):
        return 1 - bit if flip else bit

    for step in range(PLANES):
        home = lax.rem(plane + (PLANES - step), PLANES)
        for xr in range(2):
            for cr in range(2):
                base = home * (4 * rows) + flipped(side, xr) * (2 * rows)
                base = pl.multiple_of(base + flipped(core, cr) * rows, rows)
                source = came_ref if cr else kept_ref
                q_s[pl.ds(base, rows), :] = source[xr, step, 0]
                d_s[pl.ds(base, rows), :] = source[xr, step, 1]

    for at in range(PLANES):
        for xr in range(2):
            for cr in range(2):
                base = at * (4 * rows) + flipped(side, xr) * (2 * rows)
                mine = pl.multiple_of(base + flipped(core, cr) * rows, rows)
                theirs = pl.multiple_of(base + flipped(core, 1 - cr) * rows, rows)
                piece = pl.ds((2 * cr + xr) * rows, rows)
                kv_s[core, pl.ds(mine, rows), :] = own_ref[at, piece, :]
                kv_s[1 - core, pl.ds(theirs, rows), :] = oth_ref[at, piece, :]

    for block in range(total // BLK):
        span = pl.ds(block * BLK, BLK)
        vt_s[:, span] = kv_s[1, span, :].astype(f32).T.astype(jnp.bfloat16)
    dk_s[...] = jnp.zeros_like(dk_s)
    dv_s[...] = jnp.zeros_like(dv_s)

    ends = []
    run = 0
    for j in range(len_ref.shape[0]):
        run = run + len_ref[j]
        ends.append(run)

    def query_block(i, carry):
        base = pl.multiple_of(i * BLK, BLK)
        first_part = i * (BLK // rows)
        qb, db = q_s[pl.ds(base, BLK), :], d_s[pl.ds(base, BLK), :]
        p_row = base + lax.broadcasted_iota(jnp.int32, (1, BLK), 1)
        start_row = jnp.zeros((1, BLK), jnp.int32)
        first = jnp.int32(0)
        for end in ends:
            start_row = jnp.where(end <= p_row, end, start_row)
            first = jnp.where(end <= base, end, first)
        low_row = jnp.maximum(start_row, p_row - (WIN - 1))
        low_block = jnp.maximum(first, jnp.maximum(base - (WIN - 1), 0)) // BLK
        count = i - low_block + 1

        def body(n):
            def key_span(j):
                return pl.ds(pl.multiple_of((low_block + j) * BLK, BLK), BLK)

            norm = jnp.zeros((1, BLK), f32)
            out_t = jnp.zeros((HD, BLK), f32)
            for j in range(n):
                keys = key_span(j)
                scores = lax.dot_general(kv_s[0, keys, :], qb, nt, preferred_element_type=f32)
                squashed = jnp.tanh(scores * (QUERY_SCALE / SOFT_CAP))
                weights = jnp.exp(squashed * SOFT_CAP)
                n_col = (low_block + j) * BLK + lax.broadcasted_iota(jnp.int32, (BLK, 1), 0)
                allowed = n_col >= low_row
                if j == n - 1:
                    allowed = allowed & (n_col <= p_row)
                weights = jnp.where(allowed, weights, 0.0)
                t_s[j] = squashed
                e_s[j] = weights
                norm = norm + jnp.sum(weights, axis=0, keepdims=True)
                out_t = out_t + jnp.dot(
                    vt_s[:, keys], weights.astype(jnp.bfloat16), preferred_element_type=f32
                )
            inverse = 1.0 / norm
            out_f = (out_t * inverse).astype(jnp.bfloat16).astype(f32)
            delta = jnp.sum(db.astype(f32).T * out_f, axis=0, keepdims=True)
            out_b = out_f.T.astype(jnp.bfloat16)
            for j in range(BLK // rows):
                out_ref[first_part + j] = out_b[j * rows : (j + 1) * rows]
            for j in range(n):
                keys = key_span(j)
                probs = e_s[j] * inverse
                squashed = t_s[j]
                dv_s[keys, :] += jnp.dot(
                    probs.astype(jnp.bfloat16), db, preferred_element_type=f32
                )
                dprob = lax.dot_general(kv_s[1, keys, :], db, nt, preferred_element_type=f32)
                dscore = probs * (dprob - delta) * (1.0 - squashed * squashed)
                dk_s[keys, :] += jnp.dot(
                    dscore.astype(jnp.bfloat16), qb, preferred_element_type=f32
                )

        for n in range(1, REACH + 1):
            pl.when(count == n)(lambda n=n: body(n))
        return carry

    lax.fori_loop(0, total // BLK, query_block, 0)

    def finish(block, carry):
        span = pl.ds(pl.multiple_of(block * rows, rows), rows)
        key_part = dk_s[span, :] * QUERY_SCALE
        cosine, sine = rotation(turn_ref[span, :])
        key_part = key_part * cosine - pltpu.roll(key_part, HD // 2, 1) * sine
        value_part = dv_s[span, :]
        to_pair = lax.rem(block // 8 + plane // 2, 2)
        to_plane = lax.rem(block // 4 + plane, 2)
        to_side = lax.rem(block // 2 + side, 2)
        to_core = lax.rem(block + core, 2)
        is_key = core == 0
        at = pl.ds(pl.multiple_of(to_side * rows, rows), rows)
        keep_ref[to_pair, to_core, to_plane, at, :] = jnp.where(is_key, key_part, value_part)
        send_ref[to_pair, 1 - to_core, to_plane, at, :] = jnp.where(
            is_key, value_part, key_part
        ).astype(jnp.bfloat16)
        return carry

    lax.fori_loop(0, total // rows, finish, 0)


def vmem_specs(count):
    return [pl.BlockSpec(memory_space=pltpu.VMEM)] * count


def smem_specs(count):
    return [pl.BlockSpec(memory_space=pltpu.SMEM)] * count


def attention(lengths, position, kept, came, turns, own, other, *earlier):
    rows = kept.shape[3]
    total = SEQ * rows
    bf16, f32 = jnp.bfloat16, jnp.float32
    return pl.pallas_call(
        attention_kernel,
        out_shape=(
            jax.ShapeDtypeStruct((SEQ, rows, HD), bf16),
            jax.ShapeDtypeStruct((2, 2, 2, 2 * rows, HD), f32),
            jax.ShapeDtypeStruct((2, 2, 2, 2 * rows, HD), bf16),
        ),
        in_specs=smem_specs(2)
        + vmem_specs(5)
        + [pl.BlockSpec(memory_space=pl.ANY)] * len(earlier),
        out_specs=vmem_specs(3),
        scratch_shapes=[
            pltpu.VMEM((total, HD), bf16),
            pltpu.VMEM((total, HD), bf16),
            pltpu.VMEM((2, total, HD), bf16),
            pltpu.VMEM((HD, total), bf16),
            pltpu.VMEM((REACH, BLK, BLK), f32),
            pltpu.VMEM((REACH, BLK, BLK), f32),
            pltpu.VMEM((total, HD), f32),
            pltpu.VMEM((total, HD), f32),
        ],
        compiler_params=pltpu.CompilerParams(vmem_limit_bytes=22 * 2**20),
        cost_estimate=cost(300 * BLK * BLK * HD, kept, came, own, other, turns),
    )(lengths, position, kept, came, turns, own, other, *earlier)


def project_kernel(count, pos_ref, turn_ref, *refs):
    tok_refs, w_refs, out_ref = refs[:4], refs[4 : 4 + count], refs[-1]
    plane, side, core = pos_ref[0], pos_ref[1], pos_ref[2]
    rows = tok_refs[0].shape[0]
    is_key = core == 0
    for half in range(PLANES // 2):
        acc = jnp.zeros((4 * rows, 2 * HD), jnp.float32)
        for o, w_ref in enumerate(w_refs):
            depth = w_ref.shape[0]
            span = pl.ds(pl.multiple_of(pos_ref[3 + o] * depth, HD), depth)
            part = jnp.concatenate([t[:, span] for t in tok_refs], axis=0)
            acc = acc + jnp.dot(
                part,
                w_ref[:, half * 2 * HD : (half + 1) * 2 * HD],
                preferred_element_type=jnp.float32,
            )
        for b in range(2):
            at = 2 * half + b
            for piece in range(4):
                x = 1 - side if piece % 2 else side
                c = 1 - core if piece // 2 else core
                start = pl.multiple_of((plane * 4 + 2 * x + c) * rows, rows)
                head = acc[piece * rows : (piece + 1) * rows, b * HD : (b + 1) * HD]
                cosine, sine = rotation(turn_ref[pl.ds(start, rows), :])
                cosine, sine = jnp.where(is_key, cosine, 1.0), jnp.where(is_key, sine, 0.0)
                turned = head * cosine + pltpu.roll(head, HD // 2, 1) * sine
                out_ref[at, piece * rows : (piece + 1) * rows] = turned.astype(jnp.bfloat16)


def project(position, turns, pieces, weights, *earlier):
    rows, width = pieces[0].shape
    return pl.pallas_call(
        functools.partial(project_kernel, len(weights)),
        out_shape=jax.ShapeDtypeStruct((PLANES, 4 * rows, HD), jnp.bfloat16),
        in_specs=smem_specs(1)
        + vmem_specs(5 + len(weights))
        + [pl.BlockSpec(memory_space=pl.ANY)] * len(earlier),
        out_specs=vmem_specs(1)[0],
        compiler_params=pltpu.CompilerParams(vmem_limit_bytes=40 * 2**20),
        cost_estimate=cost(8 * rows * width * PLANES * HD, *pieces, *weights),
    )(position, turns, *pieces, *weights, *earlier)


def fill_columns(pos_ref, cr, mine_ref, its_ref, near_mine_ref, near_its_ref, grad_s):
    for ar in range(2):
        for br in range(2):
            block = pos_ref[0] ^ (2 * ar + br)
            if br:
                value = (near_its_ref if ar else near_mine_ref)[cr]
            else:
                value = (its_ref if ar else mine_ref)[cr, 0]
            grad_s[:, pl.ds(pl.multiple_of(block * HD, HD), HD)] = value


def other_core_kernel(count, pos_ref, mine_ref, its_ref, near_mine_ref, near_its_ref, *refs):
    w_refs, out_ref, grad_s = refs[:count], refs[-2], refs[-1]
    fill_columns(pos_ref, 1, mine_ref, its_ref, near_mine_ref, near_its_ref, grad_s)
    for o, w_ref in enumerate(w_refs):
        depth = w_ref.shape[0]
        span = pl.ds(pl.multiple_of(pos_ref[3 + o] * depth, HD), depth)
        out_ref[:, span] = lax.dot_general(
            grad_s[...], w_ref[...], (((1,), (1,)), ((), ())), preferred_element_type=jnp.float32
        ).astype(out_ref.dtype)


def same_core_kernel(count, pos_ref, mine_ref, its_ref, near_mine_ref, near_its_ref, came_ref, *refs):
    w_refs, (keep_ref, send_ref, grad_s) = refs[:count], refs[-3:]
    rows = keep_ref.shape[0]
    fill_columns(pos_ref, 0, mine_ref, its_ref, near_mine_ref, near_its_ref, grad_s)
    for o, w_ref in enumerate(w_refs):
        depth = w_ref.shape[0]
        span = pl.ds(pl.multiple_of(pos_ref[3 + o] * depth, HD), depth)
        term = lax.dot_general(
            grad_s[...], w_ref[...], (((1,), (1,)), ((), ())), preferred_element_type=jnp.float32
        ) + came_ref[:, span].astype(jnp.float32)
        keep_ref[:, span] = term[:rows]
        send_ref[:, span] = term[rows:].astype(send_ref.dtype)


def input_terms(position, blocks, weights, earlier, came=None):
    rows = blocks[0].shape[2]
    width = sum(w.shape[0] for w in weights)
    bf16 = jnp.bfloat16
    count = len(weights)
    if came is None:
        kernel, extra = functools.partial(other_core_kernel, count), ()
        shapes = jax.ShapeDtypeStruct((rows, width), bf16)
        out_specs = vmem_specs(1)[0]
    else:
        kernel, extra = functools.partial(same_core_kernel, count), (came,)
        shapes = (
            jax.ShapeDtypeStruct((rows // 2, width), jnp.float32),
            jax.ShapeDtypeStruct((rows // 2, width), bf16),
        )
        out_specs = vmem_specs(2)
    return pl.pallas_call(
        kernel,
        out_shape=shapes,
        in_specs=smem_specs(1)
        + vmem_specs(4 + len(extra) + len(weights))
        + [pl.BlockSpec(memory_space=pl.ANY)] * len(earlier),
        out_specs=out_specs,
        scratch_shapes=[pltpu.VMEM((rows, PLANES * HD), bf16)],
        compiler_params=pltpu.CompilerParams(vmem_limit_bytes=16 * 2**20),
        cost_estimate=cost(2 * rows * width * PLANES * HD, *weights),
    )(position, *blocks, *extra, *weights, *earlier)


def after(values, *earlier):
    count = len(values)
    anywhere = pl.BlockSpec(memory_space=pl.ANY)
    return pl.pallas_call(
        lambda *refs: None,
        out_shape=tuple(jax.ShapeDtypeStruct(v.shape, v.dtype) for v in values),
        in_specs=[anywhere] * (count + len(earlier)),
        out_specs=(anywhere,) * count,
        input_output_aliases={i: i for i in range(count)},
    )(*values, *earlier)


def simple_kernel(kernel, shapes, scalars, arrays, earlier=()):
    anywhere = pl.BlockSpec(memory_space=pl.ANY)
    return pl.pallas_call(
        kernel,
        out_shape=shapes,
        in_specs=smem_specs(1) + vmem_specs(len(arrays)) + [anywhere] * len(earlier),
        out_specs=jax.tree.map(lambda _: vmem_specs(1)[0], shapes),
        compiler_params=pltpu.CompilerParams(vmem_limit_bytes=32 * 2**20),
        cost_estimate=cost(0, *arrays),
    )(scalars, *arrays, *earlier)


def head_of(device):
    plane, side, core = device // 4, (device // 2) % 2, device % 2
    return 8 * (plane // 2) + 4 * side + 2 * (plane % 2) + core


def join_heads_kernel(pos_ref, in_ref, out_ref):
    for device in range(SEQ):
        head = head_of(device)
        out_ref[:, head * HD : (head + 1) * HD] = in_ref[device]


def head_columns(at):
    return (at // 2) * 1024 + lax.rem(at, 2) * 256


def planes_kernel(pos_ref, q_ref, d_ref, _, *out_refs):
    for step, out_ref in enumerate(out_refs, 1):
        start = pl.multiple_of(head_columns(lax.rem(pos_ref[0] + step, PLANES)), 256)
        for i, ref in enumerate((q_ref, d_ref)):
            out_ref[i, :, :256] = ref[:, pl.ds(start, 256)]
            out_ref[i, :, 256:] = ref[:, pl.ds(start + 512, 256)]


def sides_kernel(pos_ref, q_ref, d_ref, one_ref, two_ref, three_ref, _, kept_ref, send_ref):
    plane, side = pos_ref[0], pos_ref[1]
    for out_ref, x in ((kept_ref, side), (send_ref, 1 - side)):
        start = pl.multiple_of(head_columns(plane) + 512 * x, 256)
        for i, ref in enumerate((q_ref, d_ref)):
            out_ref[0, i] = ref[:, pl.ds(start, 256)]
        for step, ref in enumerate((one_ref, two_ref, three_ref), 1):
            out_ref[step] = ref[:, :, pl.ds(pl.multiple_of(256 * x, 256), 256)]


def cores_kernel(pos_ref, same_ref, other_ref, tok_ref, _, kept_ref, send_ref, copy_ref):
    copy_ref[...] = tok_ref[...]
    core = pos_ref[2]
    for out_ref, c in ((kept_ref, core), (send_ref, 1 - core)):
        span = pl.ds(pl.multiple_of(HD * c, HD), HD)
        out_ref[0] = same_ref[:, :, :, span]
        out_ref[1] = other_ref[:, :, :, span]


def add_kernel(pos_ref, keep_ref, came_ref, mine_ref, theirs_ref, next_ref):
    for pair, out_ref in enumerate((mine_ref, theirs_ref)):
        for cr in range(2):
            for pr in range(2):
                total = keep_ref[pair, cr, pr] + came_ref[pair, cr, pr].astype(jnp.float32)
                total = total.astype(out_ref.dtype)
                out_ref[cr, pr] = total
                if pr and not pair:
                    next_ref[cr] = total


def weight_kernel(count, pos_ref, grad_ref, *refs):
    tok_refs, out_refs = refs[:8], refs[-count:]
    for o, out_ref in enumerate(out_refs):
        depth = out_ref.shape[1]
        at = lax.rem(pos_ref[3] + o, count)
        span = pl.ds(pl.multiple_of(at * depth, HD), depth)
        acc = jnp.zeros(out_ref.shape, jnp.float32)
        for cr in range(2):
            for pr in range(2):
                grad = grad_ref[cr, pr].astype(jnp.float32).T.astype(jnp.bfloat16)
                first = 4 * cr + 2 * pr
                part = jnp.concatenate([t[:, span] for t in tok_refs[first : first + 2]], axis=0)
                acc = acc + jnp.dot(grad, part, preferred_element_type=jnp.float32)
        out_ref[...] = acc.astype(out_ref.dtype)


def sum_kernel(count, pos_ref, *refs):
    total = sum(r[...].astype(jnp.float32) for r in refs[:count])
    refs[-1][...] = total.astype(refs[-1].dtype)


def finish_kernel(pos_ref, one_ref, two_ref, _, out_ref):
    total = one_ref[...].astype(jnp.float32) + two_ref[...].astype(jnp.float32)
    out_ref[...] = total.T


def exchange(value, groups=None):
    return lax.all_to_all(value, "seq", 0, 0, axis_index_groups=groups, tiled=True)


def on_device(inputs, queries, w_kv, doc_lengths, grad_out):
    bf16, f32 = jnp.bfloat16, jnp.float32
    tokens = inputs[0]
    query_rows = queries[0]
    cotangent = grad_out[0]
    lengths = doc_lengths[0]
    rows, width = tokens.shape
    total = SEQ * rows
    half_kv = KVH * HD
    seqs = lax.axis_size("fsdp")
    depth = w_kv.shape[0]
    here = lax.axis_index("seq")
    own_seq = lax.axis_index("fsdp")
    plane, side, core = here >> 2, (here >> 1) & 1, here & 1
    origins = [(own_seq - o) % seqs for o in range(seqs)]

    first = core * half_kv + side * 256
    w_own = jnp.concatenate(
        [columns(w_kv, first, 256), columns(w_kv, first + half_kv // 2, 256)], axis=1
    )
    w_parts = [w_own] + [shift_rows(w_own, o) for o in range(1, seqs)]
    if depth % HD:
        w_full = jnp.zeros((width, PLANES * HD), bf16)
        for o in range(seqs):
            w_full = lax.dynamic_update_slice_in_dim(w_full, w_parts[o], origins[o] * depth, 0)
        w_parts, places_of = [w_full], [jnp.int32(0)]
    else:
        places_of = origins
    position = jnp.stack([plane, side, core] + places_of).astype(jnp.int32)
    seq_first = jnp.stack([plane, side, core, own_seq]).astype(jnp.int32)

    crossed = swap(tokens, 2)
    pieces = [tokens, crossed, swap(tokens, 1), swap(crossed, 1)]

    places = jnp.arange(total, dtype=jnp.int32)
    doc_ends = jnp.cumsum(lengths)
    ended = doc_ends[None, :] <= places[:, None]
    within = places - jnp.sum(jnp.where(ended, lengths[None, :], 0), axis=1)
    exponent = jnp.arange(HD // 2, dtype=f32) * (2.0 / HD)
    rate = jnp.power(ROPE_BASE, -exponent)
    angles = within.astype(f32)[:, None] * jnp.concatenate([rate, rate])[None, :]
    quarter = jnp.where(jnp.arange(HD) < HD // 2, jnp.float32(jnp.pi / 2), jnp.float32(0.0))
    turns = jnp.sin(angles + quarter[None, :])

    def bf16s(*shape):
        return jax.ShapeDtypeStruct(shape, bf16)

    for_planes = simple_kernel(
        planes_kernel, (bf16s(2, rows, 512),) * 3, position, (query_rows, cotangent), (w_own,)
    )
    from_planes = [shift_planes(part, k) for k, part in enumerate(for_planes, 1)]
    same_side, for_side = simple_kernel(
        sides_kernel,
        (bf16s(4, 2, rows, 256),) * 2,
        position,
        (query_rows, cotangent, *from_planes),
        (crossed,),
    )
    from_side = swap_sides(for_side)

    kv_blocks = project(position, turns, pieces, w_parts)
    own = exchange(kv_blocks, [[r + 4 * p for p in range(PLANES)] for r in range(4)])
    other = swap_cores(own)
    kept, for_other, tokens_later = simple_kernel(
        cores_kernel,
        (bf16s(2, 4, 2, rows, HD),) * 2 + (bf16s(rows, width),),
        position,
        (same_side, from_side, tokens),
        (own,),
    )
    came = swap_cores(for_other)

    beside = swap(tokens_later, 4)

    out_parts, keep, send = attention(
        lengths, position, kept, came, turns, own, other
    )

    (beside,) = after((beside,), send)
    beside_crossed = swap(beside, 2)
    pieces_beside = [beside, beside_crossed, swap(beside, 1), swap(beside_crossed, 1)]

    mine, theirs, mine_next = simple_kernel(
        add_kernel,
        (bf16s(2, 2, 2 * rows, HD),) * 2 + (bf16s(2, 2 * rows, HD),),
        position,
        (keep, swap_cores(send)),
    )
    its = swap(theirs, 8)

    outs = exchange(after((out_parts,), its)[0])

    blocks = (mine, its, swap(mine_next, 4), swap(its[:, 1], 4))
    pair_tokens = [*pieces[:2], *pieces_beside[:2], *pieces[2:], *pieces_beside[2:]]

    def weight_terms(grad, *earlier):
        cuts = 1 if depth % HD else seqs
        terms = simple_kernel(
            functools.partial(weight_kernel, cuts),
            (bf16s(HD, width // cuts),) * cuts,
            seq_first,
            (grad, *pair_tokens),
            earlier,
        )
        if cuts < seqs:
            terms = [columns(terms[0], ((own_seq + o) % seqs) * depth, depth) for o in range(seqs)]
        return terms

    def weight_sum(terms, *earlier):
        terms = [shift_rows(t, o) if o else t for o, t in enumerate(terms)]
        return simple_kernel(
            functools.partial(sum_kernel, seqs), bf16s(HD, depth), position, terms, earlier
        )

    mine_terms = weight_terms(mine, blocks[2])
    mine_sum = weight_sum(mine_terms)
    its_terms = weight_terms(its)

    for_core = input_terms(position, blocks, w_parts, mine_terms[:1])
    for_self, for_side = input_terms(
        position, blocks, w_parts, (mine_sum,), swap_cores(for_core)
    )
    from_side = swap_sides(for_side)

    terms = [mine_sum, weight_sum(its_terms, for_side)]

    sums = []
    for ar, term in enumerate(terms):
        pairs = []
        for s in range(SEQ):
            half = (s // 8 + ar) % 2
            pairs.append((s, (2 * (s % 2) + half) * 4 + (s & 2) + (s // 4) % 2))
        sums.append(lax.ppermute(term, "seq", pairs))

    out_rows = simple_kernel(
        join_heads_kernel, bf16s(rows, QH * HD), position, (outs,)
    )
    grad_rows = (for_self + from_side.astype(f32)).astype(bf16)
    finished = simple_kernel(
        finish_kernel, jax.ShapeDtypeStruct((depth, HD), f32), position, sums, (outs,)
    )
    return (out_rows[None], grad_rows[None], finished)


def solution(mesh):
    in_specs = (
        P("fsdp", "seq", None),
        P("fsdp", "seq", None),
        P("fsdp", None),
        P("fsdp", None),
        P("fsdp", "seq", None),
    )
    out_specs = (P("fsdp", "seq", None), P("fsdp", "seq", None), P("fsdp", "seq"))
    return jax.shard_map(
        on_device, mesh=mesh, in_specs=in_specs, out_specs=out_specs, check_vma=False
    )
```

```python
import functools

import jax
import jax.numpy as jnp
from jax import lax
from jax.experimental import pallas as pl
from jax.experimental.pallas import tpu as pltpu
from jax.sharding import PartitionSpec as P

QH = 16
KVH = 8
HD = 128
WIN = 1024
G = 2

SOFT_CAP = 50.0
QUERY_SCALE = 1.0 / 12.0
ROPE_BASE = 10000.0

SEQ = 16
PLANES = 4
BLK = 256
REACH = WIN // BLK + 1


def cost(flops, *arrays):
    moved = sum(a.size * a.dtype.itemsize for a in arrays)
    return pl.CostEstimate(flops=flops, bytes_accessed=2 * moved, transcendentals=0)


def shift_planes(value, steps):
    pairs = [(s, (s + 4 * steps) % SEQ) for s in range(SEQ)]
    return lax.ppermute(value, "seq", pairs)


def swap(value, mask):
    return lax.ppermute(value, "seq", [(s, s ^ mask) for s in range(SEQ)])


def swap_sides(value):
    return swap(value, 2)


def swap_cores(value):
    return swap(value, 1)


def shift_rows(value, steps):
    count = lax.axis_size("fsdp")
    return lax.ppermute(value, "fsdp", [(i, (i + steps) % count) for i in range(count)])


def columns(value, start, size):
    return lax.dynamic_slice_in_dim(value, start, size, value.ndim - 1)


def rotation(table):
    swapped = pltpu.roll(table, HD // 2, 1)
    first = lax.broadcasted_iota(jnp.int32, table.shape, 1) < HD // 2
    return jnp.where(first, table, swapped), jnp.where(first, -swapped, table)


def attention_kernel(
    len_ref, pos_ref, kept_ref, came_ref, turn_ref, own_ref, oth_ref, *refs
):
    out_ref, keep_ref, send_ref, q_s, d_s, kv_s, vt_s, e_s, t_s, dk_s, dv_s = refs[-11:]
    plane, side, core = pos_ref[0], pos_ref[1], pos_ref[2]
    rows = out_ref.shape[1]
    total = dk_s.shape[0]
    f32 = jnp.float32
    nt = (((1,), (1,)), ((), ()))

    def flipped(bit, flip):
        return 1 - bit if flip else bit

    for step in range(PLANES):
        home = lax.rem(plane + (PLANES - step), PLANES)
        for xr in range(2):
            for cr in range(2):
                base = home * (4 * rows) + flipped(side, xr) * (2 * rows)
                base = pl.multiple_of(base + flipped(core, cr) * rows, rows)
                source = came_ref if cr else kept_ref
                q_s[pl.ds(base, rows), :] = source[xr, step, 0]
                d_s[pl.ds(base, rows), :] = source[xr, step, 1]

    for at in range(PLANES):
        for xr in range(2):
            for cr in range(2):
                base = at * (4 * rows) + flipped(side, xr) * (2 * rows)
                mine = pl.multiple_of(base + flipped(core, cr) * rows, rows)
                theirs = pl.multiple_of(base + flipped(core, 1 - cr) * rows, rows)
                piece = pl.ds((2 * cr + xr) * rows, rows)
                kv_s[core, pl.ds(mine, rows), :] = own_ref[at, piece, :]
                kv_s[1 - core, pl.ds(theirs, rows), :] = oth_ref[at, piece, :]

    for block in range(total // BLK):
        span = pl.ds(block * BLK, BLK)
        vt_s[:, span] = kv_s[1, span, :].astype(f32).T.astype(jnp.bfloat16)
    dk_s[...] = jnp.zeros_like(dk_s)
    dv_s[...] = jnp.zeros_like(dv_s)

    ends = []
    run = 0
    for j in range(len_ref.shape[0]):
        run = run + len_ref[j]
        ends.append(run)

    def query_block(i, carry):
        base = pl.multiple_of(i * BLK, BLK)
        first_part = i * (BLK // rows)
        qb, db = q_s[pl.ds(base, BLK), :], d_s[pl.ds(base, BLK), :]
        p_row = base + lax.broadcasted_iota(jnp.int32, (1, BLK), 1)
        start_row = jnp.zeros((1, BLK), jnp.int32)
        first = jnp.int32(0)
        for end in ends:
            start_row = jnp.where(end <= p_row, end, start_row)
            first = jnp.where(end <= base, end, first)
        low_row = jnp.maximum(start_row, p_row - (WIN - 1))
        low_block = jnp.maximum(first, jnp.maximum(base - (WIN - 1), 0)) // BLK
        count = i - low_block + 1

        def body(n):
            def key_span(j):
                return pl.ds(pl.multiple_of((low_block + j) * BLK, BLK), BLK)

            norm = jnp.zeros((1, BLK), f32)
            out_t = jnp.zeros((HD, BLK), f32)
            for j in range(n):
                keys = key_span(j)
                scores = lax.dot_general(kv_s[0, keys, :], qb, nt, preferred_element_type=f32)
                squashed = jnp.tanh(scores * (QUERY_SCALE / SOFT_CAP))
                weights = jnp.exp(squashed * SOFT_CAP)
                n_col = (low_block + j) * BLK + lax.broadcasted_iota(jnp.int32, (BLK, 1), 0)
                allowed = n_col >= low_row
                if j == n - 1:
                    allowed = allowed & (n_col <= p_row)
                weights = jnp.where(allowed, weights, 0.0)
                t_s[j] = squashed
                e_s[j] = weights
                norm = norm + jnp.sum(weights, axis=0, keepdims=True)
                out_t = out_t + jnp.dot(
                    vt_s[:, keys], weights.astype(jnp.bfloat16), preferred_element_type=f32
                )
            inverse = 1.0 / norm
            out_f = (out_t * inverse).astype(jnp.bfloat16).astype(f32)
            delta = jnp.sum(db.astype(f32).T * out_f, axis=0, keepdims=True)
            out_b = out_f.T.astype(jnp.bfloat16)
            for j in range(BLK // rows):
                out_ref[first_part + j] = out_b[j * rows : (j + 1) * rows]
            for j in range(n):
                keys = key_span(j)
                probs = e_s[j] * inverse
                squashed = t_s[j]
                dv_s[keys, :] += jnp.dot(
                    probs.astype(jnp.bfloat16), db, preferred_element_type=f32
                )
                dprob = lax.dot_general(kv_s[1, keys, :], db, nt, preferred_element_type=f32)
                dscore = probs * (dprob - delta) * (1.0 - squashed * squashed)
                dk_s[keys, :] += jnp.dot(
                    dscore.astype(jnp.bfloat16), qb, preferred_element_type=f32
                )

        for n in range(1, REACH + 1):
            pl.when(count == n)(lambda n=n: body(n))
        return carry

    lax.fori_loop(0, total // BLK, query_block, 0)

    def finish(block, carry):
        span = pl.ds(pl.multiple_of(block * rows, rows), rows)
        key_part = dk_s[span, :] * QUERY_SCALE
        cosine, sine = rotation(turn_ref[span, :])
        key_part = key_part * cosine - pltpu.roll(key_part, HD // 2, 1) * sine
        value_part = dv_s[span, :]
        to_pair = lax.rem(block // 8 + plane // 2, 2)
        to_plane = lax.rem(block // 4 + plane, 2)
        to_side = lax.rem(block // 2 + side, 2)
        to_core = lax.rem(block + core, 2)
        is_key = core == 0
        at = pl.ds(pl.multiple_of(to_side * rows, rows), rows)
        keep_ref[to_pair, to_core, to_plane, at, :] = jnp.where(is_key, key_part, value_part)
        send_ref[to_pair, 1 - to_core, to_plane, at, :] = jnp.where(
            is_key, value_part, key_part
        ).astype(jnp.bfloat16)
        return carry

    lax.fori_loop(0, total // rows, finish, 0)


def vmem_specs(count):
    return [pl.BlockSpec(memory_space=pltpu.VMEM)] * count


def smem_specs(count):
    return [pl.BlockSpec(memory_space=pltpu.SMEM)] * count


def attention(lengths, position, kept, came, turns, own, other, *earlier):
    rows = kept.shape[3]
    total = SEQ * rows
    bf16, f32 = jnp.bfloat16, jnp.float32
    return pl.pallas_call(
        attention_kernel,
        out_shape=(
            jax.ShapeDtypeStruct((SEQ, rows, HD), bf16),
            jax.ShapeDtypeStruct((2, 2, 2, 2 * rows, HD), f32),
            jax.ShapeDtypeStruct((2, 2, 2, 2 * rows, HD), bf16),
        ),
        in_specs=smem_specs(2)
        + vmem_specs(5)
        + [pl.BlockSpec(memory_space=pl.ANY)] * len(earlier),
        out_specs=vmem_specs(3),
        scratch_shapes=[
            pltpu.VMEM((total, HD), bf16),
            pltpu.VMEM((total, HD), bf16),
            pltpu.VMEM((2, total, HD), bf16),
            pltpu.VMEM((HD, total), bf16),
            pltpu.VMEM((REACH, BLK, BLK), f32),
            pltpu.VMEM((REACH, BLK, BLK), f32),
            pltpu.VMEM((total, HD), f32),
            pltpu.VMEM((total, HD), f32),
        ],
        compiler_params=pltpu.CompilerParams(vmem_limit_bytes=22 * 2**20),
        cost_estimate=cost(300 * BLK * BLK * HD, kept, came, own, other, turns),
    )(lengths, position, kept, came, turns, own, other, *earlier)


def project_kernel(count, pos_ref, turn_ref, *refs):
    tok_refs, w_refs, out_ref = refs[:4], refs[4 : 4 + count], refs[-1]
    plane, side, core = pos_ref[0], pos_ref[1], pos_ref[2]
    rows = tok_refs[0].shape[0]
    is_key = core == 0
    for half in range(PLANES // 2):
        acc = jnp.zeros((4 * rows, 2 * HD), jnp.float32)
        for o, w_ref in enumerate(w_refs):
            depth = w_ref.shape[0]
            span = pl.ds(pl.multiple_of(pos_ref[3 + o] * depth, HD), depth)
            part = jnp.concatenate([t[:, span] for t in tok_refs], axis=0)
            acc = acc + jnp.dot(
                part,
                w_ref[:, half * 2 * HD : (half + 1) * 2 * HD],
                preferred_element_type=jnp.float32,
            )
        for b in range(2):
            at = 2 * half + b
            for piece in range(4):
                x = 1 - side if piece % 2 else side
                c = 1 - core if piece // 2 else core
                start = pl.multiple_of((plane * 4 + 2 * x + c) * rows, rows)
                head = acc[piece * rows : (piece + 1) * rows, b * HD : (b + 1) * HD]
                cosine, sine = rotation(turn_ref[pl.ds(start, rows), :])
                cosine, sine = jnp.where(is_key, cosine, 1.0), jnp.where(is_key, sine, 0.0)
                turned = head * cosine + pltpu.roll(head, HD // 2, 1) * sine
                out_ref[at, piece * rows : (piece + 1) * rows] = turned.astype(jnp.bfloat16)


def project(position, turns, pieces, weights, *earlier):
    rows, width = pieces[0].shape
    return pl.pallas_call(
        functools.partial(project_kernel, len(weights)),
        out_shape=jax.ShapeDtypeStruct((PLANES, 4 * rows, HD), jnp.bfloat16),
        in_specs=smem_specs(1)
        + vmem_specs(5 + len(weights))
        + [pl.BlockSpec(memory_space=pl.ANY)] * len(earlier),
        out_specs=vmem_specs(1)[0],
        compiler_params=pltpu.CompilerParams(vmem_limit_bytes=40 * 2**20),
        cost_estimate=cost(8 * rows * width * PLANES * HD, *pieces, *weights),
    )(position, turns, *pieces, *weights, *earlier)


def fill_columns(pos_ref, cr, mine_ref, its_ref, near_mine_ref, near_its_ref, grad_s):
    for ar in range(2):
        for br in range(2):
            block = pos_ref[0] ^ (2 * ar + br)
            if br:
                value = (near_its_ref if ar else near_mine_ref)[cr]
            else:
                value = (its_ref if ar else mine_ref)[cr, 0]
            grad_s[:, pl.ds(pl.multiple_of(block * HD, HD), HD)] = value


def other_core_kernel(count, pos_ref, mine_ref, its_ref, near_mine_ref, near_its_ref, *refs):
    w_refs, out_ref, grad_s = refs[:count], refs[-2], refs[-1]
    fill_columns(pos_ref, 1, mine_ref, its_ref, near_mine_ref, near_its_ref, grad_s)
    for o, w_ref in enumerate(w_refs):
        depth = w_ref.shape[0]
        span = pl.ds(pl.multiple_of(pos_ref[3 + o] * depth, HD), depth)
        out_ref[:, span] = lax.dot_general(
            grad_s[...], w_ref[...], (((1,), (1,)), ((), ())), preferred_element_type=jnp.float32
        ).astype(out_ref.dtype)


def same_core_kernel(count, pos_ref, mine_ref, its_ref, near_mine_ref, near_its_ref, came_ref, *refs):
    w_refs, (keep_ref, send_ref, grad_s) = refs[:count], refs[-3:]
    rows = keep_ref.shape[0]
    fill_columns(pos_ref, 0, mine_ref, its_ref, near_mine_ref, near_its_ref, grad_s)
    for o, w_ref in enumerate(w_refs):
        depth = w_ref.shape[0]
        span = pl.ds(pl.multiple_of(pos_ref[3 + o] * depth, HD), depth)
        term = lax.dot_general(
            grad_s[...], w_ref[...], (((1,), (1,)), ((), ())), preferred_element_type=jnp.float32
        ) + came_ref[:, span].astype(jnp.float32)
        keep_ref[:, span] = term[:rows]
        send_ref[:, span] = term[rows:].astype(send_ref.dtype)


def input_terms(position, blocks, weights, earlier, came=None):
    rows = blocks[0].shape[2]
    width = sum(w.shape[0] for w in weights)
    bf16 = jnp.bfloat16
    count = len(weights)
    if came is None:
        kernel, extra = functools.partial(other_core_kernel, count), ()
        shapes = jax.ShapeDtypeStruct((rows, width), bf16)
        out_specs = vmem_specs(1)[0]
    else:
        kernel, extra = functools.partial(same_core_kernel, count), (came,)
        shapes = (
            jax.ShapeDtypeStruct((rows // 2, width), jnp.float32),
            jax.ShapeDtypeStruct((rows // 2, width), bf16),
        )
        out_specs = vmem_specs(2)
    return pl.pallas_call(
        kernel,
        out_shape=shapes,
        in_specs=smem_specs(1)
        + vmem_specs(4 + len(extra) + len(weights))
        + [pl.BlockSpec(memory_space=pl.ANY)] * len(earlier),
        out_specs=out_specs,
        scratch_shapes=[pltpu.VMEM((rows, PLANES * HD), bf16)],
        compiler_params=pltpu.CompilerParams(vmem_limit_bytes=16 * 2**20),
        cost_estimate=cost(2 * rows * width * PLANES * HD, *weights),
    )(position, *blocks, *extra, *weights, *earlier)


def after(values, *earlier):
    count = len(values)
    anywhere = pl.BlockSpec(memory_space=pl.ANY)
    return pl.pallas_call(
        lambda *refs: None,
        out_shape=tuple(jax.ShapeDtypeStruct(v.shape, v.dtype) for v in values),
        in_specs=[anywhere] * (count + len(earlier)),
        out_specs=(anywhere,) * count,
        input_output_aliases={i: i for i in range(count)},
    )(*values, *earlier)


def simple_kernel(kernel, shapes, scalars, arrays, earlier=()):
    anywhere = pl.BlockSpec(memory_space=pl.ANY)
    return pl.pallas_call(
        kernel,
        out_shape=shapes,
        in_specs=smem_specs(1) + vmem_specs(len(arrays)) + [anywhere] * len(earlier),
        out_specs=jax.tree.map(lambda _: vmem_specs(1)[0], shapes),
        compiler_params=pltpu.CompilerParams(vmem_limit_bytes=32 * 2**20),
        cost_estimate=cost(0, *arrays),
    )(scalars, *arrays, *earlier)


def head_of(device):
    plane, side, core = device // 4, (device // 2) % 2, device % 2
    return 8 * (plane // 2) + 4 * side + 2 * (plane % 2) + core


def join_heads_kernel(pos_ref, in_ref, out_ref):
    for device in range(SEQ):
        head = head_of(device)
        out_ref[:, head * HD : (head + 1) * HD] = in_ref[device]


def head_columns(at):
    return (at // 2) * 1024 + lax.rem(at, 2) * 256


def planes_kernel(pos_ref, q_ref, d_ref, _, *out_refs):
    for step, out_ref in enumerate(out_refs, 1):
        start = pl.multiple_of(head_columns(lax.rem(pos_ref[0] + step, PLANES)), 256)
        for i, ref in enumerate((q_ref, d_ref)):
            out_ref[i, :, :256] = ref[:, pl.ds(start, 256)]
            out_ref[i, :, 256:] = ref[:, pl.ds(start + 512, 256)]


def sides_kernel(pos_ref, q_ref, d_ref, one_ref, two_ref, three_ref, _, kept_ref, send_ref):
    plane, side = pos_ref[0], pos_ref[1]
    for out_ref, x in ((kept_ref, side), (send_ref, 1 - side)):
        start = pl.multiple_of(head_columns(plane) + 512 * x, 256)
        for i, ref in enumerate((q_ref, d_ref)):
            out_ref[0, i] = ref[:, pl.ds(start, 256)]
        for step, ref in enumerate((one_ref, two_ref, three_ref), 1):
            out_ref[step] = ref[:, :, pl.ds(pl.multiple_of(256 * x, 256), 256)]


def cores_kernel(pos_ref, same_ref, other_ref, tok_ref, _, kept_ref, send_ref, copy_ref):
    copy_ref[...] = tok_ref[...]
    core = pos_ref[2]
    for out_ref, c in ((kept_ref, core), (send_ref, 1 - core)):
        span = pl.ds(pl.multiple_of(HD * c, HD), HD)
        out_ref[0] = same_ref[:, :, :, span]
        out_ref[1] = other_ref[:, :, :, span]


def add_kernel(pos_ref, keep_ref, came_ref, mine_ref, theirs_ref, next_ref):
    for pair, out_ref in enumerate((mine_ref, theirs_ref)):
        for cr in range(2):
            for pr in range(2):
                total = keep_ref[pair, cr, pr] + came_ref[pair, cr, pr].astype(jnp.float32)
                total = total.astype(out_ref.dtype)
                out_ref[cr, pr] = total
                if pr and not pair:
                    next_ref[cr] = total


def weight_kernel(count, pos_ref, grad_ref, *refs):
    tok_refs, out_refs = refs[:8], refs[-count:]
    for o, out_ref in enumerate(out_refs):
        depth = out_ref.shape[1]
        at = lax.rem(pos_ref[3] + o, count)
        span = pl.ds(pl.multiple_of(at * depth, HD), depth)
        acc = jnp.zeros(out_ref.shape, jnp.float32)
        for cr in range(2):
            for pr in range(2):
                grad = grad_ref[cr, pr].astype(jnp.float32).T.astype(jnp.bfloat16)
                first = 4 * cr + 2 * pr
                part = jnp.concatenate([t[:, span] for t in tok_refs[first : first + 2]], axis=0)
                acc = acc + jnp.dot(grad, part, preferred_element_type=jnp.float32)
        out_ref[...] = acc.astype(out_ref.dtype)


def sum_kernel(count, pos_ref, *refs):
    total = sum(r[...].astype(jnp.float32) for r in refs[:count])
    refs[-1][...] = total.astype(refs[-1].dtype)


def finish_kernel(pos_ref, one_ref, two_ref, _, out_ref):
    total = one_ref[...].astype(jnp.float32) + two_ref[...].astype(jnp.float32)
    out_ref[...] = total.T


def exchange(value, groups=None):
    return lax.all_to_all(value, "seq", 0, 0, axis_index_groups=groups, tiled=True)


def on_device(inputs, queries, w_kv, doc_lengths, grad_out):
    bf16, f32 = jnp.bfloat16, jnp.float32
    tokens = inputs[0]
    query_rows = queries[0]
    cotangent = grad_out[0]
    lengths = doc_lengths[0]
    rows, width = tokens.shape
    total = SEQ * rows
    half_kv = KVH * HD
    seqs = lax.axis_size("fsdp")
    depth = w_kv.shape[0]
    here = lax.axis_index("seq")
    own_seq = lax.axis_index("fsdp")
    plane, side, core = here >> 2, (here >> 1) & 1, here & 1
    origins = [(own_seq - o) % seqs for o in range(seqs)]

    first = core * half_kv + side * 256
    w_own = jnp.concatenate(
        [columns(w_kv, first, 256), columns(w_kv, first + half_kv // 2, 256)], axis=1
    )
    w_parts = [w_own] + [shift_rows(w_own, o) for o in range(1, seqs)]
    if depth % HD:
        w_full = jnp.zeros((width, PLANES * HD), bf16)
        for o in range(seqs):
            w_full = lax.dynamic_update_slice_in_dim(w_full, w_parts[o], origins[o] * depth, 0)
        w_parts, places_of = [w_full], [jnp.int32(0)]
    else:
        places_of = origins
    position = jnp.stack([plane, side, core] + places_of).astype(jnp.int32)
    seq_first = jnp.stack([plane, side, core, own_seq]).astype(jnp.int32)

    crossed = swap(tokens, 2)
    pieces = [tokens, crossed, swap(tokens, 1), swap(crossed, 1)]

    places = jnp.arange(total, dtype=jnp.int32)
    doc_ends = jnp.cumsum(lengths)
    ended = doc_ends[None, :] <= places[:, None]
    within = places - jnp.sum(jnp.where(ended, lengths[None, :], 0), axis=1)
    exponent = jnp.arange(HD // 2, dtype=f32) * (2.0 / HD)
    rate = jnp.power(ROPE_BASE, -exponent)
    angles = within.astype(f32)[:, None] * jnp.concatenate([rate, rate])[None, :]
    quarter = jnp.where(jnp.arange(HD) < HD // 2, jnp.float32(jnp.pi / 2), jnp.float32(0.0))
    turns = jnp.sin(angles + quarter[None, :])

    def bf16s(*shape):
        return jax.ShapeDtypeStruct(shape, bf16)

    for_planes = simple_kernel(
        planes_kernel, (bf16s(2, rows, 512),) * 3, position, (query_rows, cotangent), (w_own,)
    )
    from_planes = [shift_planes(part, k) for k, part in enumerate(for_planes, 1)]
    same_side, for_side = simple_kernel(
        sides_kernel,
        (bf16s(4, 2, rows, 256),) * 2,
        position,
        (query_rows, cotangent, *from_planes),
        (crossed,),
    )
    from_side = swap_sides(for_side)

    kv_blocks = project(position, turns, pieces, w_parts)
    own = exchange(kv_blocks, [[r + 4 * p for p in range(PLANES)] for r in range(4)])
    other = swap_cores(own)
    kept, for_other, tokens_later = simple_kernel(
        cores_kernel,
        (bf16s(2, 4, 2, rows, HD),) * 2 + (bf16s(rows, width),),
        position,
        (same_side, from_side, tokens),
        (own,),
    )
    came = swap_cores(for_other)

    beside = swap(tokens_later, 4)

    out_parts, keep, send = attention(
        lengths, position, kept, came, turns, own, other
    )

    (beside,) = after((beside,), send)
    beside_crossed = swap(beside, 2)
    pieces_beside = [beside, beside_crossed, swap(beside, 1), swap(beside_crossed, 1)]

    mine, theirs, mine_next = simple_kernel(
        add_kernel,
        (bf16s(2, 2, 2 * rows, HD),) * 2 + (bf16s(2, 2 * rows, HD),),
        position,
        (keep, swap_cores(send)),
    )
    its = swap(theirs, 8)

    outs = exchange(after((out_parts,), its)[0])

    blocks = (mine, its, swap(mine_next, 4), swap(its[:, 1], 4))
    pair_tokens = [*pieces[:2], *pieces_beside[:2], *pieces[2:], *pieces_beside[2:]]

    def weight_terms(grad, *earlier):
        cuts = 1 if depth % HD else seqs
        terms = simple_kernel(
            functools.partial(weight_kernel, cuts),
            (bf16s(HD, width // cuts),) * cuts,
            seq_first,
            (grad, *pair_tokens),
            earlier,
        )
        if cuts < seqs:
            terms = [columns(terms[0], ((own_seq + o) % seqs) * depth, depth) for o in range(seqs)]
        return terms

    def weight_sum(terms, *earlier):
        terms = [shift_rows(t, o) if o else t for o, t in enumerate(terms)]
        return simple_kernel(
            functools.partial(sum_kernel, seqs), bf16s(HD, depth), position, terms, earlier
        )

    mine_terms = weight_terms(mine, blocks[2])
    mine_sum = weight_sum(mine_terms)
    its_terms = weight_terms(its)

    for_core = input_terms(position, blocks, w_parts, (mine_terms[0], its_terms[0]))
    for_self, for_side = input_terms(
        position, blocks, w_parts, (mine_sum,), swap_cores(for_core)
    )
    from_side = swap_sides(for_side)

    terms = [mine_sum, weight_sum(its_terms, for_side)]

    sums = []
    for ar, term in enumerate(terms):
        pairs = []
        for s in range(SEQ):
            half = (s // 8 + ar) % 2
            pairs.append((s, (2 * (s % 2) + half) * 4 + (s & 2) + (s // 4) % 2))
        sums.append(lax.ppermute(term, "seq", pairs))

    out_rows = simple_kernel(
        join_heads_kernel, bf16s(rows, QH * HD), position, (outs,)
    )
    grad_rows = (for_self + from_side.astype(f32)).astype(bf16)
    finished = simple_kernel(
        finish_kernel, jax.ShapeDtypeStruct((depth, HD), f32), position, sums, (outs,)
    )
    return (out_rows[None], grad_rows[None], finished)


def solution(mesh):
    in_specs = (
        P("fsdp", "seq", None),
        P("fsdp", "seq", None),
        P("fsdp", None),
        P("fsdp", None),
        P("fsdp", "seq", None),
    )
    out_specs = (P("fsdp", "seq", None), P("fsdp", "seq", None), P("fsdp", "seq"))
    return jax.shard_map(
        on_device, mesh=mesh, in_specs=in_specs, out_specs=out_specs, check_vma=False
    )
```
